32 devices in a mesh: dp: 16 (over z, y, x), mp: 2 (over core).
Axes of the slice: x: 2, y: 2, z: 4, core: 2. Of those that a mesh axis runs over, the one named last changes fastest.
Arguments:
- tokens_in: bfloat16 [16384, 768], P('dp'), may hold values from -6 to 6
- proj_query: bfloat16 [768, 768], P(None, 'mp'), may hold values from -0.21875 to 0.21875
- bias_query: float32 [768], P('mp'), may hold values from -3 to 3
- proj_key: bfloat16 [768, 768], P(None, 'mp'), may hold values from -0.21875 to 0.21875
- proj_value: bfloat16 [768, 768], P(None, 'mp'), may hold values from -0.21875 to 0.21875
- bias_value: float32 [768], P('mp'), may hold values from -3 to 3
- proj_out: bfloat16 [768, 768], P('mp'), may hold values from -0.875 to 0.875
- bias_out: float32 [768], replicated, may hold values from -3 to 3
- gain_attn: float32 [768], replicated, may hold values from 0.5 to 1.5
- shift_attn: float32 [768], replicated, may hold values from -2 to 2
- proj_in: bfloat16 [768, 3072], P(None, 'mp'), may hold values from -0.21875 to 0.21875
- bias_in: float32 [3072], P('mp'), may hold values from -3 to 3
- proj_down: bfloat16 [3072, 768], P('mp'), may hold values from -0.109375 to 0.109375
- bias_down: float32 [768], replicated, may hold values from -3 to 3
- gain_ffn: float32 [768], replicated, may hold values from 0.5 to 1.5
- shift_ffn: float32 [768], replicated, may hold values from -0.3 to 0.3
- bucket: int32 [32], P('dp'), may hold values from 0 to 3, as said below
- lengths: int32 [32, 16], P('dp'), may hold values from 0 to 512, as said below
- positive: int32 [256], P('dp'), may hold values from 0 to 63, as said below
Outputs:
- contrast_loss: float32 [], replicated
- query_embed: float32 [256, 768], P('dp')
- passage_embed: float32 [64, 768], P('dp')
- grad_input: bfloat16 [16384, 768], P('dp')
- grad_proj_query: float32 [768, 768], P(None, 'mp')
- grad_bias_query: float32 [768], P('mp')
- grad_proj_key: float32 [768, 768], P(None, 'mp')
- grad_proj_value: float32 [768, 768], P(None, 'mp')
- grad_bias_value: float32 [768], P('mp')
- grad_proj_out: float32 [768, 768], P('mp')
- grad_bias_out: float32 [768], P('mp')
- grad_gain_attn: float32 [768], P('mp')
- grad_shift_attn: float32 [768], P('mp')
- grad_proj_in: float32 [768, 3072], P(None, 'mp')
- grad_bias_in: float32 [3072], P('mp')
- grad_proj_down: float32 [3072, 768], P('mp')
- grad_bias_down: float32 [768], P('mp')
- grad_gain_ffn: float32 [768], P('mp')
- grad_shift_ffn: float32 [768], P('mp')
The draws below stay inside these ranges and needn't reach their ends.
Inputs may be any that keep to these rules, and one draw needn't show every extreme that they name: `bucket`: Even-numbered blocks hold queries and have code 0 or 1; odd-numbered blocks hold passages and have code 2 or 3. Code c means slots of 32, 64, 128, 512 rows, so 16, 8, 4 or 1 slots a block. `lengths`: A slot that its block's code holds has a length from half its span to its span; slot 0 always has the full span; slots past the block's slot count are 0. `positive`: each value is 4 j + s for a passage block j (j-th odd block) and a slot s that is live in it.
All inputs are finite; a program needn't handle non-finite values.
Results may differ from the reference program's by a relative error of at most 0.01145.
Values may be sent and summed in bfloat16 or wider, within the bound.
No kernel may reach another device: no remote copies, remote signals or barrier semaphores. Data moves between devices by JAX's collectives and lax.ppermute only.
A program may use at most 128 MiB of HBM per device.

```python
import jax
import jax.numpy as jnp
from jax import lax

D = 768
HEADS = 12
HEAD_DIM = 64
FF = 3072
BLOCK = 512
BLOCKS = 32
TOKENS = 16384
QUERIES = 256
PASSAGES = 64


def span_of_codes(block_codes):
    span_list = jnp.array([BLOCK // 16, BLOCK // 8, BLOCK // 4, BLOCK], jnp.int32)
    return jnp.sum(jnp.where(block_codes[:, None] == jnp.arange(4, dtype=jnp.int32)[None, :], span_list[None, :], 0), 1)


def draw_layout(key):
    pair_count = BLOCKS // 2
    query_key, passage_key, length_key, forced_key = jax.random.split(key, 4)
    query_codes = jax.random.randint(query_key, (pair_count,), 0, 2)
    passage_codes = jax.random.randint(passage_key, (pair_count,), 2, 4)
    forced = jax.random.randint(forced_key, (), 0, pair_count)
    passage_codes = jnp.where(jnp.arange(pair_count) == forced, 3, passage_codes)
    block_codes = jnp.stack([query_codes, passage_codes], 1).reshape(BLOCKS).astype(jnp.int32)
    slot_spans = span_of_codes(block_codes)
    counts = BLOCK // slot_spans
    random_bits = jax.random.randint(length_key, (BLOCKS, 16), 0, 1 << 20)
    halves = slot_spans // 2
    lengths_all = halves[:, None] + random_bits % (halves[:, None] + 1)
    slot_index = jnp.arange(16, dtype=jnp.int32)[None, :]
    lengths_all = jnp.where(slot_index == 0, slot_spans[:, None], lengths_all)
    lengths_all = jnp.where(slot_index < counts[:, None], lengths_all, 0)
    return (block_codes, lengths_all.astype(jnp.int32))


def draw_bucket(key, part):
    block_codes, lengths_all = draw_layout(key)
    return block_codes


def draw_lengths(key, part):
    block_codes, lengths_all = draw_layout(key)
    return lengths_all


def draw_positive(key, part):
    block_codes, lengths_all = draw_layout(key)
    key = jax.random.fold_in(key, 7)
    pick_key, slot_key = jax.random.split(key)
    pair_count = BLOCKS // 2
    target_block = jax.random.randint(pick_key, (QUERIES,), 0, pair_count)
    passage_codes = block_codes.reshape(pair_count, 2)[:, 1]
    live_slots = jnp.where(passage_codes == 2, 4, 1)
    chosen_live = live_slots[target_block]
    slot_pick = jax.random.randint(slot_key, (QUERIES,), 0, 1 << 20) % chosen_live
    return (target_block * 4 + slot_pick).astype(jnp.int32)


def levels(own_key, shape, cuts, smallest, high):
    loudness, own = 1.0, jax.random.fold_in(own_key, 6)
    for position, shards_of in cuts:
        heights = jnp.exp(jax.random.uniform(jax.random.fold_in(own, position), (shards_of,), jnp.float32, smallest / len(cuts), high / len(cuts)))
        loudness = loudness * jnp.repeat(heights, shape[position] // shards_of).reshape([-1 if axis == position else 1 for axis in range(len(shape))])
    return loudness


def scatter_about(stream_key, extent, deviation, limit, cuts=(), kind=jnp.bfloat16):
    loudness = levels(stream_key, extent, cuts, -0.22, 0.18) if cuts else 1.0
    drawn = jax.random.normal(stream_key, extent, jnp.float32) * deviation * loudness
    return jnp.minimum(jnp.maximum(drawn, -limit), limit).astype(kind)


def setup_inputs(seed: int = 0) -> dict:
    arg_keys = jax.random.split(jax.random.key(seed), 20)
    tokens_in = scatter_about(arg_keys[0], (TOKENS, D), 1.0, 6.0, ((0, 16),))
    proj_query = scatter_about(arg_keys[1], (D, D), D ** -0.5, 0.21875, ((1, 2),))
    bias_query = scatter_about(arg_keys[2], (D,), 0.5, 3.0, ((0, 2),), jnp.float32)
    proj_key = scatter_about(arg_keys[3], (D, D), D ** -0.5, 0.21875, ((1, 2),))
    proj_value = scatter_about(arg_keys[4], (D, D), D ** -0.5, 0.21875, ((1, 2),))
    bias_value = scatter_about(arg_keys[5], (D,), 0.5, 3.0, ((0, 2),), jnp.float32)
    proj_out = scatter_about(arg_keys[6], (D, D), (D // 16) ** -0.5, 0.875, ((0, 2),))
    bias_out = scatter_about(arg_keys[7], (D,), 0.5, 3.0, (), jnp.float32)
    gain_attn = jnp.clip(1.0 + 0.1 * jax.random.normal(arg_keys[8], (D,), jnp.float32), 0.5, 1.5)
    shift_attn = scatter_about(arg_keys[9], (D,), 0.3, 2.0, (), jnp.float32)
    proj_in = scatter_about(arg_keys[10], (D, FF), D ** -0.5, 0.21875, ((1, 2),))
    bias_in = scatter_about(arg_keys[11], (FF,), 0.5, 3.0, ((0, 2),), jnp.float32)
    proj_down = scatter_about(arg_keys[12], (FF, D), FF ** -0.5, 0.109375, ((0, 2),))
    bias_down = scatter_about(arg_keys[13], (D,), 0.5, 3.0, (), jnp.float32)
    gain_ffn = jnp.clip(1.0 + 0.1 * jax.random.normal(arg_keys[14], (D,), jnp.float32), 0.5, 1.5)
    shift_ffn = scatter_about(arg_keys[15], (D,), 0.05, 0.3, (), jnp.float32)
    bucket = draw_bucket(jax.random.fold_in(arg_keys[19], 71), 0)
    lengths = draw_lengths(jax.random.fold_in(arg_keys[19], 71), 0)
    positive = draw_positive(jax.random.fold_in(arg_keys[19], 71), 0)
    return {"tokens_in": tokens_in, "proj_query": proj_query, "bias_query": bias_query, "proj_key": proj_key, "proj_value": proj_value, "bias_value": bias_value, "proj_out": proj_out, "bias_out": bias_out, "gain_attn": gain_attn, "shift_attn": shift_attn, "proj_in": proj_in, "bias_in": bias_in, "proj_down": proj_down, "bias_down": bias_down, "gain_ffn": gain_ffn, "shift_ffn": shift_ffn, "bucket": bucket, "lengths": lengths, "positive": positive}


EPS = 1e-05
TEMP = 0.01
MASKED = -10000.0
HIGH = lax.Precision.HIGHEST

@jax.custom_vjp
def low(v):
    return lax.optimization_barrier(v.astype(jnp.bfloat16)).astype(jnp.float32)

@jax.custom_vjp
def low_back(v):
    return v

def low_keep(v):
    return (low(v), None)

def low_pass(kept, grad):
    return (grad,)

def back_keep(v):
    return (v, None)

def back_low(kept, grad):
    return (low(grad),)
low.defvjp(low_keep, low_pass)
low_back.defvjp(back_keep, back_low)

def span_table(block_code):
    span_list = jnp.array([BLOCK // 16, BLOCK // 8, BLOCK // 4, BLOCK], jnp.int32)
    return jnp.sum(jnp.where(block_code == jnp.arange(4, dtype=jnp.int32), span_list, 0)).astype(jnp.int32)

def block_layout(block_code, slot_lengths):
    span_size = span_table(block_code)
    places = jnp.arange(BLOCK, dtype=jnp.int32)
    slot_of = places // span_size
    offset = places % span_size
    slot_index = jnp.arange(16, dtype=jnp.int32)
    slot_len = lax.optimization_barrier(jnp.sum(jnp.where(slot_of[:, None] == slot_index[None, :], slot_lengths[None, :], 0), axis=1)).astype(jnp.int32)
    living = offset < slot_len
    member = (slot_of[None, :] == slot_index[:, None]) & living[None, :]
    pooling = member.astype(jnp.float32) / jnp.maximum(slot_lengths, 1).astype(jnp.float32)[:, None]
    return (slot_of, living, pooling)

def layer_norm(resid, gain, shift):
    center = resid - lax.optimization_barrier(jnp.mean(resid, -1, keepdims=True))
    spread = lax.optimization_barrier(jnp.mean(center * center, -1, keepdims=True))
    return center * lax.rsqrt(spread + EPS) * gain + shift

def unit_rows(vectors):
    return vectors * lax.rsqrt(lax.optimization_barrier(jnp.sum(vectors * vectors, -1, keepdims=True)) + 1e-06)

def block_embed(params, block_tokens, block_code, slot_lengths):
    proj_query, bias_query, proj_key, proj_value, bias_value, proj_out, bias_out, gain_attn, shift_attn, proj_in, bias_in, proj_down, bias_down, gain_ffn, shift_ffn = params
    slot_of, living, pooling = block_layout(block_code, slot_lengths)
    query = low_back(low(jnp.dot(block_tokens, proj_query, precision=HIGH) + bias_query)).reshape(BLOCK, HEADS, HEAD_DIM)
    keys = low_back(low(jnp.dot(block_tokens, proj_key, precision=HIGH))).reshape(BLOCK, HEADS, HEAD_DIM)
    values = low_back(low(jnp.dot(block_tokens, proj_value, precision=HIGH) + bias_value)).reshape(BLOCK, HEADS, HEAD_DIM)
    scaling = HEAD_DIM ** (-0.5)
    scores = low_back(scaling * jnp.einsum('qhd,khd->hqk', query, keys, precision=HIGH))
    allowed = (slot_of[:, None] == slot_of[None, :]) & living[None, :]
    scores = jnp.where(allowed[None, :, :], scores, MASKED)
    summit = lax.optimization_barrier(jnp.max(scores, -1, keepdims=True))
    raised = jnp.exp(scores - summit)
    probs = raised / lax.optimization_barrier(jnp.sum(raised, -1, keepdims=True))
    context = jnp.einsum('hqk,khd->qhd', low(probs), values, precision=HIGH).reshape(BLOCK, D)
    context = low_back(low(context))
    attn = low_back(jnp.dot(context, proj_out, precision=HIGH) + bias_out)
    hidden = layer_norm(block_tokens + attn, gain_attn, shift_attn)
    inner = low_back(jnp.dot(low(hidden), proj_in, precision=HIGH) + bias_in)
    act = low(jax.nn.gelu(inner, approximate=False))
    ffn = low_back(jnp.dot(act, proj_down, precision=HIGH) + bias_down)
    output = layer_norm(hidden + ffn, gain_ffn, shift_ffn)
    return jnp.dot(pooling, output, precision=HIGH)

def reference(tokens_in, proj_query, bias_query, proj_key, proj_value, bias_value, proj_out, bias_out, gain_attn, shift_attn, proj_in, bias_in, proj_down, bias_down, gain_ffn, shift_ffn, bucket, lengths, positive):
    params = (proj_query.astype(jnp.float32), bias_query.astype(jnp.float32), proj_key.astype(jnp.float32), proj_value.astype(jnp.float32), bias_value.astype(jnp.float32), proj_out.astype(jnp.float32), bias_out.astype(jnp.float32), gain_attn.astype(jnp.float32), shift_attn.astype(jnp.float32), proj_in.astype(jnp.float32), bias_in.astype(jnp.float32), proj_down.astype(jnp.float32), bias_down.astype(jnp.float32), gain_ffn.astype(jnp.float32), shift_ffn.astype(jnp.float32))
    tokens_f = tokens_in.astype(jnp.float32)
    codes = bucket.reshape(BLOCKS // 2, 2)
    query_count = jnp.where(codes[:, 0] == 0, 16, 8).astype(jnp.int32)
    query_live = (jnp.arange(16, dtype=jnp.int32)[None, :] < query_count[:, None]).reshape(QUERIES).astype(jnp.float32)
    passage_count = jnp.where(codes[:, 1] == 2, 4, 1).astype(jnp.int32)
    passage_live = (jnp.arange(4, dtype=jnp.int32)[None, :] < passage_count[:, None]).reshape(PASSAGES)

    def objective(params, tokens_f):
        blocks = tokens_f.reshape(BLOCKS, BLOCK, D)

        def one_block(item):
            return block_embed(params, item[0], item[1], item[2])
        embeds = lax.map(jax.checkpoint(one_block), (blocks, bucket, lengths))
        query_unit = unit_rows(embeds[0::2].reshape(QUERIES, D))
        passage_unit = unit_rows(embeds[1::2, :4].reshape(PASSAGES, D))
        logits = jnp.einsum('qd,pd->qp', query_unit, passage_unit, precision=HIGH) / TEMP
        logits = jnp.where(passage_live[None, :], logits, MASKED)
        summit = lax.optimization_barrier(jnp.max(logits, 1, keepdims=True))
        normal = jnp.log(lax.optimization_barrier(jnp.sum(jnp.exp(logits - summit), 1))) + summit[:, 0]
        chosen = jnp.take_along_axis(logits, positive[:, None].astype(jnp.int32), 1)[:, 0]
        loss_value = jnp.sum(query_live * (normal - chosen)) / jnp.sum(query_live)
        return (loss_value, (query_unit, passage_unit))
    loss_value, pullback, embeds = jax.vjp(objective, params, tokens_f, has_aux=True)
    grad_params, grad_tokens = pullback(jnp.ones_like(loss_value))
    return (loss_value, embeds[0], embeds[1], grad_tokens.astype(jnp.bfloat16), grad_params[0], grad_params[1], grad_params[2], grad_params[3], grad_params[4], grad_params[5], grad_params[6], grad_params[7], grad_params[8], grad_params[9], grad_params[10], grad_params[11], grad_params[12], grad_params[13], grad_params[14])
```

```python
from functools import partial

import jax
import jax.numpy as jnp
from jax import lax
from jax.experimental import pallas as pl
from jax.experimental.pallas import tpu as pltpu
from jax.sharding import PartitionSpec as P

HEAD_DIM = 64
BLOCK = 512
PAIR = 2 * HEAD_DIM
CHUNK = 128
SLOTS = 16
EPS = 1e-05
TEMP = 0.01
MASKED = -10000.0
HIGH = lax.Precision.HIGHEST
F32 = jnp.float32
BF16 = jnp.bfloat16
VMEM = pl.BlockSpec(memory_space=pltpu.VMEM)
SMEM = pl.BlockSpec(memory_space=pltpu.SMEM)


def dot(a, b, dims=((1,), (0,)), precision=None):
    return lax.dot_general(a, b, (dims, ((), ())), precision=precision, preferred_element_type=F32)


ROWS = ((0,), (0,))
LANES = ((1,), (1,))


def params(mib):
    return pltpu.CompilerParams(vmem_limit_bytes=mib * 1024 * 1024)


def shape(*dims, kind=F32):
    return jax.ShapeDtypeStruct(dims, kind)


def lane_masks(kind):
    first = (lax.broadcasted_iota(jnp.int32, (1, PAIR), 1) < HEAD_DIM).astype(F32)
    return first.astype(kind), (1.0 - first).astype(kind)


def layout(bucket, lengths, me, axis):
    code = bucket[me]
    dims = (BLOCK, 1) if axis == 0 else (1, BLOCK)
    places = lax.broadcasted_iota(jnp.int32, dims, axis)
    shift = jnp.full(dims, jnp.where(code == 3, 9, 5 + code), jnp.int32)
    slot = lax.shift_right_logical(places, shift)
    offset = places - lax.shift_left(slot, shift)
    length = jnp.zeros(dims, jnp.int32)
    for s in range(SLOTS):
        length = jnp.where(slot == s, lengths[me, s], length)
    return slot, jnp.where(offset < length, slot, -1)


def pooling(bucket, lengths, me):
    _, kid = layout(bucket, lengths, me, 1)
    slots = lax.broadcasted_iota(jnp.int32, (SLOTS, BLOCK), 0)
    rows = lax.broadcasted_iota(jnp.int32, (SLOTS, 1), 0)
    length = jnp.zeros((SLOTS, 1), jnp.int32)
    for s in range(SLOTS):
        length = jnp.where(rows == s, lengths[me, s], length)
    member = (slots == kid).astype(F32)
    return member / jnp.maximum(length, 1).astype(F32)


def attend_kernel(where, bucket, lengths, x, wq, bq, wk, wv, bv, q_o, k_o, v_o, ctx_o, lse_o):
    width = wq.shape[1]
    me = where[1]
    tokens = x[...]
    q_o[...] = (dot(tokens, wq[...]) + bq[...]).astype(BF16)
    k_o[...] = dot(tokens, wk[...]).astype(BF16)
    v_o[...] = (dot(tokens, wv[...]) + bv[...]).astype(BF16)
    first, second = lane_masks(BF16)
    low = lax.broadcasted_iota(jnp.int32, (CHUNK, PAIR), 1) < HEAD_DIM
    lane = lax.broadcasted_iota(jnp.int32, (CHUNK, PAIR), 1)
    slot_col, _ = layout(bucket, lengths, me, 0)
    _, kid_row = layout(bucket, lengths, me, 1)
    ones = jnp.ones((BLOCK, PAIR), BF16)
    for r in range(BLOCK // CHUNK):
        rows = slice(r * CHUNK, (r + 1) * CHUNK)
        mask = slot_col[rows, :] == kid_row
        mask = jnp.concatenate([mask, mask], 0)
        levels = jnp.zeros((CHUNK, PAIR), F32)
        for pair in range(width // PAIR):
            cols = slice(pair * PAIR, (pair + 1) * PAIR)
            query = q_o[rows, cols] * jnp.asarray(HEAD_DIM**-0.5, BF16)
            both = jnp.concatenate([query * first, query * second], 0)
            scores = jnp.where(mask, dot(both, k_o[:, cols], LANES), MASKED)
            summit = jnp.max(scores, 1, keepdims=True)
            raised = jnp.exp(scores - summit).astype(BF16)
            out = dot(raised, jnp.concatenate([v_o[:, cols], ones], 1))
            mass = out[:, PAIR:]
            out = out[:, :PAIR] / mass
            ctx_o[rows, cols] = jnp.where(low, out[:CHUNK], out[CHUNK:]).astype(BF16)
            logs = jnp.log(mass) + summit
            levels = jnp.where(lane == 2 * pair, logs[:CHUNK], levels)
            levels = jnp.where(lane == 2 * pair + 1, logs[CHUNK:], levels)
        lse_o[rows, :] = levels


def whole(a):
    return pl.BlockSpec(a.shape, lambda j, *_: (0,) * len(a.shape))


def block_rows(a):
    return pl.BlockSpec((BLOCK, a.shape[1]), lambda j, where, *_: (where[1], 0))


def columns(a):
    return pl.BlockSpec((a.shape[0], TILE), lambda j, *_: (0, j))


def down_rows(a):
    return pl.BlockSpec((TILE, a.shape[1]), lambda j, *_: (j, 0))


def call(kernel, scalars, operands, in_specs, outs, out_specs, mib, steps=1, scratch=(), flops=0):
    moved = sum(a.size * a.dtype.itemsize for a in list(operands) + list(outs))
    return pl.pallas_call(
        kernel,
        grid_spec=pltpu.PrefetchScalarGridSpec(
            num_scalar_prefetch=len(scalars),
            grid=(steps,),
            in_specs=in_specs,
            out_specs=tuple(out_specs),
            scratch_shapes=list(scratch),
        ),
        out_shape=tuple(outs),
        compiler_params=params(mib),
        cost_estimate=pl.CostEstimate(flops=flops, bytes_accessed=moved, transcendentals=0),
        name=kernel.__name__,
    )(*scalars, *operands)


def attend(scalars, x, wq, bq, wk, wv, bv):
    wide, width = wq.shape
    low = shape(BLOCK, width, kind=BF16)
    outs = (low, low, low, low, shape(BLOCK, PAIR))
    operands = (x, wq, bq, wk, wv, bv)
    flops = 2 * BLOCK * width * (3 * wide + 4 * BLOCK)
    return call(
        attend_kernel, scalars, operands, [block_rows(x)] + [whole(a) for a in operands[1:]],
        outs, [whole(a) for a in outs], 40, flops=flops,
    )


def attend_back_kernel(
    where, bucket, lengths, q, k, v, ctx, lse, dctx, dqk_o, dv_o, sums_o
):
    width = q.shape[1]
    me = where[1]
    first, second = lane_masks(BF16)
    scale = jnp.asarray(HEAD_DIM**-0.5, BF16)
    head_of = lax.broadcasted_iota(jnp.int32, (width, PAIR), 0) >> 6
    select = (head_of == lax.broadcasted_iota(jnp.int32, (width, PAIR), 1)).astype(F32)
    product = dctx[...].astype(F32) * ctx[...].astype(F32)
    inner_sums = dot(select, product, ((0,), (1,)), HIGH)
    levels = jnp.transpose(lse[...])
    slots, _ = layout(bucket, lengths, me, 1)
    _, kid_col = layout(bucket, lengths, me, 0)
    sums_o[...] = jnp.zeros(sums_o.shape, F32)
    for pair in range(width // PAIR):
        cols = slice(pair * PAIR, (pair + 1) * PAIR)
        query = q[:, cols] * scale
        grad = dctx[:, cols]
        dq = [jnp.zeros((BLOCK, PAIR), F32), jnp.zeros((BLOCK, PAIR), F32)]
        sum_k = jnp.zeros((1, PAIR), F32)
        sum_v = jnp.zeros((1, PAIR), F32)
        for c in range(BLOCK // CHUNK):
            rows = slice(c * CHUNK, (c + 1) * CHUNK)
            mask = kid_col[rows, :] == slots
            key_part = k[rows, cols]
            value_part = v[rows, cols]
            dk, dv = 0.0, 0.0
            for e, here in enumerate((first, second)):
                head = 2 * pair + e
                scores = jnp.where(mask, dot(key_part * here, query, LANES), MASKED)
                probs = jnp.exp(scores - levels[head : head + 1, :])
                dprobs = dot(value_part * here, grad, LANES)
                dscores = (probs * (dprobs - inner_sums[head : head + 1, :])).astype(BF16)
                dk = dk + dot(dscores, query * here)
                dv = dv + dot(probs.astype(BF16), grad * here)
                dq[e] = dq[e] + dot(dscores, key_part * here, ROWS)
            dk, dv = dk.astype(BF16), dv.astype(BF16)
            dqk_o[rows, width + pair * PAIR : width + (pair + 1) * PAIR] = dk
            dv_o[rows, cols] = dv
            sum_k = sum_k + jnp.sum(dk.astype(F32), 0, keepdims=True)
            sum_v = sum_v + jnp.sum(dv.astype(F32), 0, keepdims=True)
        low = ((dq[0] + dq[1]) * HEAD_DIM**-0.5).astype(BF16)
        dqk_o[:, cols] = low
        sums_o[0:1, cols] = jnp.sum(low.astype(F32), 0, keepdims=True)
        sums_o[1:2, cols] = sum_k
        sums_o[2:3, cols] = sum_v


def attend_back(scalars, q, k, v, ctx, lse, dctx):
    rows, width = q.shape
    outs = (
        shape(rows, 2 * width, kind=BF16),
        shape(rows, width, kind=BF16),
        shape(8, width),
    )
    operands = (q, k, v, ctx, lse, dctx)
    return call(
        attend_back_kernel, scalars, operands, [whole(a) for a in operands],
        outs, [whole(a) for a in outs], 40, flops=20 * rows * rows * width,
    )


def normed(resid):
    center = resid - jnp.mean(resid, -1, keepdims=True)
    rate = lax.rsqrt(jnp.mean(center * center, -1, keepdims=True) + EPS)
    return center * rate, rate


def normed_back(grad, hat, rate):
    return (
        grad - jnp.mean(grad, -1, keepdims=True) - hat * jnp.mean(grad * hat, -1, keepdims=True)
    ) * rate


def feed_kernel(
    where, bucket, lengths, positive,
    x, ctx_a, ctx_b, wo_a, wo_b, bias_out, gain_one, shift_one,
    wi_a, wi_b, bi_a, bi_b, wd_a, wd_b, bias_down, gain_two, shift_two,
    hat_one_o, rate_one_o, hidden_o, act_a_o, act_b_o, slope_a_o, slope_b_o, hat_two_o, rate_two_o,
    packed_o, rate_u_o,
    total, sums, act_sums,
):
    step = pl.program_id(0)
    me = where[1]
    wide = total.shape[1]

    @pl.when(step == 0)
    def _():
        tokens = x[...].astype(F32)
        attn = dot(ctx_a[...], wo_a[...]) + dot(ctx_b[...], wo_b[...]) + bias_out[...]
        hat, rate = normed(tokens + attn)
        hidden = hat * gain_one[...] + shift_one[...]
        hat_one_o[...] = hat
        rate_one_o[...] = jnp.broadcast_to(rate, rate_one_o.shape)
        hidden_o[...] = hidden.astype(BF16)
        total[...] = hidden + bias_down[...]
        sums[...] = jnp.zeros(sums.shape, F32)
        sums[0:1, :] = jnp.sum(hidden, 0, keepdims=True)
        half = ctx_a.shape[1]
        sums[1:2, :half] = jnp.sum(ctx_a[...].astype(F32), 0, keepdims=True)
        sums[1:2, half:] = jnp.sum(ctx_b[...].astype(F32), 0, keepdims=True)
        sums[2:3, :] = jnp.sum(tokens, 0, keepdims=True)

    hidden = hidden_o[...]
    place = pl.ds(pl.multiple_of(step * TILE, TILE), TILE)
    for side, (wi, bi, wd, act_o, slope_o) in enumerate((
        (wi_a, bi_a, wd_a, act_a_o, slope_a_o),
        (wi_b, bi_b, wd_b, act_b_o, slope_b_o),
    )):
        inner = dot(hidden, wi[...]) + bi[...]
        below = 0.5 + 0.5 * lax.erf(inner * (0.5**0.5))
        bell = jnp.exp(inner * inner * -0.5) * 0.3989422804014327
        act = inner * below
        act_sums[side : side + 1, place] = jnp.sum(act, 0, keepdims=True)
        act = act.astype(BF16)
        act_o[...] = act
        slope_o[...] = (below + inner * bell).astype(BF16)
        total[...] += dot(act, wd[...])

    @pl.when(step == pl.num_programs(0) - 1)
    def _():
        hat, rate = normed(total[...])
        hat_two_o[...] = hat
        rate_two_o[...] = jnp.broadcast_to(rate, rate_two_o.shape)
        output = hat * gain_two[...] + shift_two[...]
        raw = dot(pooling(bucket, lengths, me), output, precision=HIGH)
        rate_u = lax.rsqrt(jnp.sum(raw * raw, 1, keepdims=True) + 1e-06)
        rate_u_o[...] = jnp.broadcast_to(rate_u, rate_u_o.shape)
        packed_o[...] = raw * rate_u

        @pl.when(me == 1)
        def _():
            lane = lax.broadcasted_iota(jnp.int32, (1, wide), 1)
            extra = jnp.zeros((1, wide), jnp.int32)
            for s in range(SLOTS):
                extra = jnp.where(lane == s, positive[s], extra)
            for s in range(2):
                extra = jnp.where(lane == SLOTS + s, bucket[s], extra)
            packed_o[4:5, :] = extra.astype(F32)
            packed_o[5:6, :] = act_sums[0:1, :wide]
            packed_o[6:7, :] = act_sums[0:1, wide:]
            packed_o[7:8, :] = act_sums[1:2, :wide]
            packed_o[8:9, :] = act_sums[1:2, wide:]
            packed_o[9:12, :] = sums[0:3, :]


TILE = 256


def feed(scalars, x, ctx, wo, bias_out, gain_one, shift_one, wi, bi, wd, bias_down, gain_two, shift_two):
    rows, wide = BLOCK, x.shape[1]
    units = wi[0].shape[1]
    full = shape(rows, wide)
    rate = shape(rows, PAIR)
    low = shape(rows, units, kind=BF16)
    hidden = shape(rows, wide, kind=BF16)
    operands = (
        x, ctx[0], ctx[1], wo[0], wo[1], bias_out, gain_one, shift_one,
        wi[0], wi[1], bi[0], bi[1], wd[0], wd[1], bias_down, gain_two, shift_two,
    )
    specs = [block_rows(x)] + [whole(a) for a in operands[1:]]
    for place in (8, 9, 10, 11):
        specs[place] = columns(operands[place])
    for place in (12, 13):
        specs[place] = down_rows(operands[place])
    outs = (
        full, rate, hidden, low, low, low, low, full, rate, shape(SLOTS, wide), shape(SLOTS, PAIR),
    )
    out_specs = [whole(a) for a in outs]
    for place in (3, 4, 5, 6):
        out_specs[place] = columns(outs[place])
    scratch = [pltpu.VMEM((rows, wide), F32), pltpu.VMEM((8, wide), F32), pltpu.VMEM((8, units), F32)]
    return call(
        feed_kernel, scalars, operands, specs, outs, out_specs, 48, units // TILE, scratch,
        flops=2 * rows * wide * (wide + 4 * units),
    )


def turn_kernel(act_a, act_b, hidden, ctx_a, ctx_b, x, act_a_o, act_b_o, hidden_o, ctx_a_o, ctx_b_o, x_o):
    act_a_o[...] = jnp.transpose(act_a[...])
    act_b_o[...] = jnp.transpose(act_b[...])
    step = pl.program_id(0)

    @pl.when(step < 3)
    def _():
        hidden_o[...] = jnp.transpose(hidden[...])
        x_o[...] = jnp.transpose(x[...])

    @pl.when(step >= 3)
    def _():
        ctx_a_o[...] = jnp.transpose(ctx_a[...])
        ctx_b_o[...] = jnp.transpose(ctx_b[...])


def turn(where, act, hidden, ctx, x):
    wide = x.shape[1]
    operands = (act[0], act[1], hidden, ctx[0], ctx[1], x)

    def wrapped(where, *refs):
        turn_kernel(*refs)

    wrapped.__name__ = "turn"

    def early(width):
        return lambda j, *_: jnp.minimum(j, 2)

    def late(j, *_):
        return jnp.maximum(j - 3, 0)

    def first(j, *_):
        return jnp.minimum(j, 2)

    tile = (BLOCK, TILE)
    in_specs = [
        columns(act[0]),
        columns(act[1]),
        pl.BlockSpec(tile, lambda j, *_: (0, first(j))),
        pl.BlockSpec((BLOCK, PAIR), lambda j, *_: (0, late(j))),
        pl.BlockSpec((BLOCK, PAIR), lambda j, *_: (0, late(j))),
        pl.BlockSpec(tile, lambda j, where: (where[1], first(j))),
    ]
    turned = (TILE, BLOCK)
    out_specs = [
        pl.BlockSpec(turned, lambda j, *_: (j, 0)),
        pl.BlockSpec(turned, lambda j, *_: (j, 0)),
        pl.BlockSpec(turned, lambda j, *_: (first(j), 0)),
        pl.BlockSpec((PAIR, BLOCK), lambda j, *_: (late(j), 0)),
        pl.BlockSpec((PAIR, BLOCK), lambda j, *_: (late(j), 0)),
        pl.BlockSpec(turned, lambda j, *_: (first(j), 0)),
    ]
    outs = [shape(a.shape[1], BLOCK, kind=BF16) for a in operands]
    return call(
        wrapped, (where,), operands, in_specs, outs, out_specs, 24, act[0].shape[1] // TILE
    )


def contrast_kernel(offsets, count, where, bucket, lengths, *refs):
    pieces = len(offsets)
    own, other = refs[:pieces], refs[pieces : 2 * pieces]
    packed, rate_u, hat, rate, gain = refs[2 * pieces : 2 * pieces + 5]
    loss_o, query_o, passage_o, grad_o, low_o, sums_o, common_o = refs[2 * pieces + 5 : 2 * pieces + 12]
    asks, table, notes, place_col, live_col, dlogits, common, grad_unit = refs[2 * pieces + 12 :]
    spot, me = where[0], where[1]
    wide = hat.shape[1]
    rows16 = lax.broadcasted_iota(jnp.int32, (8, 1), 0)
    common[...] = jnp.zeros(common.shape, F32)
    notes[...] = jnp.zeros(notes.shape, F32)

    def spread(query_pieces, passage_pieces):
        for piece, places in zip(query_pieces, offsets):
            for i, offset in enumerate(places):
                source = spot ^ offset
                asks[pl.ds(pl.multiple_of(source * SLOTS, SLOTS), SLOTS), :] = piece[i]
        for piece, places in zip(passage_pieces, offsets):
            for i, offset in enumerate(places):
                source = spot ^ offset
                top = piece[i, 0:8, :]
                table[pl.ds(pl.multiple_of(source * 8, 8), 8), :] = jnp.where(rows16 < 4, top, 0.0)
                notes[pl.ds(source, 1), :] = top[4:5, :PAIR]
                common[0:8, :] += top
                common[8:16, :] += piece[i, 8:16, :]

    @pl.when(me == 0)
    def _():
        spread(own, other)

    @pl.when(me == 1)
    def _():
        spread(other, own)

    share = 1.0 / (count * BLOCK)
    first, second = common[5:7, :] * share, common[7:9, :] * share
    common_o[0:2, :] = jnp.where(me == 1, first, second)
    common_o[2:4, :] = jnp.where(me == 1, second, first)
    common_o[4:7, :] = common[9:12, :] * share
    common_o[7:8, :] = jnp.zeros((1, wide), F32)
    half = wide // 2

    @pl.when(me == 0)
    def _():
        common_o[5:6, :half] = common[10:11, half:] * share
        common_o[5:6, half:] = common[10:11, :half] * share

    turned = jnp.transpose(notes[...])
    slots = lax.broadcasted_iota(jnp.int32, (SLOTS, 1), 0).astype(F32)
    for d in range(count):
        at = slice(d * SLOTS, (d + 1) * SLOTS)
        place_col[at, :] = jnp.broadcast_to(turned[0:SLOTS, d : d + 1], (SLOTS, PAIR))
        held = jnp.where(turned[SLOTS : SLOTS + 1, d : d + 1] == 0.0, 16.0, 8.0)
        live_col[at, :] = jnp.broadcast_to((slots < held).astype(F32), (SLOTS, PAIR))
    wide_p = table.shape[0]
    cells = lax.broadcasted_iota(jnp.int32, (PAIR, wide_p), 1)
    sources = lax.broadcasted_iota(jnp.int32, (PAIR, wide_p), 0)
    held = jnp.where(notes[:, SLOTS + 1 : SLOTS + 2] == 2.0, 4, 1)
    live_p = ((cells >> 3) == sources) & ((cells & 7) < held)
    live_p = jnp.sum(live_p.astype(F32), 0, keepdims=True)

    count_q = jnp.sum(live_col[:, :1], 0, keepdims=True)
    rows_q = min(asks.shape[0], BLOCK // 2)

    def part(i, total):
        at = pl.ds(pl.multiple_of(i * rows_q, rows_q), rows_q)
        alive = live_col[at, :][:, :1]
        places = place_col[at, :][:, :1].astype(jnp.int32)
        places = (places >> 2) * 8 + (places & 3)
        logits = dot(asks[at, :], table[...], LANES, HIGH) / TEMP
        logits = jnp.where(live_p > 0, logits, MASKED)
        summit = jnp.max(logits, 1, keepdims=True)
        raised = jnp.exp(logits - summit)
        mass = jnp.sum(raised, 1, keepdims=True)
        normal = summit + jnp.log(mass)
        target = lax.broadcasted_iota(jnp.int32, logits.shape, 1) == places
        picked = jnp.sum(jnp.where(target, logits, 0.0), 1, keepdims=True)
        dlogits[at, :] = (jnp.exp(logits - normal) - target.astype(F32)) * (alive / count_q)
        return total + jnp.sum(alive * (normal - picked), 0, keepdims=True)

    total = jnp.zeros((1, 1), F32)
    if asks.shape[0] == rows_q:
        total = part(0, total)
    else:
        total = lax.fori_loop(0, asks.shape[0] // rows_q, part, total)
    loss_o[...] = total / count_q

    query_o[...] = asks[pl.ds(pl.multiple_of(spot * SLOTS, SLOTS), SLOTS), :]
    passage_o[...] = table[pl.ds(pl.multiple_of(spot * 8, 8), 8), :][0:4, :]

    @pl.when(me == 0)
    def _():
        mine = dlogits[pl.ds(pl.multiple_of(spot * SLOTS, SLOTS), SLOTS), :]
        grad_unit[...] = dot(mine, table[...], precision=HIGH) / TEMP

    @pl.when(me == 1)
    def _():
        cell = lax.broadcasted_iota(jnp.int32, (SLOTS, wide_p), 1)
        slot = lax.broadcasted_iota(jnp.int32, (SLOTS, wide_p), 0)
        mine = ((cell == slot + spot * 8) & (slot < 4)).astype(F32)
        weights = dot(mine, dlogits[...], LANES, HIGH)
        grad_unit[...] = dot(weights, asks[...], precision=HIGH) / TEMP

    slot = lax.broadcasted_iota(jnp.int32, (SLOTS, 1), 0)
    units = jnp.where((slot < 4) | (me == 0), packed[...], 0.0)
    grads = grad_unit[...]
    grad_embed = (grads - units * jnp.sum(units * grads, 1, keepdims=True)) * rate_u[:, :1]
    grad_out = dot(pooling(bucket, lengths, me), grad_embed, ROWS, HIGH)
    hats = hat[...]
    resid = normed_back(grad_out * gain[...], hats, rate[:, :1])
    grad_o[...] = resid
    low = resid.astype(BF16)
    low_o[...] = low
    sums_o[0:1, :] = jnp.sum(grad_out * hats, 0, keepdims=True)
    sums_o[1:2, :] = jnp.sum(grad_out, 0, keepdims=True)
    sums_o[2:3, :] = jnp.sum(low.astype(F32), 0, keepdims=True)
    sums_o[3:8, :] = jnp.zeros((5, wide), F32)


def contrast(scalars, own, other, offsets, packed, rate_u, hat, rate, gain):
    rows, wide = hat.shape
    count = sum(len(o) for o in offsets)
    operands = (*own, *other, packed, rate_u, hat, rate, gain)
    outs = (
        shape(1, 1), shape(SLOTS, wide), shape(4, wide), shape(rows, wide),
        shape(rows, wide, kind=BF16), shape(8, wide), shape(8, wide),
    )
    queries, passages = count * SLOTS, count * 8
    scratch = [
        pltpu.VMEM(dims, F32)
        for dims in (
            (queries, wide), (passages, wide), (PAIR, PAIR), (queries, PAIR), (queries, PAIR),
            (queries, passages), (SLOTS, wide), (SLOTS, wide),
        )
    ]
    kernel = partial(contrast_kernel, offsets, count)
    kernel.__name__ = "contrast"
    specs = [whole(a) for a in operands]
    return call(
        kernel, scalars, operands, specs, outs, [whole(a) for a in outs],
        40 if count <= 16 else 62, 1, scratch, flops=2_000_000_000,
    )


def feed_back_kernel(
    where, dffn, gres, wd_a, wd_b, wi_a, wi_b, slope_a, slope_b, hat, rate, gain,
    inner_a_o, inner_b_o, bias_a_o, bias_b_o, grad_o, low_o, sums_o,
    total,
):
    step = pl.program_id(0)

    @pl.when(step == 0)
    def _():
        total[...] = gres[...]

    for wd, wi, slope, inner_o, bias_o in (
        (wd_a, wi_a, slope_a, inner_a_o, bias_a_o),
        (wd_b, wi_b, slope_b, inner_b_o, bias_b_o),
    ):
        inner = (dot(dffn[...], wd[...], LANES) * slope[...].astype(F32)).astype(BF16)
        inner_o[...] = inner
        bias_o[...] = jnp.sum(inner.astype(F32), 0, keepdims=True)
        total[...] += dot(inner, wi[...], LANES)

    @pl.when(step == pl.num_programs(0) - 1)
    def _():
        grad = total[...]
        hats = hat[...]
        resid = normed_back(grad * gain[...], hats, rate[:, :1])
        grad_o[...] = resid
        low = resid.astype(BF16)
        low_o[...] = low
        sums_o[0:1, :] = jnp.sum(grad * hats, 0, keepdims=True)
        sums_o[1:2, :] = jnp.sum(grad, 0, keepdims=True)
        sums_o[2:3, :] = jnp.sum(low.astype(F32), 0, keepdims=True)
        sums_o[3:8, :] = jnp.zeros((5, sums_o.shape[1]), F32)


def feed_back(where, dffn, gres, wd, wi, slope, hat, rate, gain):
    rows, wide = dffn.shape
    units = wd[0].shape[0]
    operands = (dffn, gres, wd[0], wd[1], wi[0], wi[1], slope[0], slope[1], hat, rate, gain)
    specs = [whole(a) for a in operands]
    for place in (2, 3):
        specs[place] = down_rows(operands[place])
    for place in (4, 5, 6, 7):
        specs[place] = columns(operands[place])
    low = shape(rows, units, kind=BF16)
    bias = shape(1, units)
    outs = (low, low, bias, bias, shape(rows, wide), shape(rows, wide, kind=BF16), shape(8, wide))
    out_specs = [whole(a) for a in outs]
    for place in (0, 1, 2, 3):
        out_specs[place] = columns(outs[place])
    return call(
        feed_back_kernel, (where,), operands, specs, outs, out_specs, 48, units // TILE,
        [pltpu.VMEM((rows, wide), F32)], flops=8 * rows * wide * units,
    )


def swap(tensor):
    return lax.ppermute(tensor, "mp", [(0, 1), (1, 0)])


def flip(tensor, bits):
    count = lax.axis_size("dp")
    return lax.ppermute(tensor, "dp", [(i, i ^ bits) for i in range(count)])


def bit_count():
    return lax.axis_size("dp").bit_length() - 1


def tie(*tensors):
    return lax.optimization_barrier(tensors)


def halve(tensor, bit):
    half = tensor.shape[0] // 2
    side = (lax.axis_index("dp") >> bit) & 1
    gone = lax.dynamic_slice_in_dim(tensor, (1 - side) * half, half, 0)
    kept = lax.dynamic_slice_in_dim(tensor, side * half, half, 0)
    return (kept.astype(F32) + flip(gone, 1 << bit).astype(F32)).astype(BF16)


def double(tensor, bit):
    other = flip(tensor, 1 << bit)
    side = (lax.axis_index("dp") >> bit) & 1
    return jnp.where(
        side == 0, jnp.concatenate([tensor, other], 0), jnp.concatenate([other, tensor], 0)
    )


def gather_small(tensor):
    bits = list(range(bit_count()))
    groups = []
    while bits:
        groups.append(bits[-2:])
        bits = bits[:-2]
    tensor, offsets = tensor[None], [0]
    for number, group in enumerate(groups):
        ways = range(1 << len(group))
        pieces = [tensor] + [flip(tensor, way << group[0]) for way in ways if way]
        places = [[(way << group[0]) | o for o in offsets] for way in ways]
        if number == len(groups) - 1:
            return pieces, places
        tensor = jnp.concatenate(pieces, 0)
        offsets = [o for part in places for o in part]


def shards(
    tokens_in, proj_query, bias_query, proj_key, proj_value, bias_value, proj_out, bias_out,
    gain_attn, shift_attn, proj_in, bias_in, proj_down, bias_down, gain_ffn, shift_ffn,
    bucket, lengths, positive,
):
    spot, me = lax.axis_index("dp"), lax.axis_index("mp")
    wide = tokens_in.shape[1]
    width = proj_query.shape[1]
    units = proj_in.shape[1]
    where = jnp.stack([spot, me]).astype(jnp.int32)
    scalars = (where, bucket, lengths)
    x = tokens_in

    wq, wk, wv, wo = [(w, swap(w)) for w in (proj_query, proj_key, proj_value, proj_out)]
    wi, wd = [(w, swap(w)) for w in (proj_in, proj_down)]
    bq, bv, bi = [(b[None], swap(b)[None]) for b in (bias_query, bias_value, bias_in)]

    heads = [attend(scalars, x, wq[i], bq[i], wk[i], wv[i], bv[i]) for i in range(2)]
    ctx = [h[3] for h in heads]
    (hat_one, rate_one, hidden, act_a, act_b, slope_a, slope_b, hat_two, rate_two, packed, rate_u) = feed(
        scalars + (positive,), x, ctx, wo, bias_out[None], gain_attn[None], shift_attn[None], wi, bi, wd,
        bias_down[None], gain_ffn[None], shift_ffn[None],
    )

    own, offsets = gather_small(packed)
    other = [swap(piece) for piece in own]
    act_a, act_b, hidden, ctx_a, ctx_b, x_t = turn(where, (act_a, act_b), hidden, ctx, x)
    tied = tie(act_a, act_b, hidden, ctx_a, ctx_b, x_t, *own, *other)
    act_t, hidden_t, ctx_t, x_t = tied[:2], tied[2], tied[3:5], tied[5]
    own, other = tied[6 : 6 + len(own)], tied[6 + len(own) :]

    loss, query_embed, passage_embed, gres_two, dffn, sums_two, common = contrast(
        scalars, own, other, offsets, packed, rate_u, hat_two, rate_two, gain_ffn[None]
    )
    act_mean = [common[0:2].reshape(units), common[2:4].reshape(units)]
    hidden_mean, x_mean = common[4], common[6]
    ctx_mean = [common[5, :width], common[5, width:]]

    def outer(mean, sums):
        return mean[:, None] * sums[None, :]

    def total(own, sent):
        return (own + swap(sent.astype(BF16)).astype(F32)).astype(BF16)

    bits = bit_count()
    rest = list(range(2, bits))
    order = ([0, 1] + rest, [1, 0] + rest)
    half = units // 2
    cuts = (slice(0, half), slice(half, units))

    def level(tensors, step):
        return [halve(t, o[step]) for t, o in zip(tensors, order)]

    def levels(tensors, steps):
        for step in steps:
            tensors = level(tensors, step)
        return tensors

    def spread(tensors):
        for step in reversed(range(bits)):
            tensors = [double(t, o[step]) for t, o in zip(tensors, order)]
        return [t.astype(F32) for t in tensors]

    down_sum = sums_two[2]

    def down_part(i, cut):
        return dot(act_t[i][cut], dffn) - outer(act_mean[i][cut], down_sum)

    down = [total(down_part(0, cut), down_part(1, cut)) for cut in cuts]
    dffn, *down = tie(dffn, *down)
    inner_a, inner_b, bias_a, bias_b, gres_one, dattn, sums_one = feed_back(
        where, dffn, gres_two, wd, wi, (slope_a, slope_b), hat_one, rate_one, gain_attn[None]
    )
    down = level(down, 0)
    inner_a, inner_b, dattn, *down = tie(inner_a, inner_b, dattn, *down)
    inner, bias = (inner_a, inner_b), (bias_a[0], bias_b[0])

    def in_part(i, cut):
        return dot(hidden_t, inner[i][:, cut]) - outer(hidden_mean, bias[i][cut])

    into = [total(in_part(0, cut), in_part(1, cut)) for cut in cuts]
    down = level(down, 1)
    dattn, *rest_ = tie(dattn, *into, *down)
    into, down = rest_[:2], rest_[2:]
    dctx = [dot(dattn, w, LANES).astype(BF16) for w in wo]
    backs = [
        attend_back(scalars, *h, d) for h, d in zip(heads, dctx)
    ]
    down = levels(down, range(2, bits))
    into = level(into, 0)
    tied = tie(*backs[0], *backs[1], *down, *into)
    backs, down, into = (tied[0:3], tied[3:6]), tied[6:8], tied[8:10]

    def attn_part(i):
        dqk, dv, sums = backs[i]
        qk = dot(x_t, dqk) - outer(x_mean, sums[0:2].reshape(2 * width))
        v = dot(x_t, dv) - outer(x_mean, sums[2])
        cut = wide // 2
        outs = [
            dot(ctx_t[i], dattn[:, at]) - outer(ctx_mean[i], sums_one[2, at])
            for at in (slice(0, cut), slice(cut, wide))
        ]
        return qk, jnp.concatenate([v, jnp.concatenate(outs, 0)], 1)

    attn = [total(*pair) for pair in zip(attn_part(0), attn_part(1))]
    into = level(into, 1)
    tied = tie(*attn, *into)
    attn, into = tied[:2], tied[2:]
    down = spread(down)
    into = spread(levels(into, range(2, bits)))
    attn = spread(levels(attn, range(bits)))

    grad_in = gres_one
    for i in range(2):
        dqk, dv, _ = backs[i]
        grad_in = grad_in + dot(dqk[:, :width], wq[i], LANES) + dot(dqk[:, width:], wk[i], LANES)
        grad_in = grad_in + dot(dv, wv[i], LANES)
    grad_in = grad_in.astype(BF16)
    other_in = swap(grad_in)
    grad_input = jnp.where(
        me == 0,
        jnp.concatenate([grad_in, other_in], 0),
        jnp.concatenate([other_in, grad_in], 0),
    )

    def vectors(i):
        rows = [backs[i][2][0:3].reshape(-1), bias[i], jnp.zeros(width, F32)]
        return jnp.concatenate(
            [sums_two[0:3], sums_one[0:3], jnp.concatenate(rows).reshape(-1, wide)], 0
        )

    small = vectors(0) + swap(vectors(1))
    for bit in range(bits):
        small = small + flip(small, 1 << bit)

    share = lax.dynamic_slice_in_dim(small[0:6], me * width, width, 1)
    d_g2, d_s2, d_bd, d_g1, d_s1, d_bo = [share[i] for i in range(6)]
    own_half = small[6:].reshape(-1)
    d_bq, d_bk, d_bv = [own_half[i * width : (i + 1) * width] for i in range(3)]
    d_bi = own_half[3 * width : 3 * width + units]
    grad_qk = attn[0] + outer(x_mean, own_half[: 2 * width])
    grad_out = jnp.concatenate([attn[1][:width, width:], attn[1][width:, width:]], 1)
    return (
        loss[0, 0],
        query_embed,
        passage_embed,
        grad_input,
        grad_qk[:, :width],
        d_bq,
        grad_qk[:, width:],
        attn[1][:, :width] + outer(x_mean, d_bv),
        d_bv,
        grad_out + outer(ctx_mean[0], small[5]),
        d_bo,
        d_g1,
        d_s1,
        jnp.concatenate(into, 1) + outer(hidden_mean, d_bi),
        d_bi,
        jnp.concatenate(down, 0) + outer(act_mean[0], small[2]),
        d_bd,
        d_g2,
        d_s2,
    )


def solution(mesh):
    half, rows = P(None, "mp"), P("mp", None)
    return jax.shard_map(
        shards,
        mesh=mesh,
        in_specs=(
            P("dp", None), half, P("mp"), half, half, P("mp"), rows, P(), P(), P(),
            half, P("mp"), rows, P(), P(), P(), P("dp"), P("dp", None), P("dp"),
        ),
        out_specs=(
            P(), P("dp", None), P("dp", None), P("dp", None),
            half, P("mp"), half, half, P("mp"), rows, P("mp"), P("mp"), P("mp"),
            half, P("mp"), rows, P("mp"), P("mp"), P("mp"),
        ),
        check_vma=False,
    )
```

```python
from functools import partial

import jax
import jax.numpy as jnp
from jax import lax
from jax.experimental import pallas as pl
from jax.experimental.pallas import tpu as pltpu
from jax.sharding import PartitionSpec as P

HEAD_DIM = 64
BLOCK = 512
PAIR = 2 * HEAD_DIM
CHUNK = 128
SLOTS = 16
EPS = 1e-05
TEMP = 0.01
MASKED = -10000.0
HIGH = lax.Precision.HIGHEST
F32 = jnp.float32
BF16 = jnp.bfloat16
VMEM = pl.BlockSpec(memory_space=pltpu.VMEM)
SMEM = pl.BlockSpec(memory_space=pltpu.SMEM)


def dot(a, b, dims=((1,), (0,)), precision=None):
    return lax.dot_general(a, b, (dims, ((), ())), precision=precision, preferred_element_type=F32)


ROWS = ((0,), (0,))
LANES = ((1,), (1,))


def params(mib):
    return pltpu.CompilerParams(vmem_limit_bytes=mib * 1024 * 1024)


def row(ref):
    return ref[...].reshape(1, ref.shape[0])


def shape(*dims, kind=F32):
    return jax.ShapeDtypeStruct(dims, kind)


def lane_masks(kind):
    first = (lax.broadcasted_iota(jnp.int32, (1, PAIR), 1) < HEAD_DIM).astype(F32)
    return first.astype(kind), (1.0 - first).astype(kind)


def layout(bucket, lengths, me, axis):
    code = bucket[me]
    dims = (BLOCK, 1) if axis == 0 else (1, BLOCK)
    places = lax.broadcasted_iota(jnp.int32, dims, axis)
    shift = jnp.full(dims, jnp.where(code == 3, 9, 5 + code), jnp.int32)
    slot = lax.shift_right_logical(places, shift)
    offset = places - lax.shift_left(slot, shift)
    length = jnp.zeros(dims, jnp.int32)
    for s in range(SLOTS):
        length = jnp.where(slot == s, lengths[me, s], length)
    return slot, jnp.where(offset < length, slot, -1)


def pooling(bucket, lengths, me):
    _, kid = layout(bucket, lengths, me, 1)
    slots = lax.broadcasted_iota(jnp.int32, (SLOTS, BLOCK), 0)
    rows = lax.broadcasted_iota(jnp.int32, (SLOTS, 1), 0)
    length = jnp.zeros((SLOTS, 1), jnp.int32)
    for s in range(SLOTS):
        length = jnp.where(rows == s, lengths[me, s], length)
    member = (slots == kid).astype(F32)
    return member / jnp.maximum(length, 1).astype(F32)


def attend_kernel(
    where, bucket, lengths,
    x, wq_a, wq_b, bq_a, bq_b, wk_a, wk_b, wv_a, wv_b, bv_a, bv_b,
    q_a, q_b, k_a, k_b, v_a, v_b, ctx_a, ctx_b, lse_a, lse_b, x_t,
):
    width = wq_a.shape[1]
    me = where[1]
    tokens = x[...]
    x_t[...] = jnp.transpose(tokens)
    first, second = lane_masks(BF16)
    low = lax.broadcasted_iota(jnp.int32, (CHUNK, PAIR), 1) < HEAD_DIM
    lane = lax.broadcasted_iota(jnp.int32, (CHUNK, PAIR), 1)
    slot_col, _ = layout(bucket, lengths, me, 0)
    _, kid_row = layout(bucket, lengths, me, 1)
    ones = jnp.ones((BLOCK, PAIR), BF16)
    for wq, bq, wk, wv, bv, q_o, k_o, v_o, ctx_o, lse_o in (
        (wq_a, bq_a, wk_a, wv_a, bv_a, q_a, k_a, v_a, ctx_a, lse_a),
        (wq_b, bq_b, wk_b, wv_b, bv_b, q_b, k_b, v_b, ctx_b, lse_b),
    ):
        q_o[...] = (dot(tokens, wq[...]) + row(bq)).astype(BF16)
        k_o[...] = dot(tokens, wk[...]).astype(BF16)
        v_o[...] = (dot(tokens, wv[...]) + row(bv)).astype(BF16)
        for r in range(BLOCK // CHUNK):
            rows = slice(r * CHUNK, (r + 1) * CHUNK)
            mask = slot_col[rows, :] == kid_row
            mask = jnp.concatenate([mask, mask], 0)
            levels = jnp.zeros((CHUNK, PAIR), F32)
            for pair in range(width // PAIR):
                cols = slice(pair * PAIR, (pair + 1) * PAIR)
                query = q_o[rows, cols] * jnp.asarray(HEAD_DIM**-0.5, BF16)
                both = jnp.concatenate([query * first, query * second], 0)
                scores = jnp.where(mask, dot(both, k_o[:, cols], LANES), MASKED)
                summit = jnp.max(scores, 1, keepdims=True)
                raised = jnp.exp(scores - summit).astype(BF16)
                out = dot(raised, jnp.concatenate([v_o[:, cols], ones], 1))
                mass = out[:, PAIR:]
                out = out[:, :PAIR] / mass
                ctx_o[rows, cols] = jnp.where(low, out[:CHUNK], out[CHUNK:]).astype(BF16)
                logs = jnp.log(mass) + summit
                levels = jnp.where(lane == 2 * pair, logs[:CHUNK], levels)
                levels = jnp.where(lane == 2 * pair + 1, logs[CHUNK:], levels)
            lse_o[rows, :] = levels


def whole(a):
    return pl.BlockSpec(a.shape, lambda j, *_: (0,) * len(a.shape))


def block_rows(a):
    return pl.BlockSpec((BLOCK, a.shape[1]), lambda j, where, *_: (where[1], 0))


def columns(a):
    return pl.BlockSpec((a.shape[0], TILE), lambda j, *_: (0, j))


def down_rows(a):
    return pl.BlockSpec((TILE, a.shape[1]), lambda j, *_: (j, 0))


def call(
    kernel, scalars, operands, in_specs, outs, out_specs, steps=1, scratch=(), flops=0, mib=60, far=()
):
    operands = [
        pltpu.with_memory_space_constraint(a, pltpu.HBM) if i in far else a
        for i, a in enumerate(operands)
    ]
    moved = sum(a.size * a.dtype.itemsize for a in list(operands) + list(outs))
    return pl.pallas_call(
        kernel,
        grid_spec=pltpu.PrefetchScalarGridSpec(
            num_scalar_prefetch=len(scalars),
            grid=(steps,),
            in_specs=in_specs,
            out_specs=tuple(out_specs),
            scratch_shapes=list(scratch),
        ),
        out_shape=tuple(outs),
        compiler_params=params(mib),
        cost_estimate=pl.CostEstimate(flops=flops, bytes_accessed=moved, transcendentals=0),
        name=kernel.__name__,
    )(*scalars, *operands)


def attend(scalars, x, wq, bq, wk, wv, bv):
    wide, width = wq[0].shape
    low, level = shape(BLOCK, width, kind=BF16), shape(BLOCK, PAIR)
    outs = (low,) * 8 + (level,) * 2 + (shape(wide, BLOCK, kind=BF16),)
    operands = (x, *wq, *bq, *wk, *wv, *bv)
    flops = 4 * BLOCK * width * (3 * wide + 4 * BLOCK)
    *halves, x_t = call(
        attend_kernel, scalars, operands, [block_rows(x)] + [whole(a) for a in operands[1:]],
        outs, [whole(a) for a in outs], flops=flops,
    )
    return halves[0::2], halves[1::2], x_t


def attend_back_kernel(
    side, where, bucket, lengths,
    q, k, v, ctx, lse, dattn, wo, x_t, means, sums_one,
    part_o, dqk_o, dv_o, sums_o,
):
    width = q.shape[1]
    wide = dattn.shape[1]
    me = where[1]
    first, second = lane_masks(BF16)
    scale = jnp.asarray(HEAD_DIM**-0.5, BF16)
    dctx = dot(dattn[...], wo[...], LANES).astype(BF16)
    context = ctx[...]
    head_of = lax.broadcasted_iota(jnp.int32, (width, PAIR), 0) >> 6
    select = (head_of == lax.broadcasted_iota(jnp.int32, (width, PAIR), 1)).astype(F32)
    inner_sums = dot(select, dctx.astype(F32) * context.astype(F32), ((0,), (1,)), HIGH)
    levels = jnp.transpose(lse[...])
    slots, _ = layout(bucket, lengths, me, 1)
    _, kid_col = layout(bucket, lengths, me, 0)
    sums_o[...] = jnp.zeros(sums_o.shape, F32)
    for pair in range(width // PAIR):
        cols = slice(pair * PAIR, (pair + 1) * PAIR)
        query = q[:, cols] * scale
        grad = dctx[:, cols]
        dq = [jnp.zeros((BLOCK, PAIR), F32), jnp.zeros((BLOCK, PAIR), F32)]
        sum_k = jnp.zeros((1, PAIR), F32)
        sum_v = jnp.zeros((1, PAIR), F32)
        for c in range(BLOCK // CHUNK):
            rows = slice(c * CHUNK, (c + 1) * CHUNK)
            mask = kid_col[rows, :] == slots
            key_part = k[rows, cols]
            value_part = v[rows, cols]
            dk, dv = 0.0, 0.0
            for e, here in enumerate((first, second)):
                head = 2 * pair + e
                scores = jnp.where(mask, dot(key_part * here, query, LANES), MASKED)
                probs = jnp.exp(scores - levels[head : head + 1, :])
                dprobs = dot(value_part * here, grad, LANES)
                dscores = (probs * (dprobs - inner_sums[head : head + 1, :])).astype(BF16)
                dk = dk + dot(dscores, query * here)
                dv = dv + dot(probs.astype(BF16), grad * here)
                dq[e] = dq[e] + dot(dscores, key_part * here, ROWS)
            dk, dv = dk.astype(BF16), dv.astype(BF16)
            dqk_o[rows, width + pair * PAIR : width + (pair + 1) * PAIR] = dk
            dv_o[rows, cols] = dv
            sum_k = sum_k + jnp.sum(dk.astype(F32), 0, keepdims=True)
            sum_v = sum_v + jnp.sum(dv.astype(F32), 0, keepdims=True)
        low = ((dq[0] + dq[1]) * HEAD_DIM**-0.5).astype(BF16)
        dqk_o[:, cols] = low
        sums_o[0:1, cols] = jnp.sum(low.astype(F32), 0, keepdims=True)
        sums_o[1:2, cols] = sum_k
        sums_o[2:3, cols] = sum_v
    x_mean = means[:, 6:7]
    for i, (source, at) in enumerate(((dqk_o, 0), (dqk_o, width), (dv_o, 0))):
        grads = dot(x_t[...], source[:, at : at + width]) - x_mean * sums_o[i : i + 1, :]
        part_o[:, i * width : (i + 1) * width] = grads.astype(BF16)
    turned = jnp.transpose(context)
    ctx_mean = means[side * width : (side + 1) * width, 5:6]
    grads = dot(turned, dattn[...]) - ctx_mean * sums_one[2:3, :]
    part_o[:width, 3 * width :] = grads[:, :width].astype(BF16)
    part_o[width:, 3 * width :] = grads[:, width:].astype(BF16)


def attend_back(side, scalars, q, k, v, ctx, lse, dattn, wo, x_t, means, sums_one):
    rows, width = q.shape
    wide = dattn.shape[1]
    outs = (
        shape(wide, 4 * width, kind=BF16),
        shape(rows, 2 * width, kind=BF16),
        shape(rows, width, kind=BF16),
        shape(8, width),
    )
    operands = (q, k, v, ctx, lse, dattn, wo, x_t, means, sums_one)
    kernel = partial(attend_back_kernel, side)
    kernel.__name__ = "attend_back"
    return call(
        kernel, scalars, operands, [whole(a) for a in operands],
        outs, [whole(a) for a in outs], flops=24 * rows * rows * width,
    )


def normed(resid):
    center = resid - jnp.mean(resid, -1, keepdims=True)
    rate = lax.rsqrt(jnp.mean(center * center, -1, keepdims=True) + EPS)
    return center * rate, rate


def normed_back(grad, hat, rate):
    return (
        grad - jnp.mean(grad, -1, keepdims=True) - hat * jnp.mean(grad * hat, -1, keepdims=True)
    ) * rate


def feed_kernel(
    where, bucket, lengths, positive,
    x, ctx_a, ctx_b, wo_a, wo_b, bias_out, gain_one, shift_one,
    wi_a, wi_b, bi_a, bi_b, wd_a, wd_b, bias_down, gain_two, shift_two,
    hat_one_o, rate_one_o, hidden_t_o, act_a_o, act_b_o, slope_a_o, slope_b_o, hat_two_o, rate_two_o,
    packed_o, rate_u_o,
    total, sums, act_sums, hidden_o,
):
    step = pl.program_id(0)
    me = where[1]
    wide = total.shape[1]

    @pl.when(step == 0)
    def _():
        tokens = x[...].astype(F32)
        attn = dot(ctx_a[...], wo_a[...]) + dot(ctx_b[...], wo_b[...]) + row(bias_out)
        hat, rate = normed(tokens + attn)
        hidden = hat * row(gain_one) + row(shift_one)
        hat_one_o[...] = hat
        rate_one_o[...] = jnp.broadcast_to(rate, rate_one_o.shape)
        hidden_low = hidden.astype(BF16)
        hidden_o[...] = hidden_low
        hidden_t_o[...] = jnp.transpose(hidden_low)
        total[...] = hidden + row(bias_down)
        sums[...] = jnp.zeros(sums.shape, F32)
        sums[0:1, :] = jnp.sum(hidden, 0, keepdims=True)
        half = ctx_a.shape[1]
        sums[1:2, :half] = jnp.sum(ctx_a[...].astype(F32), 0, keepdims=True)
        sums[1:2, half:] = jnp.sum(ctx_b[...].astype(F32), 0, keepdims=True)
        sums[2:3, :] = jnp.sum(tokens, 0, keepdims=True)

    hidden = hidden_o[...]
    place = pl.ds(pl.multiple_of(step * TILE, TILE), TILE)
    for side, (wi, bi, wd, act_o, slope_o) in enumerate((
        (wi_a, bi_a, wd_a, act_a_o, slope_a_o),
        (wi_b, bi_b, wd_b, act_b_o, slope_b_o),
    )):
        inner = dot(hidden, wi[...]) + row(bi)
        below = 0.5 + 0.5 * lax.erf(inner * (0.5**0.5))
        bell = jnp.exp(inner * inner * -0.5) * 0.3989422804014327
        act = inner * below
        act_sums[side : side + 1, place] = jnp.sum(act, 0, keepdims=True)
        act = act.astype(BF16)
        act_o[...] = act
        slope_o[...] = (below + inner * bell).astype(BF16)
        total[...] += dot(act, wd[...])

    @pl.when(step == pl.num_programs(0) - 1)
    def _():
        hat, rate = normed(total[...])
        hat_two_o[...] = hat
        rate_two_o[...] = jnp.broadcast_to(rate, rate_two_o.shape)
        output = hat * row(gain_two) + row(shift_two)
        raw = dot(pooling(bucket, lengths, me), output, precision=HIGH)
        rate_u = lax.rsqrt(jnp.sum(raw * raw, 1, keepdims=True) + 1e-06)
        rate_u_o[...] = jnp.broadcast_to(rate_u, rate_u_o.shape)
        packed_o[...] = raw * rate_u

        @pl.when(me == 1)
        def _():
            lane = lax.broadcasted_iota(jnp.int32, (1, wide), 1)
            extra = jnp.zeros((1, wide), jnp.int32)
            for s in range(SLOTS):
                extra = jnp.where(lane == s, positive[s], extra)
            for s in range(2):
                extra = jnp.where(lane == SLOTS + s, bucket[s], extra)
            packed_o[4:5, :] = extra.astype(F32)
            packed_o[5:6, :] = act_sums[0:1, :wide]
            packed_o[6:7, :] = act_sums[0:1, wide:]
            packed_o[7:8, :] = act_sums[1:2, :wide]
            packed_o[8:9, :] = act_sums[1:2, wide:]
            packed_o[9:12, :] = sums[0:3, :]


TILE = 256


def feed(scalars, x, ctx, wo, bias_out, gain_one, shift_one, wi, bi, wd, bias_down, gain_two, shift_two):
    rows, wide = BLOCK, x.shape[1]
    units = wi[0].shape[1]
    full = shape(rows, wide)
    rate = shape(rows, PAIR)
    low = shape(rows, units, kind=BF16)
    hidden = shape(wide, rows, kind=BF16)
    operands = (
        x, ctx[0], ctx[1], wo[0], wo[1], bias_out, gain_one, shift_one,
        wi[0], wi[1], bi[0], bi[1], wd[0], wd[1], bias_down, gain_two, shift_two,
    )
    specs = [block_rows(x)] + [whole(a) for a in operands[1:]]
    for place in (8, 9):
        specs[place] = columns(operands[place])
    for place in (10, 11):
        specs[place] = pl.BlockSpec((TILE,), lambda j, *_: (j,))
    for place in (12, 13):
        specs[place] = down_rows(operands[place])
    outs = (
        full, rate, hidden, low, low, low, low, full, rate, shape(SLOTS, wide), shape(SLOTS, PAIR),
    )
    out_specs = [whole(a) for a in outs]
    for place in (3, 4, 5, 6):
        out_specs[place] = columns(outs[place])
    scratch = [
        pltpu.VMEM((rows, wide), F32), pltpu.VMEM((8, wide), F32), pltpu.VMEM((8, units), F32),
        pltpu.VMEM((rows, wide), BF16),
    ]
    return call(
        feed_kernel, scalars, operands, specs, outs, out_specs, units // TILE, scratch,
        flops=2 * rows * wide * (wide + 4 * units),
    )


def turn(operands, where):
    def turn_kernel(where, *refs):
        for source, target in zip(refs, refs[len(operands) :]):
            target[...] = jnp.transpose(source[...])

    width = operands[0].shape[1]
    tile = min(TILE, width // 3)
    in_specs = [
        pl.BlockSpec((BLOCK, tile), lambda j, where, k=a.shape[0] // BLOCK - 1: (k * where[1], j))
        for a in operands
    ]
    outs = [shape(a.shape[1], BLOCK, kind=BF16) for a in operands]
    out_specs = [pl.BlockSpec((tile, BLOCK), lambda j, *_: (j, 0)) for _ in operands]
    return call(turn_kernel, (where,), operands, in_specs, outs, out_specs, width // tile)


def contrast_kernel(offsets, count, where, bucket, lengths, *refs):
    pieces = len(offsets)
    own, other = refs[:pieces], refs[pieces : 2 * pieces]
    packed, rate_u, hat, rate, gain = refs[2 * pieces : 2 * pieces + 5]
    loss_o, query_o, passage_o, grad_o, low_o, sums_o, common_o, columns_o = refs[2 * pieces + 5 : 2 * pieces + 13]
    asks, table, notes, place_col, live_col, dlogits, common, grad_unit = refs[2 * pieces + 13 :]
    spot, me = where[0], where[1]
    wide = hat.shape[1]
    rows16 = lax.broadcasted_iota(jnp.int32, (8, 1), 0)
    common[...] = jnp.zeros(common.shape, F32)
    notes[...] = jnp.zeros(notes.shape, F32)

    def spread(query_pieces, passage_pieces):
        for piece, places in zip(query_pieces, offsets):
            for i, offset in enumerate(places):
                source = spot ^ offset
                asks[pl.ds(pl.multiple_of(source * SLOTS, SLOTS), SLOTS), :] = piece[i]
        for piece, places in zip(passage_pieces, offsets):
            for i, offset in enumerate(places):
                source = spot ^ offset
                top = piece[i, 0:8, :]
                table[pl.ds(pl.multiple_of(source * 8, 8), 8), :] = jnp.where(rows16 < 4, top, 0.0)
                notes[pl.ds(source, 1), :] = top[4:5, :PAIR]
                common[0:8, :] += top
                common[8:16, :] += piece[i, 8:16, :]

    @pl.when(me == 0)
    def _():
        spread(own, other)

    @pl.when(me == 1)
    def _():
        spread(other, own)

    share = 1.0 / (count * BLOCK)
    first, second = common[5:7, :] * share, common[7:9, :] * share
    common_o[0:2, :] = jnp.where(me == 1, first, second)
    common_o[2:4, :] = jnp.where(me == 1, second, first)
    common_o[4:7, :] = common[9:12, :] * share
    common_o[7:8, :] = jnp.zeros((1, wide), F32)
    half = wide // 2

    @pl.when(me == 0)
    def _():
        common_o[5:6, :half] = common[10:11, half:] * share
        common_o[5:6, half:] = common[10:11, :half] * share

    padding = jnp.zeros((PAIR - 8, wide), F32)
    columns_o[...] = jnp.transpose(jnp.concatenate([common_o[...], padding], 0))

    turned = jnp.transpose(notes[...])
    slots = lax.broadcasted_iota(jnp.int32, (SLOTS, 1), 0).astype(F32)
    for d in range(count):
        at = slice(d * SLOTS, (d + 1) * SLOTS)
        place_col[at, :] = jnp.broadcast_to(turned[0:SLOTS, d : d + 1], (SLOTS, PAIR))
        held = jnp.where(turned[SLOTS : SLOTS + 1, d : d + 1] == 0.0, 16.0, 8.0)
        live_col[at, :] = jnp.broadcast_to((slots < held).astype(F32), (SLOTS, PAIR))
    wide_p = table.shape[0]
    cells = lax.broadcasted_iota(jnp.int32, (PAIR, wide_p), 1)
    sources = lax.broadcasted_iota(jnp.int32, (PAIR, wide_p), 0)
    held = jnp.where(notes[:, SLOTS + 1 : SLOTS + 2] == 2.0, 4, 1)
    live_p = ((cells >> 3) == sources) & ((cells & 7) < held)
    live_p = jnp.sum(live_p.astype(F32), 0, keepdims=True)

    count_q = jnp.sum(live_col[:, :1], 0, keepdims=True)
    rows_q = min(asks.shape[0], BLOCK // 2)

    def part(i, total):
        at = pl.ds(pl.multiple_of(i * rows_q, rows_q), rows_q)
        alive = live_col[at, :][:, :1]
        places = place_col[at, :][:, :1].astype(jnp.int32)
        places = (places >> 2) * 8 + (places & 3)
        logits = dot(asks[at, :], table[...], LANES, HIGH) / TEMP
        logits = jnp.where(live_p > 0, logits, MASKED)
        summit = jnp.max(logits, 1, keepdims=True)
        raised = jnp.exp(logits - summit)
        mass = jnp.sum(raised, 1, keepdims=True)
        normal = summit + jnp.log(mass)
        target = lax.broadcasted_iota(jnp.int32, logits.shape, 1) == places
        picked = jnp.sum(jnp.where(target, logits, 0.0), 1, keepdims=True)
        dlogits[at, :] = (jnp.exp(logits - normal) - target.astype(F32)) * (alive / count_q)
        return total + jnp.sum(alive * (normal - picked), 0, keepdims=True)

    total = jnp.zeros((1, 1), F32)
    if asks.shape[0] == rows_q:
        total = part(0, total)
    else:
        total = lax.fori_loop(0, asks.shape[0] // rows_q, part, total)
    loss_o[...] = total / count_q

    query_o[...] = asks[pl.ds(pl.multiple_of(spot * SLOTS, SLOTS), SLOTS), :]
    passage_o[...] = table[pl.ds(pl.multiple_of(spot * 8, 8), 8), :][0:4, :]

    @pl.when(me == 0)
    def _():
        mine = dlogits[pl.ds(pl.multiple_of(spot * SLOTS, SLOTS), SLOTS), :]
        grad_unit[...] = dot(mine, table[...], precision=HIGH) / TEMP

    @pl.when(me == 1)
    def _():
        cell = lax.broadcasted_iota(jnp.int32, (SLOTS, wide_p), 1)
        slot = lax.broadcasted_iota(jnp.int32, (SLOTS, wide_p), 0)
        mine = ((cell == slot + spot * 8) & (slot < 4)).astype(F32)
        weights = dot(mine, dlogits[...], LANES, HIGH)
        grad_unit[...] = dot(weights, asks[...], precision=HIGH) / TEMP

    slot = lax.broadcasted_iota(jnp.int32, (SLOTS, 1), 0)
    units = jnp.where((slot < 4) | (me == 0), packed[...], 0.0)
    grads = grad_unit[...]
    grad_embed = (grads - units * jnp.sum(units * grads, 1, keepdims=True)) * rate_u[:, :1]
    grad_out = dot(pooling(bucket, lengths, me), grad_embed, ROWS, HIGH)
    hats = hat[...]
    resid = normed_back(grad_out * row(gain), hats, rate[:, :1])
    grad_o[...] = resid
    low = resid.astype(BF16)
    low_o[...] = low
    sums_o[0:1, :] = jnp.sum(grad_out * hats, 0, keepdims=True)
    sums_o[1:2, :] = jnp.sum(grad_out, 0, keepdims=True)
    sums_o[2:3, :] = jnp.sum(low.astype(F32), 0, keepdims=True)
    sums_o[3:8, :] = jnp.zeros((5, wide), F32)


def contrast(scalars, own, other, offsets, packed, rate_u, hat, rate, gain):
    rows, wide = hat.shape
    count = sum(len(o) for o in offsets)
    operands = (*own, *other, packed, rate_u, hat, rate, gain)
    outs = (
        shape(1, 1), shape(SLOTS, wide), shape(4, wide), shape(rows, wide),
        shape(rows, wide, kind=BF16), shape(8, wide), shape(8, wide), shape(wide, PAIR),
    )
    queries, passages = count * SLOTS, count * 8
    scratch = [
        pltpu.VMEM(dims, F32)
        for dims in (
            (queries, wide), (passages, wide), (PAIR, PAIR), (queries, PAIR), (queries, PAIR),
            (queries, passages), (SLOTS, wide), (SLOTS, wide),
        )
    ]
    kernel = partial(contrast_kernel, offsets, count)
    kernel.__name__ = "contrast"
    specs = [whole(a) for a in operands]
    return call(
        kernel, scalars, operands, specs, outs, [whole(a) for a in outs],
        1, scratch, flops=2_000_000_000, mib=40 if count <= 16 else 60,
        far=range(2 * len(own), len(operands)),
    )


def feed_back_kernel(
    where, dffn, gres, wd_a, wd_b, wi_a, wi_b, slope_a, slope_b, hat, rate, gain, hidden_t, means,
    into_a_o, into_b_o, bias_a_o, bias_b_o, grad_o, low_o, sums_o,
    total,
):
    step = pl.program_id(0)

    @pl.when(step == 0)
    def _():
        total[...] = gres[...]

    mean = means[:, 4:5]
    for wd, wi, slope, into_o, bias_o in (
        (wd_a, wi_a, slope_a, into_a_o, bias_a_o),
        (wd_b, wi_b, slope_b, into_b_o, bias_b_o),
    ):
        inner = (dot(dffn[...], wd[...], LANES) * slope[...].astype(F32)).astype(BF16)
        sums = jnp.sum(inner.astype(F32), 0, keepdims=True)
        bias_o[...] = sums
        total[...] += dot(inner, wi[...], LANES)
        into_o[...] = (dot(hidden_t[...], inner) - mean * sums).astype(BF16)

    @pl.when(step == pl.num_programs(0) - 1)
    def _():
        grad = total[...]
        hats = hat[...]
        resid = normed_back(grad * row(gain), hats, rate[:, :1])
        grad_o[...] = resid
        low = resid.astype(BF16)
        low_o[...] = low
        sums_o[0:1, :] = jnp.sum(grad * hats, 0, keepdims=True)
        sums_o[1:2, :] = jnp.sum(grad, 0, keepdims=True)
        sums_o[2:3, :] = jnp.sum(low.astype(F32), 0, keepdims=True)
        sums_o[3:8, :] = jnp.zeros((5, sums_o.shape[1]), F32)


def feed_back(where, dffn, gres, wd, wi, slope, hat, rate, gain, hidden_t, means):
    rows, wide = dffn.shape
    units = wd[0].shape[0]
    operands = (
        dffn, gres, wd[0], wd[1], wi[0], wi[1], slope[0], slope[1], hat, rate, gain, hidden_t, means,
    )
    specs = [whole(a) for a in operands]
    for place in (2, 3):
        specs[place] = down_rows(operands[place])
    for place in (4, 5, 6, 7):
        specs[place] = columns(operands[place])
    into = shape(wide, units, kind=BF16)
    bias = shape(1, units)
    outs = (into, into, bias, bias, shape(rows, wide), shape(rows, wide, kind=BF16), shape(8, wide))
    out_specs = [whole(a) for a in outs]
    for place in (0, 1, 2, 3):
        out_specs[place] = columns(outs[place])
    return call(
        feed_back_kernel, (where,), operands, specs, outs, out_specs, units // TILE,
        [pltpu.VMEM((rows, wide), F32)], flops=12 * rows * wide * units,
    )


def down_grad(side, act_t, dffn, means, sums):
    units, rows = act_t.shape
    wide = dffn.shape[1]
    tile = wide // 2

    def down_grad_kernel(act_t, dffn, means, sums, out):
        lane = lax.broadcasted_iota(jnp.int32, (1, PAIR), 1)
        chosen = jnp.where(lane == 2 * side + (pl.program_id(0) >> 1), means[...], 0.0)
        mean = jnp.sum(chosen, 1, keepdims=True)
        out[...] = (dot(act_t[...], dffn[...]) - mean * sums[2:3, :]).astype(BF16)

    out = shape(units, wide, kind=BF16)
    return call(
        down_grad_kernel, (), (act_t, dffn, means, sums),
        [
            pl.BlockSpec((tile, rows), lambda j: (j, 0)),
            whole(dffn),
            pl.BlockSpec((tile, PAIR), lambda j: (j % 2, 0)),
            whole(sums),
        ],
        (out,),
        [pl.BlockSpec((tile, wide), lambda j: (j, 0))],
        units // tile, flops=2 * rows * units * wide, mib=32,
    )[0]


def swap(tensor):
    return lax.ppermute(tensor, "mp", [(0, 1), (1, 0)])


def flip(tensor, bits):
    count = lax.axis_size("dp")
    return lax.ppermute(tensor, "dp", [(i, i ^ bits) for i in range(count)])


def bit_count():
    return lax.axis_size("dp").bit_length() - 1


def seal(*values):
    return lax.optimization_barrier(values)


def plane(step):
    return lax.axis_index("mp") ^ step


def cross(tensor, step):
    count = lax.axis_size("dp")
    pairs = [
        (2 * d + c, 2 * (d ^ (1 << (step ^ c))) + c) for d in range(count) for c in range(2)
    ]
    return lax.ppermute(tensor, ("dp", "mp"), pairs)


def part_of(parts, bit, own):
    half = parts[0].shape[0] // 2
    side = (lax.axis_index("dp") >> bit) & 1
    start = (side if own else 1 - side) * half
    terms = [lax.dynamic_slice_in_dim(t, start, half, 0).astype(F32) for t in parts]
    return sum(terms[1:], terms[0]).astype(BF16)


def added(parts):
    return (parts[0].astype(F32) + parts[1].astype(F32)).astype(BF16)


def joined(pieces, bit):
    first, second = pieces
    side = (lax.axis_index("dp") >> bit) & 1
    return jnp.where(
        side == 0, jnp.concatenate([first, second], 0), jnp.concatenate([second, first], 0)
    )


def gather_small(tensor, beside):
    bits = list(range(bit_count()))
    groups = []
    while bits:
        groups.append(bits[-2:])
        bits = bits[:-2]
    tensor, offsets = tensor[None], [0]
    done = []
    for number, group in enumerate(groups):
        ways = range(1 << len(group))
        pieces = [tensor] + [flip(tensor, way << group[0]) for way in ways if way]
        places = [[(way << group[0]) | o for o in offsets] for way in ways]
        if number < len(beside) and beside[number]:
            pieces, work, tensor = seal(pieces, beside[number](tensor), tensor)
            done.append(work)
        if number == len(groups) - 1:
            return pieces, places, done
        tensor = jnp.concatenate(pieces, 0)
        offsets = [o for part in places for o in part]


def shards(
    tokens_in, proj_query, bias_query, proj_key, proj_value, bias_value, proj_out, bias_out,
    gain_attn, shift_attn, proj_in, bias_in, proj_down, bias_down, gain_ffn, shift_ffn,
    bucket, lengths, positive,
):
    spot, me = lax.axis_index("dp"), lax.axis_index("mp")
    wide = tokens_in.shape[1]
    width = proj_query.shape[1]
    units = proj_in.shape[1]
    where = jnp.stack([spot, me]).astype(jnp.int32)
    scalars = (where, bucket, lengths)
    x = tokens_in

    bq, bv, bi = [(b, swap(b)) for b in (bias_query, bias_value, bias_in)]
    wq, wk, wv = [(w, swap(w)) for w in (proj_query, proj_key, proj_value)]
    later = seal((proj_out, proj_in, proj_down), (bi[1], wq[1], wk[1], wv[1]))[0]
    wo, wi, wd = [(w, swap(w)) for w in later]

    *heads, x_t = attend(scalars, x, wq, bq, wk, wv, bv)
    ctx = [h[3] for h in heads]
    (hat_one, rate_one, hidden_t, act_a, act_b, slope_a, slope_b, hat_two, rate_two, packed, rate_u) = feed(
        scalars + (positive,), x, ctx, wo, bias_out, gain_attn, shift_attn, wi, bi, wd,
        bias_down, gain_ffn, shift_ffn,
    )

    def turn_beside(operands):
        def work(tensor):
            return turn(seal(operands, tensor)[0], where)

        return work

    own, offsets, (act_t,) = gather_small(packed, [None, turn_beside([act_a, act_b])])
    other = [swap(piece) for piece in own]

    loss, query_embed, passage_embed, gres_two, dffn, sums_two, common, means = contrast(
        scalars, own, other, offsets, packed, rate_u, hat_two, rate_two, gain_ffn
    )

    def outer(mean, sums):
        return mean[:, None] * sums[None, :]

    bits = bit_count()
    rest = list(range(2, bits))

    def vectors(sums_two, sums_one, sums, bias):
        rows = [sums[0:3].reshape(-1), bias[0], jnp.zeros(width, F32)]
        return jnp.concatenate(
            [sums_two[0:3], sums_one[0:3], jnp.concatenate(rows).reshape(-1, wide)], 0
        )

    sent = down_grad(1, act_t[1], dffn, means, sums_two)
    sent, dffn = seal(sent, dffn)
    down = [down_grad(0, act_t[0], dffn, means, sums_two), swap(sent)]
    down, common, sums_two = seal(down, common, sums_two)

    low, *high = rest

    def exchange(tensor):
        for bit in high:
            tensor = added([tensor, flip(tensor, 1 << bit)])
        return tensor

    gone = part_of(down, plane(0), False)
    gone, down, dffn = seal(gone, down, dffn)
    down = [part_of(down, plane(0), True), cross(gone, 0)]
    fed = feed_back(
        where, dffn, gres_two, wd, wi, (slope_a, slope_b), hat_one, rate_one, gain_attn, hidden_t,
        means,
    )
    down, fed = seal(down, fed)
    into_a, into_b, bias_a, bias_b, gres_one, dattn, sums_one = fed

    gone = part_of(down, plane(1), False)
    gone, down, dattn, into_b = seal(gone, down, dattn, into_b)
    down = [part_of(down, plane(1), True), cross(gone, 1)]
    into = [into_a, swap(into_b)]
    back_b = attend_back(1, scalars, *heads[1], dattn, wo[1], x_t, means, sums_one)
    down, into, back_b = seal(down, into, back_b)

    gone = part_of(into, plane(0), False), part_of(down, low, False)
    gone, into, down, dattn, back_b = seal(gone, into, down, dattn, back_b)
    into = [part_of(into, plane(0), True), cross(gone[0], 0)]
    down = [part_of(down, low, True), flip(gone[1], 1 << low)]
    attn_sent = swap(back_b[0])
    back_a = attend_back(0, scalars, *heads[0], dattn, wo[0], x_t, means, sums_one)
    into, down, attn_sent, back_a = seal(into, down, attn_sent, back_a)
    attn = [back_a[0], attn_sent]

    gone = part_of(into, plane(1), False)
    down = added(down)
    gone, into, down, attn, backs, gres_one = seal(
        gone, into, down, attn, (back_a[1:3], back_b[1:3]), gres_one
    )
    into = [part_of(into, plane(1), True), cross(gone, 1)]
    down = exchange(down)
    gone = part_of(attn, plane(0), False)
    gone_z = part_of(into, low, False)
    grad_in = gres_one
    for i, (dqk, dv) in enumerate(backs):
        grad_in = grad_in + dot(dqk[:, :width], wq[i], LANES) + dot(dqk[:, width:], wk[i], LANES)
        grad_in = grad_in + dot(dv, wv[i], LANES)
    grad_in = grad_in.astype(BF16)
    into, down, gone, gone_z, attn, grad_in = seal(into, down, gone, gone_z, attn, grad_in)

    attn = [part_of(attn, plane(0), True), cross(gone, 0)]
    into = [part_of(into, low, True), flip(gone_z, 1 << low)]
    down = [down, flip(down, 1 << low)]
    other_in = swap(grad_in)
    sums = sums_two, sums_one, (back_a[3], bias_a), (back_b[3], bias_b)
    sums, attn, into, down, other_in, grad_in = seal(sums, attn, into, down, other_in, grad_in)

    down = joined(down, low)
    gone = part_of(attn, plane(1), False)
    into = added(into)
    gone, attn, into, down, grad_in, other_in, sums = seal(
        gone, attn, into, down, grad_in, other_in, sums
    )
    attn = [part_of(attn, plane(1), True), cross(gone, 1)]
    down = [down, cross(down, 1)]
    into = exchange(into)
    small = [vectors(*sums[:2], *half) for half in sums[2:]]
    small = small[0] + swap(small[1])
    attn, down, into, small = seal(attn, down, into, small)

    down = joined(down, plane(1))
    gone = part_of(attn, low, False)
    gone, attn, down, into, small = seal(gone, attn, down, into, small)
    down = [down, cross(down, 0)]
    attn = [part_of(attn, low, True), flip(gone, 1 << low)]
    into = [into, flip(into, 1 << low)]
    small = small + flip(small, 1)
    attn, down, into, small = seal(attn, down, into, small)

    into, attn = joined(into, low), added(attn)
    attn, into, down, small = seal(attn, into, down, small)
    into = [into, cross(into, 1)]
    attn = exchange(attn)
    small = small + flip(small, 2)
    down = joined(down, plane(0))
    grad_input = jnp.where(
        me == 0,
        jnp.concatenate([grad_in, other_in], 0),
        jnp.concatenate([other_in, grad_in], 0),
    )
    attn, into, down, small, grad_input = seal(attn, into, down, small, grad_input)

    into = joined(into, plane(1))
    attn, into, down, small = seal(attn, into, down, small)
    into = [into, cross(into, 0)]
    attn = [attn, flip(attn, 1 << low)]
    small = small + flip(small, 1 << low)
    attn, into, small, down = seal(attn, into, small, down)

    attn = joined(attn, low)
    attn, into, small = seal(attn, into, small)
    attn = [attn, cross(attn, 1)]
    for bit in high:
        small = small + flip(small, 1 << bit)
    into = joined(into, plane(0))
    attn, into, small, down = seal(attn, into, small, down)

    attn = joined(attn, plane(1))
    attn, into, small, down, common = seal(attn, into, small, down, common)
    attn = [attn, cross(attn, 0)]
    share = lax.dynamic_slice_in_dim(small[0:6], me * width, width, 1)
    d_g2, d_s2, d_bd, d_g1, d_s1, d_bo = [share[i] for i in range(6)]
    own_half = small[6:].reshape(-1)
    d_bq, d_bk, d_bv = [own_half[i * width : (i + 1) * width] for i in range(3)]
    d_bi = own_half[3 * width : 3 * width + units]
    act_mean, hidden_mean, x_mean = common[0:2].reshape(units), common[4], common[6]
    ctx_mean = common[5, :width]
    grad_down = down.astype(F32) + outer(act_mean, small[2])
    grad_into = into.astype(F32) + outer(hidden_mean, d_bi)
    attn, grad_down, grad_into = seal(attn, grad_down, grad_into)
    attn = joined(attn, plane(0))
    grad_q, grad_k, grad_v, grad_o = [
        attn[:, i * width : (i + 1) * width].astype(F32) for i in range(4)
    ]
    grad_o = jnp.concatenate([grad_o[:width], grad_o[width:]], 1)
    return (
        loss[0, 0],
        query_embed,
        passage_embed,
        grad_input,
        grad_q + outer(x_mean, d_bq),
        d_bq,
        grad_k + outer(x_mean, d_bk),
        grad_v + outer(x_mean, d_bv),
        d_bv,
        grad_o + outer(ctx_mean, small[5]),
        d_bo,
        d_g1,
        d_s1,
        grad_into,
        d_bi,
        grad_down,
        d_bd,
        d_g2,
        d_s2,
    )


def solution(mesh):
    half, rows = P(None, "mp"), P("mp", None)
    return jax.shard_map(
        shards,
        mesh=mesh,
        in_specs=(
            P("dp", None), half, P("mp"), half, half, P("mp"), rows, P(), P(), P(),
            half, P("mp"), rows, P(), P(), P(), P("dp"), P("dp", None), P("dp"),
        ),
        out_specs=(
            P(), P("dp", None), P("dp", None), P("dp", None),
            half, P("mp"), half, half, P("mp"), rows, P("mp"), P("mp"), P("mp"),
            half, P("mp"), rows, P("mp"), P("mp"), P("mp"),
        ),
        check_vma=False,
    )
```

```python
from functools import partial

import jax
import jax.numpy as jnp
from jax import lax
from jax.experimental import pallas as pl
from jax.experimental.pallas import tpu as pltpu
from jax.sharding import PartitionSpec as P

HEAD_DIM = 64
BLOCK = 512
PAIR = 2 * HEAD_DIM
CHUNK = 128
SLOTS = 16
EPS = 1e-05
TEMP = 0.01
MASKED = -10000.0
HIGH = lax.Precision.HIGHEST
F32 = jnp.float32
BF16 = jnp.bfloat16
VMEM = pl.BlockSpec(memory_space=pltpu.VMEM)
SMEM = pl.BlockSpec(memory_space=pltpu.SMEM)


def dot(a, b, dims=((1,), (0,)), precision=None):
    return lax.dot_general(a, b, (dims, ((), ())), precision=precision, preferred_element_type=F32)


ROWS = ((0,), (0,))
LANES = ((1,), (1,))


def params(mib):
    return pltpu.CompilerParams(vmem_limit_bytes=mib * 1024 * 1024)


def row(ref):
    return ref[...].reshape(1, ref.shape[0])


def shape(*dims, kind=F32):
    return jax.ShapeDtypeStruct(dims, kind)


def lane_masks(kind):
    first = (lax.broadcasted_iota(jnp.int32, (1, PAIR), 1) < HEAD_DIM).astype(F32)
    return first.astype(kind), (1.0 - first).astype(kind)


def layout(bucket, lengths, me, axis):
    code = bucket[me]
    dims = (BLOCK, 1) if axis == 0 else (1, BLOCK)
    places = lax.broadcasted_iota(jnp.int32, dims, axis)
    shift = jnp.full(dims, jnp.where(code == 3, 9, 5 + code), jnp.int32)
    slot = lax.shift_right_logical(places, shift)
    offset = places - lax.shift_left(slot, shift)
    length = jnp.zeros(dims, jnp.int32)
    for s in range(SLOTS):
        length = jnp.where(slot == s, lengths[me, s], length)
    return slot, jnp.where(offset < length, slot, -1)


def pooling(bucket, lengths, me):
    _, kid = layout(bucket, lengths, me, 1)
    slots = lax.broadcasted_iota(jnp.int32, (SLOTS, BLOCK), 0)
    rows = lax.broadcasted_iota(jnp.int32, (SLOTS, 1), 0)
    length = jnp.zeros((SLOTS, 1), jnp.int32)
    for s in range(SLOTS):
        length = jnp.where(rows == s, lengths[me, s], length)
    member = (slots == kid).astype(F32)
    return member / jnp.maximum(length, 1).astype(F32)


def attend_kernel(
    where, bucket, lengths,
    x, wq_a, wq_b, bq_a, bq_b, wk_a, wk_b, wv_a, wv_b, bv_a, bv_b,
    q_a, q_b, k_a, k_b, v_a, v_b, ctx_a, ctx_b, lse_a, lse_b, x_t,
):
    width = wq_a.shape[1]
    me = where[1]
    tokens = x[...]
    x_t[...] = jnp.transpose(tokens)
    first, second = lane_masks(BF16)
    low = lax.broadcasted_iota(jnp.int32, (CHUNK, PAIR), 1) < HEAD_DIM
    lane = lax.broadcasted_iota(jnp.int32, (CHUNK, PAIR), 1)
    slot_col, _ = layout(bucket, lengths, me, 0)
    _, kid_row = layout(bucket, lengths, me, 1)
    ones = jnp.ones((BLOCK, PAIR), BF16)
    for wq, bq, wk, wv, bv, q_o, k_o, v_o, ctx_o, lse_o in (
        (wq_a, bq_a, wk_a, wv_a, bv_a, q_a, k_a, v_a, ctx_a, lse_a),
        (wq_b, bq_b, wk_b, wv_b, bv_b, q_b, k_b, v_b, ctx_b, lse_b),
    ):
        q_o[...] = (dot(tokens, wq[...]) + row(bq)).astype(BF16)
        k_o[...] = dot(tokens, wk[...]).astype(BF16)
        v_o[...] = (dot(tokens, wv[...]) + row(bv)).astype(BF16)
        for r in range(BLOCK // CHUNK):
            rows = slice(r * CHUNK, (r + 1) * CHUNK)
            mask = slot_col[rows, :] == kid_row
            mask = jnp.concatenate([mask, mask], 0)
            levels = jnp.zeros((CHUNK, PAIR), F32)
            for pair in range(width // PAIR):
                cols = slice(pair * PAIR, (pair + 1) * PAIR)
                query = q_o[rows, cols] * jnp.asarray(HEAD_DIM**-0.5, BF16)
                both = jnp.concatenate([query * first, query * second], 0)
                scores = jnp.where(mask, dot(both, k_o[:, cols], LANES), MASKED)
                summit = jnp.max(scores, 1, keepdims=True)
                raised = jnp.exp(scores - summit).astype(BF16)
                out = dot(raised, jnp.concatenate([v_o[:, cols], ones], 1))
                mass = out[:, PAIR:]
                out = out[:, :PAIR] / mass
                ctx_o[rows, cols] = jnp.where(low, out[:CHUNK], out[CHUNK:]).astype(BF16)
                logs = jnp.log(mass) + summit
                levels = jnp.where(lane == 2 * pair, logs[:CHUNK], levels)
                levels = jnp.where(lane == 2 * pair + 1, logs[CHUNK:], levels)
            lse_o[rows, :] = levels


def whole(a):
    return pl.BlockSpec(a.shape, lambda j, *_: (0,) * len(a.shape))


def block_rows(a):
    return pl.BlockSpec((BLOCK, a.shape[1]), lambda j, where, *_: (where[1], 0))


def turn_of(side, steps):
    if side is None:
        return lambda j: j
    if side == 0:
        return lambda j: jnp.minimum(j, steps - 1)
    return lambda j: jnp.maximum(j - steps, 0)


def columns(a, tile, side=None):
    at = turn_of(side, a.shape[1] // tile)
    return pl.BlockSpec((a.shape[0], tile), lambda j, *_: (0, at(j)))


def down_rows(a, tile, side=None):
    at = turn_of(side, a.shape[0] // tile)
    return pl.BlockSpec((tile, a.shape[1]), lambda j, *_: (at(j), 0))


def call(
    kernel, scalars, operands, in_specs, outs, out_specs, steps=1, scratch=(), flops=0, mib=60, far=()
):
    operands = [
        pltpu.with_memory_space_constraint(a, pltpu.HBM) if i in far else a
        for i, a in enumerate(operands)
    ]
    moved = sum(a.size * a.dtype.itemsize for a in list(operands) + list(outs))
    return pl.pallas_call(
        kernel,
        grid_spec=pltpu.PrefetchScalarGridSpec(
            num_scalar_prefetch=len(scalars),
            grid=(steps,),
            in_specs=in_specs,
            out_specs=tuple(out_specs),
            scratch_shapes=list(scratch),
        ),
        out_shape=tuple(outs),
        compiler_params=params(mib),
        cost_estimate=pl.CostEstimate(flops=flops, bytes_accessed=moved, transcendentals=0),
        name=kernel.__name__,
    )(*scalars, *operands)


def attend(scalars, x, wq, bq, wk, wv, bv):
    wide, width = wq[0].shape
    low, level = shape(BLOCK, width, kind=BF16), shape(BLOCK, PAIR)
    outs = (low,) * 8 + (level,) * 2 + (shape(wide, BLOCK, kind=BF16),)
    operands = (x, *wq, *bq, *wk, *wv, *bv)
    flops = 4 * BLOCK * width * (3 * wide + 4 * BLOCK)
    *halves, x_t = call(
        attend_kernel, scalars, operands, [block_rows(x)] + [whole(a) for a in operands[1:]],
        outs, [whole(a) for a in outs], flops=flops,
    )
    return halves[0::2], halves[1::2], x_t


def attend_back_kernel(
    side, where, bucket, lengths,
    q, k, v, ctx, lse, dattn, wo, x_t, means, vectors,
    part_o, dqk_o, dv_o, vectors_o,
    dscore_s, sums_o,
):
    width = q.shape[1]
    wide = dattn.shape[1]
    me = where[1]
    first, second = lane_masks(BF16)
    scale = jnp.asarray(HEAD_DIM**-0.5, BF16)
    dctx = dot(dattn[...], wo[...], LANES).astype(BF16)
    context = ctx[...]
    head_of = lax.broadcasted_iota(jnp.int32, (width, PAIR), 0) >> 6
    select = (head_of == lax.broadcasted_iota(jnp.int32, (width, PAIR), 1)).astype(F32)
    inner_sums = dot(select, dctx.astype(F32) * context.astype(F32), ((0,), (1,)), HIGH)
    levels = jnp.transpose(lse[...])
    slots, _ = layout(bucket, lengths, me, 1)
    _, kid_col = layout(bucket, lengths, me, 0)
    sums_o[...] = jnp.zeros(sums_o.shape, F32)
    low = lax.broadcasted_iota(jnp.int32, (TILE, PAIR), 1) < HEAD_DIM
    for pair in range(width // PAIR):
        cols = slice(pair * PAIR, (pair + 1) * PAIR)
        query = q[:, cols] * scale
        grad = dctx[:, cols]
        sum_k = jnp.zeros((1, PAIR), F32)
        sum_v = jnp.zeros((1, PAIR), F32)
        for c in range(BLOCK // TILE):
            rows = slice(c * TILE, (c + 1) * TILE)
            mask = kid_col[rows, :] == slots
            key_part, value_part = k[rows, cols], v[rows, cols]
            keys = jnp.concatenate([key_part * first, key_part * second], 0)
            values = jnp.concatenate([value_part * first, value_part * second], 0)
            scores, dprobs = dot(keys, query, LANES), dot(values, grad, LANES)
            probs, dscores = [], []
            for e in range(2):
                head, at = 2 * pair + e, slice(e * TILE, (e + 1) * TILE)
                prob = jnp.exp(jnp.where(mask, scores[at], MASKED) - levels[head : head + 1, :])
                dscore = (prob * (dprobs[at] - inner_sums[head : head + 1, :])).astype(BF16)
                dscore_s[e, rows, :] = dscore
                probs.append(prob.astype(BF16))
                dscores.append(dscore)
            dk = dot(jnp.concatenate(dscores, 0), query)
            dv = dot(jnp.concatenate(probs, 0), grad)
            dk = jnp.where(low, dk[:TILE], dk[TILE:]).astype(BF16)
            dv = jnp.where(low, dv[:TILE], dv[TILE:]).astype(BF16)
            dqk_o[rows, width + pair * PAIR : width + (pair + 1) * PAIR] = dk
            dv_o[rows, cols] = dv
            sum_k = sum_k + jnp.sum(dk.astype(F32), 0, keepdims=True)
            sum_v = sum_v + jnp.sum(dv.astype(F32), 0, keepdims=True)
        keys = jnp.transpose(k[:, cols])
        dq = [dot(keys[:HEAD_DIM], dscore_s[0]), dot(keys[HEAD_DIM:], dscore_s[1])]
        dq = (jnp.transpose(jnp.concatenate(dq, 0)) * HEAD_DIM**-0.5).astype(BF16)
        dqk_o[:, cols] = dq
        sums_o[0:1, cols] = jnp.sum(dq.astype(F32), 0, keepdims=True)
        sums_o[1:2, cols] = sum_k
        sums_o[2:3, cols] = sum_v
    x_mean = means[:, 6:7]
    for i, (source, at) in enumerate(((dqk_o, 0), (dqk_o, width), (dv_o, 0))):
        grads = dot(x_t[...], source[:, at : at + width]) - x_mean * sums_o[i : i + 1, :]
        part_o[:, i * width : (i + 1) * width] = grads.astype(BF16)
    turned = jnp.transpose(context)
    ctx_mean = means[side * width : (side + 1) * width, 5:6]
    grads = dot(turned, dattn[...]) - ctx_mean * vectors[5:6, :]
    part_o[:width, 3 * width :] = grads[:, :width].astype(BF16)
    part_o[width:, 3 * width :] = grads[:, width:].astype(BF16)
    vectors_o[...] = vectors[...]
    vectors_o[6:7, :width] = sums_o[0:1, :]
    vectors_o[6:7, width:] = sums_o[1:2, :]
    vectors_o[7:8, :width] = sums_o[2:3, :]


def attend_back(side, scalars, q, k, v, ctx, lse, dattn, wo, x_t, means, vectors):
    rows, width = q.shape
    wide = dattn.shape[1]
    outs = (
        shape(wide, 4 * width, kind=BF16),
        shape(rows, 2 * width, kind=BF16),
        shape(rows, width, kind=BF16),
        shape(SLOTS, wide),
    )
    operands = (q, k, v, ctx, lse, dattn, wo, x_t, means, vectors)
    kernel = partial(attend_back_kernel, side)
    kernel.__name__ = "attend_back"
    return call(
        kernel, scalars, operands, [whole(a) for a in operands],
        outs, [whole(a) for a in outs], 1,
        [pltpu.VMEM((2, rows, rows), BF16), pltpu.VMEM((8, width), F32)],
        flops=24 * rows * rows * width,
    )


def normed(resid):
    center = resid - jnp.mean(resid, -1, keepdims=True)
    rate = lax.rsqrt(jnp.mean(center * center, -1, keepdims=True) + EPS)
    return center * rate, rate


def normed_back(grad, hat, rate):
    return (
        grad - jnp.mean(grad, -1, keepdims=True) - hat * jnp.mean(grad * hat, -1, keepdims=True)
    ) * rate


def feed_kernel(
    where, bucket, lengths, positive,
    x, ctx_a, ctx_b, wo_a, wo_b, bias_out, gain_one, shift_one,
    wi_a, wi_b, bi_a, bi_b, wd_a, wd_b, bias_down, gain_two, shift_two,
    hat_one_o, rate_one_o, hidden_t_o, act_a_o, act_b_o, slope_a_o, slope_b_o, hat_two_o, rate_two_o,
    packed_o, rate_u_o,
    total, sums, act_sums, hidden_o,
):
    step = pl.program_id(0)
    me = where[1]
    wide = total.shape[1]

    @pl.when(step == 0)
    def _():
        tokens = x[...].astype(F32)
        attn = dot(ctx_a[...], wo_a[...]) + dot(ctx_b[...], wo_b[...]) + row(bias_out)
        hat, rate = normed(tokens + attn)
        hidden = hat * row(gain_one) + row(shift_one)
        hat_one_o[...] = hat
        rate_one_o[...] = jnp.broadcast_to(rate, rate_one_o.shape)
        hidden_low = hidden.astype(BF16)
        hidden_o[...] = hidden_low
        hidden_t_o[...] = jnp.transpose(hidden_low)
        total[...] = hidden + row(bias_down)
        sums[...] = jnp.zeros(sums.shape, F32)
        act_sums[...] = jnp.zeros(act_sums.shape, F32)
        sums[0:1, :] = jnp.sum(hidden, 0, keepdims=True)
        half = ctx_a.shape[1]
        sums[1:2, :half] = jnp.sum(ctx_a[...].astype(F32), 0, keepdims=True)
        sums[1:2, half:] = jnp.sum(ctx_b[...].astype(F32), 0, keepdims=True)
        sums[2:3, :] = jnp.sum(tokens, 0, keepdims=True)

    place = pl.ds(pl.multiple_of(step * WIDE, WIDE), WIDE)

    def chunk(c, carry):
        rows = pl.ds(pl.multiple_of(c * ROWS_AT_ONCE, ROWS_AT_ONCE), ROWS_AT_ONCE)
        hidden = hidden_o[rows, :]
        added = []
        for side, (wi, bi, wd, act_o, slope_o) in enumerate((
            (wi_a, bi_a, wd_a, act_a_o, slope_a_o),
            (wi_b, bi_b, wd_b, act_b_o, slope_b_o),
        )):
            inner = dot(hidden, wi[...]) + row(bi)
            below = 0.5 + 0.5 * lax.erf(inner * (0.5**0.5))
            bell = jnp.exp(inner * inner * -0.5) * 0.3989422804014327
            act = inner * below
            act_sums[side : side + 1, place] += jnp.sum(act, 0, keepdims=True)
            act = act.astype(BF16)
            act_o[rows, :] = act
            slope_o[rows, :] = (below + inner * bell).astype(BF16)
            added.append(dot(act, wd[...]))
        total[rows, :] += added[0] + added[1]
        return carry

    lax.fori_loop(0, BLOCK // ROWS_AT_ONCE, chunk, 0)

    @pl.when(step == pl.num_programs(0) - 1)
    def _():
        hat, rate = normed(total[...])
        hat_two_o[...] = hat
        rate_two_o[...] = jnp.broadcast_to(rate, rate_two_o.shape)
        output = hat * row(gain_two) + row(shift_two)
        raw = dot(pooling(bucket, lengths, me), output, precision=HIGH)
        rate_u = lax.rsqrt(jnp.sum(raw * raw, 1, keepdims=True) + 1e-06)
        rate_u_o[...] = jnp.broadcast_to(rate_u, rate_u_o.shape)
        packed_o[...] = raw * rate_u

        @pl.when(me == 1)
        def _():
            lane = lax.broadcasted_iota(jnp.int32, (1, wide), 1)
            extra = jnp.zeros((1, wide), jnp.int32)
            for s in range(SLOTS):
                extra = jnp.where(lane == s, positive[s], extra)
            for s in range(2):
                extra = jnp.where(lane == SLOTS + s, bucket[s], extra)
            packed_o[4:5, :] = extra.astype(F32)
            packed_o[5:6, :] = act_sums[0:1, :wide]
            packed_o[6:7, :] = act_sums[0:1, wide:]
            packed_o[7:8, :] = act_sums[1:2, :wide]
            packed_o[8:9, :] = act_sums[1:2, wide:]
            packed_o[9:12, :] = sums[0:3, :]


TILE = 256
WIDE = 512
ROWS_AT_ONCE = 256


def feed(scalars, x, ctx, wo, bias_out, gain_one, shift_one, wi, bi, wd, bias_down, gain_two, shift_two):
    rows, wide = BLOCK, x.shape[1]
    units = wi[0].shape[1]
    full = shape(rows, wide)
    rate = shape(rows, PAIR)
    low = shape(rows, units, kind=BF16)
    hidden = shape(wide, rows, kind=BF16)
    operands = (
        x, ctx[0], ctx[1], wo[0], wo[1], bias_out, gain_one, shift_one,
        wi[0], wi[1], bi[0], bi[1], wd[0], wd[1], bias_down, gain_two, shift_two,
    )
    specs = [block_rows(x)] + [whole(a) for a in operands[1:]]
    for side in range(2):
        specs[8 + side] = columns(wi[side], WIDE)
        specs[10 + side] = pl.BlockSpec((WIDE,), lambda j, *_: (j,))
        specs[12 + side] = down_rows(wd[side], WIDE)
    outs = (
        full, rate, hidden, low, low, low, low, full, rate, shape(SLOTS, wide), shape(SLOTS, PAIR),
    )
    out_specs = [whole(a) for a in outs]
    for place in (3, 4, 5, 6):
        out_specs[place] = columns(outs[place], WIDE)
    scratch = [
        pltpu.VMEM((rows, wide), F32), pltpu.VMEM((8, wide), F32), pltpu.VMEM((8, units), F32),
        pltpu.VMEM((rows, wide), BF16),
    ]
    return call(
        feed_kernel, scalars, operands, specs, outs, out_specs, units // WIDE, scratch,
        flops=2 * rows * wide * (wide + 4 * units),
    )


def turn(operands, where):
    def turn_kernel(where, *refs):
        for source, target in zip(refs, refs[len(operands) :]):
            target[...] = jnp.transpose(source[...])

    width = operands[0].shape[1]
    tile = min(TILE, width // 3)
    in_specs = [
        pl.BlockSpec((BLOCK, tile), lambda j, where, k=a.shape[0] // BLOCK - 1: (k * where[1], j))
        for a in operands
    ]
    outs = [shape(a.shape[1], BLOCK, kind=BF16) for a in operands]
    out_specs = [pl.BlockSpec((tile, BLOCK), lambda j, *_: (j, 0)) for _ in operands]
    return call(turn_kernel, (where,), operands, in_specs, outs, out_specs, width // tile, mib=16)


def contrast_kernel(offsets, count, where, bucket, lengths, *refs):
    pieces = len(offsets)
    own, other = refs[:pieces], refs[pieces : 2 * pieces]
    packed, rate_u, hat, rate, gain = refs[2 * pieces : 2 * pieces + 5]
    loss_o, query_o, passage_o, grad_o, low_o, sums_o, common_o, columns_o = refs[2 * pieces + 5 : 2 * pieces + 13]
    asks, table, notes, place_col, live_col, dlogits, common, grad_unit = refs[2 * pieces + 13 :]
    spot, me = where[0], where[1]
    wide = hat.shape[1]
    rows16 = lax.broadcasted_iota(jnp.int32, (8, 1), 0)
    common[...] = jnp.zeros(common.shape, F32)
    notes[...] = jnp.zeros(notes.shape, F32)

    def spread(query_pieces, passage_pieces):
        for piece, places in zip(query_pieces, offsets):
            for i, offset in enumerate(places):
                source = spot ^ offset
                asks[pl.ds(pl.multiple_of(source * SLOTS, SLOTS), SLOTS), :] = piece[i]
        for piece, places in zip(passage_pieces, offsets):
            for i, offset in enumerate(places):
                source = spot ^ offset
                top = piece[i, 0:8, :]
                table[pl.ds(pl.multiple_of(source * 8, 8), 8), :] = jnp.where(rows16 < 4, top, 0.0)
                notes[pl.ds(source, 1), :] = top[4:5, :PAIR]
                common[0:8, :] += top
                common[8:16, :] += piece[i, 8:16, :]

    @pl.when(me == 0)
    def _():
        spread(own, other)

    @pl.when(me == 1)
    def _():
        spread(other, own)

    share = 1.0 / (count * BLOCK)
    first, second = common[5:7, :] * share, common[7:9, :] * share
    common_o[0:2, :] = jnp.where(me == 1, first, second)
    common_o[2:4, :] = jnp.where(me == 1, second, first)
    common_o[4:7, :] = common[9:12, :] * share
    common_o[7:8, :] = jnp.zeros((1, wide), F32)
    half = wide // 2

    @pl.when(me == 0)
    def _():
        common_o[5:6, :half] = common[10:11, half:] * share
        common_o[5:6, half:] = common[10:11, :half] * share

    padding = jnp.zeros((PAIR - 8, wide), F32)
    columns_o[...] = jnp.transpose(jnp.concatenate([common_o[...], padding], 0))

    turned = jnp.transpose(notes[...])
    slots = lax.broadcasted_iota(jnp.int32, (SLOTS, 1), 0).astype(F32)
    for d in range(count):
        at = slice(d * SLOTS, (d + 1) * SLOTS)
        place_col[at, :] = jnp.broadcast_to(turned[0:SLOTS, d : d + 1], (SLOTS, PAIR))
        held = jnp.where(turned[SLOTS : SLOTS + 1, d : d + 1] == 0.0, 16.0, 8.0)
        live_col[at, :] = jnp.broadcast_to((slots < held).astype(F32), (SLOTS, PAIR))
    wide_p = table.shape[0]
    cells = lax.broadcasted_iota(jnp.int32, (PAIR, wide_p), 1)
    sources = lax.broadcasted_iota(jnp.int32, (PAIR, wide_p), 0)
    held = jnp.where(notes[:, SLOTS + 1 : SLOTS + 2] == 2.0, 4, 1)
    live_p = ((cells >> 3) == sources) & ((cells & 7) < held)
    live_p = jnp.sum(live_p.astype(F32), 0, keepdims=True)

    count_q = jnp.sum(live_col[:, :1], 0, keepdims=True)
    rows_q = min(asks.shape[0], BLOCK // 2)

    def part(i, total):
        at = pl.ds(pl.multiple_of(i * rows_q, rows_q), rows_q)
        alive = live_col[at, :][:, :1]
        places = place_col[at, :][:, :1].astype(jnp.int32)
        places = (places >> 2) * 8 + (places & 3)
        logits = dot(asks[at, :], table[...], LANES, HIGH) / TEMP
        logits = jnp.where(live_p > 0, logits, MASKED)
        summit = jnp.max(logits, 1, keepdims=True)
        raised = jnp.exp(logits - summit)
        mass = jnp.sum(raised, 1, keepdims=True)
        normal = summit + jnp.log(mass)
        target = lax.broadcasted_iota(jnp.int32, logits.shape, 1) == places
        picked = jnp.sum(jnp.where(target, logits, 0.0), 1, keepdims=True)
        dlogits[at, :] = (jnp.exp(logits - normal) - target.astype(F32)) * (alive / count_q)
        return total + jnp.sum(alive * (normal - picked), 0, keepdims=True)

    total = jnp.zeros((1, 1), F32)
    if asks.shape[0] == rows_q:
        total = part(0, total)
    else:
        total = lax.fori_loop(0, asks.shape[0] // rows_q, part, total)
    loss_o[...] = total / count_q

    query_o[...] = asks[pl.ds(pl.multiple_of(spot * SLOTS, SLOTS), SLOTS), :]
    passage_o[...] = table[pl.ds(pl.multiple_of(spot * 8, 8), 8), :][0:4, :]

    @pl.when(me == 0)
    def _():
        mine = dlogits[pl.ds(pl.multiple_of(spot * SLOTS, SLOTS), SLOTS), :]
        grad_unit[...] = dot(mine, table[...], precision=HIGH) / TEMP

    @pl.when(me == 1)
    def _():
        cell = lax.broadcasted_iota(jnp.int32, (SLOTS, wide_p), 1)
        slot = lax.broadcasted_iota(jnp.int32, (SLOTS, wide_p), 0)
        mine = ((cell == slot + spot * 8) & (slot < 4)).astype(F32)
        weights = dot(mine, dlogits[...], LANES, HIGH)
        grad_unit[...] = dot(weights, asks[...], precision=HIGH) / TEMP

    slot = lax.broadcasted_iota(jnp.int32, (SLOTS, 1), 0)
    units = jnp.where((slot < 4) | (me == 0), packed[...], 0.0)
    grads = grad_unit[...]
    grad_embed = (grads - units * jnp.sum(units * grads, 1, keepdims=True)) * rate_u[:, :1]
    grad_out = dot(pooling(bucket, lengths, me), grad_embed, ROWS, HIGH)
    hats = hat[...]
    resid = normed_back(grad_out * row(gain), hats, rate[:, :1])
    grad_o[...] = resid
    low = resid.astype(BF16)
    low_o[...] = low
    sums_o[0:1, :] = jnp.sum(grad_out * hats, 0, keepdims=True)
    sums_o[1:2, :] = jnp.sum(grad_out, 0, keepdims=True)
    sums_o[2:3, :] = jnp.sum(low.astype(F32), 0, keepdims=True)
    sums_o[3:8, :] = jnp.zeros((5, wide), F32)


def contrast(scalars, own, other, offsets, packed, rate_u, hat, rate, gain):
    rows, wide = hat.shape
    count = sum(len(o) for o in offsets)
    operands = (*own, *other, packed, rate_u, hat, rate, gain)
    outs = (
        shape(1, 1), shape(SLOTS, wide), shape(4, wide), shape(rows, wide),
        shape(rows, wide, kind=BF16), shape(8, wide), shape(8, wide), shape(wide, PAIR),
    )
    queries, passages = count * SLOTS, count * 8
    scratch = [
        pltpu.VMEM(dims, F32)
        for dims in (
            (queries, wide), (passages, wide), (PAIR, PAIR), (queries, PAIR), (queries, PAIR),
            (queries, passages), (SLOTS, wide), (SLOTS, wide),
        )
    ]
    kernel = partial(contrast_kernel, offsets, count)
    kernel.__name__ = "contrast"
    specs = [whole(a) for a in operands]
    return call(
        kernel, scalars, operands, specs, outs, [whole(a) for a in outs],
        1, scratch, flops=2_000_000_000, mib=40 if count <= 16 else 60,
        far=range(2 * len(own), len(operands)),
    )


def feed_back_kernel(
    where, dffn, gres, wd_a, wd_b, wi_a, wi_b, slope_a, slope_b, hat, rate, gain, hidden_t, means, sums_two,
    into_a_o, into_b_o, grad_o, low_o, vectors_a_o, vectors_b_o,
    total, bias,
):
    step = pl.program_id(0)
    steps = pl.num_programs(0) // 2
    wide = total.shape[1]

    @pl.when(step == 0)
    def _():
        total[...] = gres[...]

    def units(side, step, wd, wi, slope, into_o):
        inner = (dot(dffn[...], wd[...], LANES) * slope[...].astype(F32)).astype(BF16)
        sums = jnp.sum(inner.astype(F32), 0, keepdims=True)
        bias[side : side + 1, pl.ds(pl.multiple_of(step * WIDE, WIDE), WIDE)] = sums
        total[...] += dot(inner, wi[...], LANES)
        into_o[...] = (dot(hidden_t[...], inner) - means[:, 4:5] * sums).astype(BF16)

    @pl.when(step < steps)
    def _():
        units(0, step, wd_a, wi_a, slope_a, into_a_o)

    @pl.when(step >= steps)
    def _():
        units(1, step - steps, wd_b, wi_b, slope_b, into_b_o)

    @pl.when(step == pl.num_programs(0) - 1)
    def _():
        grad = total[...]
        hats = hat[...]
        resid = normed_back(grad * row(gain), hats, rate[:, :1])
        grad_o[...] = resid
        low = resid.astype(BF16)
        low_o[...] = low
        for side, vectors in enumerate((vectors_a_o, vectors_b_o)):
            vectors[...] = jnp.zeros(vectors.shape, F32)
            vectors[0:3, :] = sums_two[0:3, :]
            vectors[3:4, :] = jnp.sum(grad * hats, 0, keepdims=True)
            vectors[4:5, :] = jnp.sum(grad, 0, keepdims=True)
            vectors[5:6, :] = jnp.sum(low.astype(F32), 0, keepdims=True)
            vectors[8:9, :] = bias[side : side + 1, :wide]
            vectors[9:10, :] = bias[side : side + 1, wide:]


def feed_back(where, dffn, gres, wd, wi, slope, hat, rate, gain, hidden_t, means, sums_two):
    rows, wide = dffn.shape
    units = wd[0].shape[0]
    operands = (
        dffn, gres, wd[0], wd[1], wi[0], wi[1], slope[0], slope[1], hat, rate, gain, hidden_t, means, sums_two,
    )
    specs = [whole(a) for a in operands]
    for side in range(2):
        specs[2 + side] = down_rows(wd[side], WIDE, side)
        specs[4 + side] = columns(wi[side], WIDE, side)
        specs[6 + side] = columns(slope[side], WIDE, side)
    into = shape(wide, units, kind=BF16)
    vectors = shape(SLOTS, wide)
    outs = (into, into, shape(rows, wide), shape(rows, wide, kind=BF16), vectors, vectors)
    out_specs = [whole(a) for a in outs]
    for side in range(2):
        out_specs[side] = columns(into, WIDE, side)
    return call(
        feed_back_kernel, (where,), operands, specs, outs, out_specs, 2 * units // WIDE,
        [pltpu.VMEM((rows, wide), F32), pltpu.VMEM((8, units), F32)],
        flops=12 * rows * wide * units, mib=44,
    )


def down_grad(where, act_t, dffn, means):
    units, rows = act_t[0].shape
    wide = dffn[0].shape[1]
    tile = wide // 2

    def half(j, where):
        side = (where[0] >> where[1]) & 1
        return jnp.where(j < 2, 1 - side, side)

    def down_grad_kernel(where, act_a, act_b, dffn_a, dffn_b, means, gone, kept, sums):
        step = pl.program_id(0)

        @pl.when(step == 0)
        def _():
            both = dffn_a[...].astype(F32) + dffn_b[...].astype(F32)
            sums[...] = jnp.broadcast_to(jnp.sum(both, 0, keepdims=True), sums.shape)

        mean = jnp.where(half(step, where) == 0, means[:, 0:1], means[:, 1:2])
        grads = dot(act_a[...], dffn_a[...]) + dot(act_b[...], dffn_b[...])
        grads = (grads - mean * sums[0:1, :]).astype(BF16)

        @pl.when(step < 2)
        def _():
            gone[...] = grads

        @pl.when(step >= 2)
        def _():
            kept[...] = grads

    out = shape(units // 2, wide, kind=BF16)
    act_spec = pl.BlockSpec((tile, rows), lambda j, where: (2 * half(j, where) + j % 2, 0))
    return call(
        down_grad_kernel, (where,), (*act_t, *dffn, means),
        [act_spec, act_spec, whole(dffn[0]), whole(dffn[1]), pl.BlockSpec((tile, PAIR), lambda j, *_: (j % 2, 0))],
        (out, out),
        [
            pl.BlockSpec((tile, wide), lambda j, *_: (jnp.minimum(j, 1), 0)),
            pl.BlockSpec((tile, wide), lambda j, *_: (jnp.maximum(j - 2, 0), 0)),
        ],
        4, [pltpu.VMEM((8, wide), F32)], flops=4 * rows * units * wide, mib=24,
    )


def part(terms, bit, own=False):
    return "part", terms, bit, own


def add(terms):
    return "add", terms, None, None


def join(pieces, bit):
    return "join", pieces, bit, None


def mixed(where, *jobs):
    if any(job[1][0].shape[0] % 32 for job in jobs):
        return [plain(where, *job) for job in jobs]
    operands, specs, outs = [], [], []
    for kind, tensors, bit, own in jobs:
        rows, columns = tensors[0].shape
        block = (rows // 2, columns) if kind == "part" else (rows, columns)

        def place(j, where, bit=bit, own=own, kind=kind):
            if kind != "part":
                return 0, 0
            side = (where[0] >> bit(where)) & 1
            return (side if own else 1 - side), 0

        for t in tensors:
            operands.append(t)
            specs.append(pl.BlockSpec(block, place))
        outs.append(shape(2 * rows if kind == "join" else block[0], columns, kind=BF16))

    def mixed_kernel(where, *refs):
        sources, targets = refs[: len(operands)], refs[len(operands) :]
        for kind, tensors, bit, _ in jobs:
            mine, sources = sources[: len(tensors)], sources[len(tensors) :]
            target, targets = targets[0], targets[1:]
            if kind == "join":
                rows = mine[0].shape[0]
                side = (where[0] >> bit(where)) & 1
                target[pl.ds(pl.multiple_of(side * rows, 32), rows), :] = mine[0][...]
                target[pl.ds(pl.multiple_of((1 - side) * rows, 32), rows), :] = mine[1][...]
            else:
                total = mine[0][...].astype(F32)
                for other in mine[1:]:
                    total = total + other[...].astype(F32)
                target[...] = total.astype(BF16)

    return call(
        mixed_kernel, (where,), operands, specs, outs, [whole(a) for a in outs], mib=24
    )


def plain(where, kind, tensors, bit, own):
    if kind == "add":
        return added(tensors)
    side = (where[0] >> bit(where)) & 1
    if kind == "join":
        first, second = tensors
        return jnp.where(
            side == 0, jnp.concatenate([first, second], 0), jnp.concatenate([second, first], 0)
        )
    half = tensors[0].shape[0] // 2
    start = (side if own else 1 - side) * half
    return added([lax.dynamic_slice_in_dim(t, start, half, 0) for t in tensors])


def swap(tensor):
    return lax.ppermute(tensor, "mp", [(0, 1), (1, 0)])


def flip(tensor, bits):
    count = lax.axis_size("dp")
    return lax.ppermute(tensor, "dp", [(i, i ^ bits) for i in range(count)])


def bit_count():
    return lax.axis_size("dp").bit_length() - 1


def seal(*values):
    return lax.optimization_barrier(values)


def plane(step):
    return lambda where: where[1] ^ step


def over(bit):
    return lambda where: bit


def cross(tensor, step):
    count = lax.axis_size("dp")
    pairs = [
        (2 * d + c, 2 * (d ^ (1 << (step ^ c))) + c) for d in range(count) for c in range(2)
    ]
    return lax.ppermute(tensor, ("dp", "mp"), pairs)


def added(parts):
    return sum([t.astype(F32) for t in parts[1:]], parts[0].astype(F32)).astype(BF16)


def gather_small(tensor, beside):
    bits = list(range(bit_count()))
    groups = []
    while bits:
        groups.append(bits[-2:])
        bits = bits[:-2]
    tensor, offsets = tensor[None], [0]
    done = []
    for number, group in enumerate(groups):
        ways = range(1 << len(group))
        pieces = [tensor] + [flip(tensor, way << group[0]) for way in ways if way]
        places = [[(way << group[0]) | o for o in offsets] for way in ways]
        if number < len(beside) and beside[number]:
            pieces, work, tensor = seal(pieces, beside[number](tensor), tensor)
            done.append(work)
        if number == len(groups) - 1:
            return pieces, places, done
        tensor = jnp.concatenate(pieces, 0)
        offsets = [o for part in places for o in part]


def shards(
    tokens_in, proj_query, bias_query, proj_key, proj_value, bias_value, proj_out, bias_out,
    gain_attn, shift_attn, proj_in, bias_in, proj_down, bias_down, gain_ffn, shift_ffn,
    bucket, lengths, positive,
):
    spot, me = lax.axis_index("dp"), lax.axis_index("mp")
    wide = tokens_in.shape[1]
    width = proj_query.shape[1]
    units = proj_in.shape[1]
    where = jnp.stack([spot, me]).astype(jnp.int32)
    scalars = (where, bucket, lengths)
    x = tokens_in

    bq, bv, bi = [(b, swap(b)) for b in (bias_query, bias_value, bias_in)]
    wq, wk, wv = [(w, swap(w)) for w in (proj_query, proj_key, proj_value)]
    later = seal((proj_out, proj_in, proj_down), (bq[1], bv[1], bi[1], wq[1], wk[1], wv[1]))[0]
    wo, wi, wd = [(w, swap(w)) for w in later]

    *heads, x_t = attend(scalars, x, wq, bq, wk, wv, bv)
    ctx = [h[3] for h in heads]
    (hat_one, rate_one, hidden_t, act_a, act_b, slope_a, slope_b, hat_two, rate_two, packed, rate_u) = feed(
        scalars + (positive,), x, ctx, wo, bias_out, gain_attn, shift_attn, wi, bi, wd,
        bias_down, gain_ffn, shift_ffn,
    )

    def turn_beside(operands):
        def work(tensor):
            return turn(seal(operands, tensor)[0], where)

        return work

    own, offsets, (act_t,) = gather_small(packed, [None, turn_beside([act_a, act_b])])
    other = [swap(piece) for piece in own]
    act_t = act_t[0], swap(act_t[1])

    loss, query_embed, passage_embed, gres_two, dffn, sums_two, common, means = contrast(
        scalars, own, other, offsets, packed, rate_u, hat_two, rate_two, gain_ffn
    )

    def outer(mean, sums):
        return mean[:, None] * sums[None, :]

    bits = bit_count()
    rest = list(range(2, bits))

    low, *high = rest

    def kept(terms, bit):
        return plain(where, *part(terms, bit, True))

    def exchange(tensor, sent=()):
        for number, bit in enumerate(high):
            other = sent[number] if number < len(sent) else flip(tensor, 1 << bit)
            tensor = added([tensor, other])
        return tensor

    dffns = dffn, swap(dffn)
    gone, own = down_grad(where, act_t, dffns, means)
    gone, own, dffn, common, sums_two = seal(gone, own, dffn, common, sums_two)
    down = [own, cross(gone, 0)]
    fed = feed_back(
        where, dffn, gres_two, wd, wi, (slope_a, slope_b), hat_one, rate_one, gain_attn, hidden_t,
        means, sums_two,
    )
    down, fed = seal(down, fed)
    into_a, into_b, gres_one, dattn, vectors_a, vectors_b = fed

    (gone,) = mixed(where, part(down, plane(1)))
    gone, down, dattn, into_b = seal(gone, down, dattn, into_b)
    down = [kept(down, plane(1)), cross(gone, 1)]
    into = [into_a, swap(into_b)]
    back_b = attend_back(1, scalars, *heads[1], dattn, wo[1], x_t, means, vectors_b)
    down, into, back_b = seal(down, into, back_b)

    gone = mixed(where, part(into, plane(0)), part(down, over(low)))
    gone, into, down, dattn, back_b = seal(gone, into, down, dattn, back_b)
    into = [kept(into, plane(0)), cross(gone[0], 0)]
    down = [kept(down, over(low)), flip(gone[1], 1 << low)]
    attn_sent = swap(back_b[0])
    back_a = attend_back(0, scalars, *heads[0], dattn, wo[0], x_t, means, vectors_a)
    into, down, attn_sent, back_a = seal(into, down, attn_sent, back_a)
    attn = [back_a[0], attn_sent]

    gone, down = mixed(where, part(into, plane(1)), add(down))
    gone, into, down, attn = seal(gone, into, down, attn)
    into = [kept(into, plane(1)), cross(gone, 1)]
    sent = [flip(down, 1 << bit) for bit in high[:1]]
    into, attn = seal(into, attn)
    gone = mixed(where, part(attn, plane(0)), part(into, over(low)))
    gone, attn, down = seal(gone, attn, down)
    down = exchange(down, sent)
    into, down, gone, attn = seal(into, down, gone, attn)

    attn = [kept(attn, plane(0)), cross(gone[0], 0)]
    into = [kept(into, over(low)), flip(gone[1], 1 << low)]
    down = [down, flip(down, 1 << low)]
    small = back_a[3] + swap(back_b[3])
    small, attn, into, down = seal(small, attn, into, down)

    gone, down, into = mixed(where, part(attn, plane(1)), join(down, over(low)), add(into))
    gone, attn, into, down, small = seal(gone, attn, into, down, small)
    attn = [kept(attn, plane(1)), cross(gone, 1)]
    down = [down, cross(down, 1)]
    into = exchange(into)
    small = small + flip(small, 1)
    attn, down, into, small = seal(attn, down, into, small)

    down, gone = mixed(where, join(down, plane(1)), part(attn, over(low)))
    gone, attn, down, into, small = seal(gone, attn, down, into, small)
    down = [down, cross(down, 0)]
    attn = [kept(attn, over(low)), flip(gone, 1 << low)]
    into = [into, flip(into, 1 << low)]
    small = small + flip(small, 2)
    attn, down, into, small = seal(attn, down, into, small)

    into, attn = mixed(where, join(into, over(low)), add(attn))
    attn, into, down, small = seal(attn, into, down, small)
    into = [into, cross(into, 1)]
    sent = [flip(attn, 1 << bit) for bit in high[:1]]
    small = small + flip(small, 1 << low)
    into, small, down, gres_one, backs = seal(
        into, small, down, gres_one, (back_a[1:3], back_b[1:3])
    )
    grad_in = gres_one
    for i, (dqk, dv) in enumerate(backs):
        grad_in = grad_in + dot(dqk[:, :width], wq[i], LANES) + dot(dqk[:, width:], wk[i], LANES)
        grad_in = grad_in + dot(dv, wv[i], LANES)
    grad_in = grad_in.astype(BF16)
    down = plain(where, *join(down, plane(0)))
    attn, grad_in, down = seal(attn, grad_in, down)
    attn = exchange(attn, sent)
    attn, into, down, small, grad_in = seal(attn, into, down, small, grad_in)

    into = plain(where, *join(into, plane(1)))
    attn, into, small, grad_in = seal(attn, into, small, grad_in)
    into = [into, cross(into, 0)]
    attn = [attn, flip(attn, 1 << low)]
    for bit in high:
        small = small + flip(small, 1 << bit)
    other_in = swap(grad_in)
    grad_input = jnp.where(
        me == 0,
        jnp.concatenate([grad_in, other_in], 0),
        jnp.concatenate([other_in, grad_in], 0),
    )
    attn, into, small, down, grad_input, common = seal(attn, into, small, down, grad_input, common)

    attn = plain(where, *join(attn, over(low)))
    attn, into, small, common = seal(attn, into, small, common)
    attn = [attn, cross(attn, 1)]
    into = plain(where, *join(into, plane(0)))
    share = lax.dynamic_slice_in_dim(small[0:6], me * width, width, 1)
    d_g2, d_s2, d_bd, d_g1, d_s1, d_bo = [share[i] for i in range(6)]
    own_half = small[6:].reshape(-1)
    d_bq, d_bk, d_bv = [own_half[i * width : (i + 1) * width] for i in range(3)]
    d_bi = small[8:10].reshape(units)
    act_mean, hidden_mean, x_mean = common[0:2].reshape(units), common[4], common[6]
    ctx_mean = common[5, :width]
    factors = act_mean, small[2], hidden_mean, d_bi
    attn, into, down, factors = seal(attn, into, down, factors)

    (attn,) = mixed(where, join(attn, plane(1)))
    attn, into, down, factors = seal(attn, into, down, factors)
    attn = [attn, cross(attn, 0)]
    grad_down = down.astype(F32) + outer(*factors[0:2])
    grad_into = into.astype(F32) + outer(*factors[2:4])
    attn, grad_down, grad_into = seal(attn, grad_down, grad_into)
    attn = plain(where, *join(attn, plane(0)))
    grad_q, grad_k, grad_v, grad_o = [
        attn[:, i * width : (i + 1) * width].astype(F32) for i in range(4)
    ]
    grad_o = jnp.concatenate([grad_o[:width], grad_o[width:]], 1)
    return (
        loss[0, 0],
        query_embed,
        passage_embed,
        grad_input,
        grad_q + outer(x_mean, d_bq),
        d_bq,
        grad_k + outer(x_mean, d_bk),
        grad_v + outer(x_mean, d_bv),
        d_bv,
        grad_o + outer(ctx_mean, small[5]),
        d_bo,
        d_g1,
        d_s1,
        grad_into,
        d_bi,
        grad_down,
        d_bd,
        d_g2,
        d_s2,
    )


def solution(mesh):
    half, rows = P(None, "mp"), P("mp", None)
    return jax.shard_map(
        shards,
        mesh=mesh,
        in_specs=(
            P("dp", None), half, P("mp"), half, half, P("mp"), rows, P(), P(), P(),
            half, P("mp"), rows, P(), P(), P(), P("dp"), P("dp", None), P("dp"),
        ),
        out_specs=(
            P(), P("dp", None), P("dp", None), P("dp", None),
            half, P("mp"), half, half, P("mp"), rows, P("mp"), P("mp"), P("mp"),
            half, P("mp"), rows, P("mp"), P("mp"), P("mp"),
        ),
        check_vma=False,
    )
```

```python
from functools import partial

import jax
import jax.numpy as jnp
from jax import lax
from jax.experimental import pallas as pl
from jax.experimental.pallas import tpu as pltpu
from jax.sharding import PartitionSpec as P

HEAD_DIM = 64
BLOCK = 512
PAIR = 2 * HEAD_DIM
CHUNK = 128
SLOTS = 16
EPS = 1e-05
TEMP = 0.01
MASKED = -10000.0
HIGH = lax.Precision.HIGHEST
F32 = jnp.float32
BF16 = jnp.bfloat16
VMEM = pl.BlockSpec(memory_space=pltpu.VMEM)
SMEM = pl.BlockSpec(memory_space=pltpu.SMEM)


def dot(a, b, dims=((1,), (0,)), precision=None):
    return lax.dot_general(a, b, (dims, ((), ())), precision=precision, preferred_element_type=F32)


ROWS = ((0,), (0,))
LANES = ((1,), (1,))


def params(mib):
    return pltpu.CompilerParams(vmem_limit_bytes=mib * 1024 * 1024)


def row(ref):
    return ref[...].reshape(1, ref.shape[0])


def shape(*dims, kind=F32):
    return jax.ShapeDtypeStruct(dims, kind)


def lane_masks(kind):
    first = (lax.broadcasted_iota(jnp.int32, (1, PAIR), 1) < HEAD_DIM).astype(F32)
    return first.astype(kind), (1.0 - first).astype(kind)


def layout(bucket, lengths, me, axis):
    code = bucket[me]
    dims = (BLOCK, 1) if axis == 0 else (1, BLOCK)
    places = lax.broadcasted_iota(jnp.int32, dims, axis)
    shift = jnp.full(dims, jnp.where(code == 3, 9, 5 + code), jnp.int32)
    slot = lax.shift_right_logical(places, shift)
    offset = places - lax.shift_left(slot, shift)
    length = jnp.zeros(dims, jnp.int32)
    for s in range(SLOTS):
        length = jnp.where(slot == s, lengths[me, s], length)
    return slot, jnp.where(offset < length, slot, -1)


def pooling(bucket, lengths, me):
    _, kid = layout(bucket, lengths, me, 1)
    slots = lax.broadcasted_iota(jnp.int32, (SLOTS, BLOCK), 0)
    rows = lax.broadcasted_iota(jnp.int32, (SLOTS, 1), 0)
    length = jnp.zeros((SLOTS, 1), jnp.int32)
    for s in range(SLOTS):
        length = jnp.where(rows == s, lengths[me, s], length)
    member = (slots == kid).astype(F32)
    return member / jnp.maximum(length, 1).astype(F32)


def attend_kernel(
    where, bucket, lengths,
    x, wq, bq, wk, wv, bv,
    q_a, q_b, k_a, k_b, v_a, v_b, ctx_a, ctx_b, lse_a, lse_b, x_t_a, x_t_b,
):
    width = wq.shape[1]
    first, second = lane_masks(BF16)
    low = lax.broadcasted_iota(jnp.int32, (CHUNK, PAIR), 1) < HEAD_DIM
    lane = lax.broadcasted_iota(jnp.int32, (CHUNK, PAIR), 1)
    ones = jnp.ones((BLOCK, PAIR), BF16)
    for me, q_o, k_o, v_o, ctx_o, lse_o, x_t in (
        (1 - where[1], q_b, k_b, v_b, ctx_b, lse_b, x_t_b),
        (where[1], q_a, k_a, v_a, ctx_a, lse_a, x_t_a),
    ):
        tokens = x[pl.ds(pl.multiple_of(me * BLOCK, BLOCK), BLOCK), :]
        x_t[...] = jnp.transpose(tokens)
        slot_col, _ = layout(bucket, lengths, me, 0)
        _, kid_row = layout(bucket, lengths, me, 1)
        q_o[...] = (dot(tokens, wq[...]) + row(bq)).astype(BF16)
        k_o[...] = dot(tokens, wk[...]).astype(BF16)
        v_o[...] = (dot(tokens, wv[...]) + row(bv)).astype(BF16)
        for r in range(BLOCK // CHUNK):
            rows = slice(r * CHUNK, (r + 1) * CHUNK)
            mask = slot_col[rows, :] == kid_row
            mask = jnp.concatenate([mask, mask], 0)
            levels = jnp.zeros((CHUNK, PAIR), F32)
            for pair in range(width // PAIR):
                cols = slice(pair * PAIR, (pair + 1) * PAIR)
                query = q_o[rows, cols] * jnp.asarray(HEAD_DIM**-0.5, BF16)
                both = jnp.concatenate([query * first, query * second], 0)
                scores = jnp.where(mask, dot(both, k_o[:, cols], LANES), MASKED)
                summit = jnp.max(scores, 1, keepdims=True)
                raised = jnp.exp(scores - summit).astype(BF16)
                out = dot(raised, jnp.concatenate([v_o[:, cols], ones], 1))
                mass = out[:, PAIR:]
                out = out[:, :PAIR] / mass
                ctx_o[rows, cols] = jnp.where(low, out[:CHUNK], out[CHUNK:]).astype(BF16)
                logs = jnp.log(mass) + summit
                levels = jnp.where(lane == 2 * pair, logs[:CHUNK], levels)
                levels = jnp.where(lane == 2 * pair + 1, logs[CHUNK:], levels)
            lse_o[rows, :] = levels


def whole(a):
    return pl.BlockSpec(a.shape, lambda j, *_: (0,) * len(a.shape))


def block_rows(a):
    return pl.BlockSpec((BLOCK, a.shape[1]), lambda j, where, *_: (where[1], 0))


def turn_of(side, steps):
    if side is None:
        return lambda j: j
    if side == 0:
        return lambda j: jnp.minimum(j, steps - 1)
    return lambda j: jnp.maximum(j - steps, 0)


def columns(a, tile, side=None):
    at = turn_of(side, a.shape[1] // tile)
    return pl.BlockSpec((a.shape[0], tile), lambda j, *_: (0, at(j)))


def down_rows(a, tile, side=None):
    at = turn_of(side, a.shape[0] // tile)
    return pl.BlockSpec((tile, a.shape[1]), lambda j, *_: (at(j), 0))


def call(
    kernel, scalars, operands, in_specs, outs, out_specs, steps=1, scratch=(), flops=0, mib=60, far=()
):
    operands = [
        pltpu.with_memory_space_constraint(a, pltpu.HBM) if i in far else a
        for i, a in enumerate(operands)
    ]
    moved = sum(a.size * a.dtype.itemsize for a in list(operands) + list(outs))
    return pl.pallas_call(
        kernel,
        grid_spec=pltpu.PrefetchScalarGridSpec(
            num_scalar_prefetch=len(scalars),
            grid=(steps,),
            in_specs=in_specs,
            out_specs=tuple(out_specs),
            scratch_shapes=list(scratch),
        ),
        out_shape=tuple(outs),
        compiler_params=params(mib),
        cost_estimate=pl.CostEstimate(flops=flops, bytes_accessed=moved, transcendentals=0),
        name=kernel.__name__,
    )(*scalars, *operands)


def attend(scalars, x, wq, bq, wk, wv, bv):
    wide, width = wq.shape
    low, level = shape(BLOCK, width, kind=BF16), shape(BLOCK, PAIR)
    turned = shape(wide, BLOCK, kind=BF16)
    outs = (low,) * 8 + (level,) * 2 + (turned,) * 2
    operands = (x, wq, bq, wk, wv, bv)
    flops = 4 * BLOCK * width * (3 * wide + 4 * BLOCK)
    outs = call(
        attend_kernel, scalars, operands, [whole(a) for a in operands],
        outs, [whole(a) for a in outs], flops=flops,
    )
    return outs[0::2], outs[1::2]


def attend_back_block(
    me, bucket, lengths, q, k, v, ctx, lse, dattn, wo, dqk_o, dv_o, sums_o, dscore_s
):
    width = q.shape[1]
    first, second = lane_masks(BF16)
    scale = jnp.asarray(HEAD_DIM**-0.5, BF16)
    dctx = dot(dattn[...], wo[...], LANES).astype(BF16)
    head_of = lax.broadcasted_iota(jnp.int32, (width, PAIR), 0) >> 6
    select = (head_of == lax.broadcasted_iota(jnp.int32, (width, PAIR), 1)).astype(F32)
    inner_sums = dot(select, dctx.astype(F32) * ctx[...].astype(F32), ((0,), (1,)), HIGH)
    levels = jnp.transpose(lse[...])
    slots, _ = layout(bucket, lengths, me, 1)
    _, kid_col = layout(bucket, lengths, me, 0)
    sums_o[...] = jnp.zeros(sums_o.shape, F32)
    low = lax.broadcasted_iota(jnp.int32, (TILE, PAIR), 1) < HEAD_DIM
    for pair in range(width // PAIR):
        cols = slice(pair * PAIR, (pair + 1) * PAIR)
        query = q[:, cols] * scale
        grad = dctx[:, cols]
        sum_k = jnp.zeros((1, PAIR), F32)
        sum_v = jnp.zeros((1, PAIR), F32)
        for c in range(BLOCK // TILE):
            rows = slice(c * TILE, (c + 1) * TILE)
            mask = kid_col[rows, :] == slots
            key_part, value_part = k[rows, cols], v[rows, cols]
            keys = jnp.concatenate([key_part * first, key_part * second], 0)
            values = jnp.concatenate([value_part * first, value_part * second], 0)
            scores, dprobs = dot(keys, query, LANES), dot(values, grad, LANES)
            probs, dscores = [], []
            for e in range(2):
                head, at = 2 * pair + e, slice(e * TILE, (e + 1) * TILE)
                prob = jnp.exp(jnp.where(mask, scores[at], MASKED) - levels[head : head + 1, :])
                dscore = (prob * (dprobs[at] - inner_sums[head : head + 1, :])).astype(BF16)
                dscore_s[e, rows, :] = dscore
                probs.append(prob.astype(BF16))
                dscores.append(dscore)
            dk = dot(jnp.concatenate(dscores, 0), query)
            dv = dot(jnp.concatenate(probs, 0), grad)
            dk = jnp.where(low, dk[:TILE], dk[TILE:]).astype(BF16)
            dv = jnp.where(low, dv[:TILE], dv[TILE:]).astype(BF16)
            dqk_o[rows, width + pair * PAIR : width + (pair + 1) * PAIR] = dk
            dv_o[rows, cols] = dv
            sum_k = sum_k + jnp.sum(dk.astype(F32), 0, keepdims=True)
            sum_v = sum_v + jnp.sum(dv.astype(F32), 0, keepdims=True)
        keys = jnp.transpose(k[:, cols])
        dq = [dot(keys[:HEAD_DIM], dscore_s[0]), dot(keys[HEAD_DIM:], dscore_s[1])]
        dq = (jnp.transpose(jnp.concatenate(dq, 0)) * HEAD_DIM**-0.5).astype(BF16)
        dqk_o[:, cols] = dq
        sums_o[0:1, cols] = jnp.sum(dq.astype(F32), 0, keepdims=True)
        sums_o[1:2, cols] = sum_k
        sums_o[2:3, cols] = sum_v


def own_back_kernel(
    where, bucket, lengths, q, k, v, ctx, lse, dattn, wo, dqk_o, dv_o, sums_o, dscore_s
):
    attend_back_block(
        where[1], bucket, lengths, q, k, v, ctx, lse, dattn, wo, dqk_o, dv_o, sums_o, dscore_s
    )


def other_back_kernel(
    where, bucket, lengths, q, k, v, ctx, lse, dattn, wo,
    x_t_a, x_t_b, ctx_a, dattn_a, dqk_a, dv_a, sums_a, means, vectors,
    dqk_o, dv_o, gone_o, kept_o, vectors_o,
    dscore_s, sums_o,
):
    attend_back_block(
        1 - where[1], bucket, lengths, q, k, v, ctx, lse, dattn, wo, dqk_o, dv_o, sums_o, dscore_s
    )
    width = q.shape[1]
    sums = sums_o[...] + sums_a[...]
    vectors_o[...] = vectors[...]
    vectors_o[6:7, :width] = sums[0:1, :]
    vectors_o[6:7, width:] = sums[1:2, :]
    vectors_o[7:8, :width] = sums[2:3, :]
    bias_out = vectors[5:6, :] + jnp.sum(dattn[...].astype(F32), 0, keepdims=True)
    turned_a, turned_b = jnp.transpose(ctx_a[...]), jnp.transpose(ctx[...])
    side = (where[0] >> where[1]) & 1
    for half, out in ((1 - side, gone_o), (side, kept_o)):
        rows = pl.ds(pl.multiple_of(half * width, width), width)
        rows_a, rows_b = x_t_a[rows, :], x_t_b[rows, :]
        x_mean = means[rows, :][:, 6:7]
        for i, (source_a, source_b, at) in enumerate(
            ((dqk_a, dqk_o, 0), (dqk_a, dqk_o, width), (dv_a, dv_o, 0))
        ):
            grads = dot(rows_a, source_a[:, at : at + width])
            grads = grads + dot(rows_b, source_b[:, at : at + width]) - x_mean * sums[i : i + 1, :]
            out[:, i * width : (i + 1) * width] = grads.astype(BF16)
        grads = dot(turned_a, dattn_a[:, rows]) + dot(turned_b, dattn[:, rows])
        sums_here = jnp.where(half == 0, bias_out[:, :width], bias_out[:, width:])
        grads = grads - means[:width, 5:6] * sums_here
        out[:, 3 * width :] = grads.astype(BF16)


def attend_back(scalars, heads, dattn, wo, extra=None):
    rows, width = heads[0].shape
    wide = dattn.shape[1]
    outs = [shape(rows, 2 * width, kind=BF16), shape(rows, width, kind=BF16)]
    operands = (*heads, dattn, wo)
    scratch = [pltpu.VMEM((2, rows, rows), BF16)]
    if extra is None:
        kernel = own_back_kernel
        outs += [shape(8, width)]
    else:
        kernel = other_back_kernel
        operands += extra
        outs += [shape(wide // 2, 4 * width, kind=BF16)] * 2 + [shape(SLOTS, wide)]
        scratch += [pltpu.VMEM((8, width), F32)]
    return call(
        kernel, scalars, operands, [whole(a) for a in operands],
        outs, [whole(a) for a in outs], 1, scratch, flops=24 * rows * rows * width,
    )


def normed(resid):
    center = resid - jnp.mean(resid, -1, keepdims=True)
    rate = lax.rsqrt(jnp.mean(center * center, -1, keepdims=True) + EPS)
    return center * rate, rate


def normed_back(grad, hat, rate):
    return (
        grad - jnp.mean(grad, -1, keepdims=True) - hat * jnp.mean(grad * hat, -1, keepdims=True)
    ) * rate


def feed_kernel(
    where, bucket, lengths, positive,
    x, ctx_a, ctx_b, wo_a, wo_b, bias_out, gain_one, shift_one,
    wi_a, wi_b, bi_a, bi_b, wd_a, wd_b, bias_down, gain_two, shift_two,
    hat_one_o, rate_one_o, hidden_t_o, act_a_o, act_b_o, slope_a_o, slope_b_o, hat_two_o, rate_two_o,
    packed_o, rate_u_o,
    total, sums, act_sums, hidden_o,
):
    step = pl.program_id(0)
    me = where[1]
    wide = total.shape[1]

    @pl.when(step == 0)
    def _():
        tokens = x[...].astype(F32)
        attn = dot(ctx_a[...], wo_a[...]) + dot(ctx_b[...], wo_b[...]) + row(bias_out)
        hat, rate = normed(tokens + attn)
        hidden = hat * row(gain_one) + row(shift_one)
        hat_one_o[...] = hat
        rate_one_o[...] = jnp.broadcast_to(rate, rate_one_o.shape)
        hidden_low = hidden.astype(BF16)
        hidden_o[...] = hidden_low
        hidden_t_o[...] = jnp.transpose(hidden_low)
        total[...] = hidden + row(bias_down)
        sums[...] = jnp.zeros(sums.shape, F32)
        act_sums[...] = jnp.zeros(act_sums.shape, F32)
        sums[0:1, :] = jnp.sum(hidden, 0, keepdims=True)
        half = ctx_a.shape[1]
        sums[1:2, :half] = jnp.sum(ctx_a[...].astype(F32), 0, keepdims=True)
        sums[1:2, half:] = jnp.sum(ctx_b[...].astype(F32), 0, keepdims=True)
        sums[2:3, :] = jnp.sum(tokens, 0, keepdims=True)

    place = pl.ds(pl.multiple_of(step * WIDE, WIDE), WIDE)

    def chunk(c, carry):
        rows = pl.ds(pl.multiple_of(c * ROWS_AT_ONCE, ROWS_AT_ONCE), ROWS_AT_ONCE)
        hidden = hidden_o[rows, :]
        added = []
        for side, (wi, bi, wd, act_o, slope_o) in enumerate((
            (wi_a, bi_a, wd_a, act_a_o, slope_a_o),
            (wi_b, bi_b, wd_b, act_b_o, slope_b_o),
        )):
            inner = dot(hidden, wi[...]) + row(bi)
            below = 0.5 + 0.5 * lax.erf(inner * (0.5**0.5))
            bell = jnp.exp(inner * inner * -0.5) * 0.3989422804014327
            act = inner * below
            act_sums[side : side + 1, place] += jnp.sum(act, 0, keepdims=True)
            act = act.astype(BF16)
            act_o[rows, :] = act
            slope_o[rows, :] = (below + inner * bell).astype(BF16)
            added.append(dot(act, wd[...]))
        total[rows, :] += added[0] + added[1]
        return carry

    lax.fori_loop(0, BLOCK // ROWS_AT_ONCE, chunk, 0)

    @pl.when(step == pl.num_programs(0) - 1)
    def _():
        hat, rate = normed(total[...])
        hat_two_o[...] = hat
        rate_two_o[...] = jnp.broadcast_to(rate, rate_two_o.shape)
        output = hat * row(gain_two) + row(shift_two)
        raw = dot(pooling(bucket, lengths, me), output, precision=HIGH)
        rate_u = lax.rsqrt(jnp.sum(raw * raw, 1, keepdims=True) + 1e-06)
        rate_u_o[...] = jnp.broadcast_to(rate_u, rate_u_o.shape)
        packed_o[...] = raw * rate_u

        @pl.when(me == 1)
        def _():
            lane = lax.broadcasted_iota(jnp.int32, (1, wide), 1)
            extra = jnp.zeros((1, wide), jnp.int32)
            for s in range(SLOTS):
                extra = jnp.where(lane == s, positive[s], extra)
            for s in range(2):
                extra = jnp.where(lane == SLOTS + s, bucket[s], extra)
            packed_o[4:5, :] = extra.astype(F32)
            packed_o[5:6, :] = act_sums[0:1, :wide]
            packed_o[6:7, :] = act_sums[0:1, wide:]
            packed_o[7:8, :] = act_sums[1:2, :wide]
            packed_o[8:9, :] = act_sums[1:2, wide:]
            packed_o[9:12, :] = sums[0:3, :]


TILE = 256
WIDE = 512
ROWS_AT_ONCE = 256


def feed(scalars, x, ctx, wo, bias_out, gain_one, shift_one, wi, bi, wd, bias_down, gain_two, shift_two):
    rows, wide = BLOCK, x.shape[1]
    units = wi[0].shape[1]
    full = shape(rows, wide)
    rate = shape(rows, PAIR)
    low = shape(rows, units, kind=BF16)
    hidden = shape(wide, rows, kind=BF16)
    operands = (
        x, ctx[0], ctx[1], wo[0], wo[1], bias_out, gain_one, shift_one,
        wi[0], wi[1], bi[0], bi[1], wd[0], wd[1], bias_down, gain_two, shift_two,
    )
    specs = [block_rows(x)] + [whole(a) for a in operands[1:]]
    for side in range(2):
        specs[8 + side] = columns(wi[side], WIDE)
        specs[10 + side] = pl.BlockSpec((WIDE,), lambda j, *_: (j,))
        specs[12 + side] = down_rows(wd[side], WIDE)
    outs = (
        full, rate, hidden, low, low, low, low, full, rate, shape(SLOTS, wide), shape(SLOTS, PAIR),
    )
    out_specs = [whole(a) for a in outs]
    for place in (3, 4, 5, 6):
        out_specs[place] = columns(outs[place], WIDE)
    scratch = [
        pltpu.VMEM((rows, wide), F32), pltpu.VMEM((8, wide), F32), pltpu.VMEM((8, units), F32),
        pltpu.VMEM((rows, wide), BF16),
    ]
    return call(
        feed_kernel, scalars, operands, specs, outs, out_specs, units // WIDE, scratch,
        flops=2 * rows * wide * (wide + 4 * units),
    )


def turn(operands, where):
    def turn_kernel(where, *refs):
        for source, target in zip(refs, refs[len(operands) :]):
            target[...] = jnp.transpose(source[...])

    width = operands[0].shape[1]
    tile = min(TILE, width // 3)
    in_specs = [
        pl.BlockSpec((BLOCK, tile), lambda j, where, k=a.shape[0] // BLOCK - 1: (k * where[1], j))
        for a in operands
    ]
    outs = [shape(a.shape[1], BLOCK, kind=BF16) for a in operands]
    out_specs = [pl.BlockSpec((tile, BLOCK), lambda j, *_: (j, 0)) for _ in operands]
    return call(turn_kernel, (where,), operands, in_specs, outs, out_specs, width // tile, mib=16)


def contrast_kernel(offsets, count, where, bucket, lengths, *refs):
    pieces = len(offsets)
    own, other = refs[:pieces], refs[pieces : 2 * pieces]
    packed, rate_u, hat, rate, gain = refs[2 * pieces : 2 * pieces + 5]
    loss_o, query_o, passage_o, grad_o, low_o, sums_o, common_o, columns_o = refs[2 * pieces + 5 : 2 * pieces + 13]
    asks, table, notes, place_col, live_col, dlogits, common, grad_unit = refs[2 * pieces + 13 :]
    spot, me = where[0], where[1]
    wide = hat.shape[1]
    rows16 = lax.broadcasted_iota(jnp.int32, (8, 1), 0)
    common[...] = jnp.zeros(common.shape, F32)
    notes[...] = jnp.zeros(notes.shape, F32)

    def spread(query_pieces, passage_pieces):
        for piece, places in zip(query_pieces, offsets):
            for i, offset in enumerate(places):
                source = spot ^ offset
                asks[pl.ds(pl.multiple_of(source * SLOTS, SLOTS), SLOTS), :] = piece[i]
        for piece, places in zip(passage_pieces, offsets):
            for i, offset in enumerate(places):
                source = spot ^ offset
                top = piece[i, 0:8, :]
                table[pl.ds(pl.multiple_of(source * 8, 8), 8), :] = jnp.where(rows16 < 4, top, 0.0)
                notes[pl.ds(source, 1), :] = top[4:5, :PAIR]
                common[0:8, :] += top
                common[8:16, :] += piece[i, 8:16, :]

    @pl.when(me == 0)
    def _():
        spread(own, other)

    @pl.when(me == 1)
    def _():
        spread(other, own)

    share = 1.0 / (count * BLOCK)
    first, second = common[5:7, :] * share, common[7:9, :] * share
    common_o[0:2, :] = jnp.where(me == 1, first, second)
    common_o[2:4, :] = jnp.where(me == 1, second, first)
    common_o[4:7, :] = common[9:12, :] * share
    common_o[7:8, :] = jnp.zeros((1, wide), F32)
    half = wide // 2

    @pl.when(me == 0)
    def _():
        common_o[5:6, :half] = common[10:11, half:] * share
        common_o[5:6, half:] = common[10:11, :half] * share

    padding = jnp.zeros((PAIR - 8, wide), F32)
    columns_o[...] = jnp.transpose(jnp.concatenate([common_o[...], padding], 0))

    turned = jnp.transpose(notes[...])
    slots = lax.broadcasted_iota(jnp.int32, (SLOTS, 1), 0).astype(F32)
    for d in range(count):
        at = slice(d * SLOTS, (d + 1) * SLOTS)
        place_col[at, :] = jnp.broadcast_to(turned[0:SLOTS, d : d + 1], (SLOTS, PAIR))
        held = jnp.where(turned[SLOTS : SLOTS + 1, d : d + 1] == 0.0, 16.0, 8.0)
        live_col[at, :] = jnp.broadcast_to((slots < held).astype(F32), (SLOTS, PAIR))
    wide_p = table.shape[0]
    cells = lax.broadcasted_iota(jnp.int32, (PAIR, wide_p), 1)
    sources = lax.broadcasted_iota(jnp.int32, (PAIR, wide_p), 0)
    held = jnp.where(notes[:, SLOTS + 1 : SLOTS + 2] == 2.0, 4, 1)
    live_p = ((cells >> 3) == sources) & ((cells & 7) < held)
    live_p = jnp.sum(live_p.astype(F32), 0, keepdims=True)

    count_q = jnp.sum(live_col[:, :1], 0, keepdims=True)
    rows_q = min(asks.shape[0], BLOCK // 2)

    def part(i, total):
        at = pl.ds(pl.multiple_of(i * rows_q, rows_q), rows_q)
        alive = live_col[at, :][:, :1]
        places = place_col[at, :][:, :1].astype(jnp.int32)
        places = (places >> 2) * 8 + (places & 3)
        logits = dot(asks[at, :], table[...], LANES, HIGH) / TEMP
        logits = jnp.where(live_p > 0, logits, MASKED)
        summit = jnp.max(logits, 1, keepdims=True)
        raised = jnp.exp(logits - summit)
        mass = jnp.sum(raised, 1, keepdims=True)
        normal = summit + jnp.log(mass)
        target = lax.broadcasted_iota(jnp.int32, logits.shape, 1) == places
        picked = jnp.sum(jnp.where(target, logits, 0.0), 1, keepdims=True)
        dlogits[at, :] = (jnp.exp(logits - normal) - target.astype(F32)) * (alive / count_q)
        return total + jnp.sum(alive * (normal - picked), 0, keepdims=True)

    total = jnp.zeros((1, 1), F32)
    if asks.shape[0] == rows_q:
        total = part(0, total)
    else:
        total = lax.fori_loop(0, asks.shape[0] // rows_q, part, total)
    loss_o[...] = total / count_q

    query_o[...] = asks[pl.ds(pl.multiple_of(spot * SLOTS, SLOTS), SLOTS), :]
    passage_o[...] = table[pl.ds(pl.multiple_of(spot * 8, 8), 8), :][0:4, :]

    @pl.when(me == 0)
    def _():
        mine = dlogits[pl.ds(pl.multiple_of(spot * SLOTS, SLOTS), SLOTS), :]
        grad_unit[...] = dot(mine, table[...], precision=HIGH) / TEMP

    @pl.when(me == 1)
    def _():
        cell = lax.broadcasted_iota(jnp.int32, (SLOTS, wide_p), 1)
        slot = lax.broadcasted_iota(jnp.int32, (SLOTS, wide_p), 0)
        mine = ((cell == slot + spot * 8) & (slot < 4)).astype(F32)
        weights = dot(mine, dlogits[...], LANES, HIGH)
        grad_unit[...] = dot(weights, asks[...], precision=HIGH) / TEMP

    slot = lax.broadcasted_iota(jnp.int32, (SLOTS, 1), 0)
    units = jnp.where((slot < 4) | (me == 0), packed[...], 0.0)
    grads = grad_unit[...]
    grad_embed = (grads - units * jnp.sum(units * grads, 1, keepdims=True)) * rate_u[:, :1]
    grad_out = dot(pooling(bucket, lengths, me), grad_embed, ROWS, HIGH)
    hats = hat[...]
    resid = normed_back(grad_out * row(gain), hats, rate[:, :1])
    grad_o[...] = resid
    low = resid.astype(BF16)
    low_o[...] = low
    sums_o[0:1, :] = jnp.sum(grad_out * hats, 0, keepdims=True)
    sums_o[1:2, :] = jnp.sum(grad_out, 0, keepdims=True)
    sums_o[2:3, :] = jnp.sum(low.astype(F32), 0, keepdims=True)
    sums_o[3:8, :] = jnp.zeros((5, wide), F32)


def contrast(scalars, own, other, offsets, packed, rate_u, hat, rate, gain):
    rows, wide = hat.shape
    count = sum(len(o) for o in offsets)
    operands = (*own, *other, packed, rate_u, hat, rate, gain)
    outs = (
        shape(1, 1), shape(SLOTS, wide), shape(4, wide), shape(rows, wide),
        shape(rows, wide, kind=BF16), shape(8, wide), shape(8, wide), shape(wide, PAIR),
    )
    queries, passages = count * SLOTS, count * 8
    scratch = [
        pltpu.VMEM(dims, F32)
        for dims in (
            (queries, wide), (passages, wide), (PAIR, PAIR), (queries, PAIR), (queries, PAIR),
            (queries, passages), (SLOTS, wide), (SLOTS, wide),
        )
    ]
    kernel = partial(contrast_kernel, offsets, count)
    kernel.__name__ = "contrast"
    specs = [whole(a) for a in operands]
    return call(
        kernel, scalars, operands, specs, outs, [whole(a) for a in outs],
        1, scratch, flops=2_000_000_000, mib=40 if count <= 16 else 60,
        far=range(2 * len(own), len(operands)),
    )


def feed_back_kernel(
    where, dffn, gres, wd_a, wd_b, wi_a, wi_b, slope_a, slope_b, hat, rate, gain, hidden_t, means, sums_two,
    into_a_o, into_b_o, grad_o, low_o, vectors_a_o, vectors_b_o,
    total, bias,
):
    step = pl.program_id(0)
    steps = pl.num_programs(0) // 2
    wide = total.shape[1]

    @pl.when(step == 0)
    def _():
        total[...] = gres[...]

    def units(side, step, wd, wi, slope, into_o):
        inner = (dot(dffn[...], wd[...], LANES) * slope[...].astype(F32)).astype(BF16)
        sums = jnp.sum(inner.astype(F32), 0, keepdims=True)
        bias[side : side + 1, pl.ds(pl.multiple_of(step * WIDE, WIDE), WIDE)] = sums
        total[...] += dot(inner, wi[...], LANES)
        into_o[...] = (dot(hidden_t[...], inner) - means[:, 4:5] * sums).astype(BF16)

    @pl.when(step < steps)
    def _():
        units(0, step, wd_a, wi_a, slope_a, into_a_o)

    @pl.when(step >= steps)
    def _():
        units(1, step - steps, wd_b, wi_b, slope_b, into_b_o)

    @pl.when(step == pl.num_programs(0) - 1)
    def _():
        grad = total[...]
        hats = hat[...]
        resid = normed_back(grad * row(gain), hats, rate[:, :1])
        grad_o[...] = resid
        low = resid.astype(BF16)
        low_o[...] = low
        for side, vectors in enumerate((vectors_a_o, vectors_b_o)):
            vectors[...] = jnp.zeros(vectors.shape, F32)
            vectors[0:3, :] = sums_two[0:3, :]
            vectors[3:4, :] = jnp.sum(grad * hats, 0, keepdims=True)
            vectors[4:5, :] = jnp.sum(grad, 0, keepdims=True)
            vectors[5:6, :] = jnp.sum(low.astype(F32), 0, keepdims=True)
            vectors[8:9, :] = bias[side : side + 1, :wide]
            vectors[9:10, :] = bias[side : side + 1, wide:]


def feed_back(where, dffn, gres, wd, wi, slope, hat, rate, gain, hidden_t, means, sums_two):
    rows, wide = dffn.shape
    units = wd[0].shape[0]
    operands = (
        dffn, gres, wd[0], wd[1], wi[0], wi[1], slope[0], slope[1], hat, rate, gain, hidden_t, means, sums_two,
    )
    specs = [whole(a) for a in operands]
    for side in range(2):
        specs[2 + side] = down_rows(wd[side], WIDE, side)
        specs[4 + side] = columns(wi[side], WIDE, side)
        specs[6 + side] = columns(slope[side], WIDE, side)
    into = shape(wide, units, kind=BF16)
    vectors = shape(SLOTS, wide)
    outs = (into, into, shape(rows, wide), shape(rows, wide, kind=BF16), vectors, vectors)
    out_specs = [whole(a) for a in outs]
    for side in range(2):
        out_specs[side] = columns(into, WIDE, side)
    return call(
        feed_back_kernel, (where,), operands, specs, outs, out_specs, 2 * units // WIDE,
        [pltpu.VMEM((rows, wide), F32), pltpu.VMEM((8, units), F32)],
        flops=12 * rows * wide * units, mib=44,
    )


def down_grad(where, act_t, dffn, means):
    units, rows = act_t[0].shape
    wide = dffn[0].shape[1]
    tile = wide // 2

    def half(j, where):
        side = (where[0] >> where[1]) & 1
        return jnp.where(j < 2, 1 - side, side)

    def down_grad_kernel(where, act_a, act_b, dffn_a, dffn_b, means, gone, kept, sums):
        step = pl.program_id(0)

        @pl.when(step == 0)
        def _():
            both = dffn_a[...].astype(F32) + dffn_b[...].astype(F32)
            sums[...] = jnp.broadcast_to(jnp.sum(both, 0, keepdims=True), sums.shape)

        mean = jnp.where(half(step, where) == 0, means[:, 0:1], means[:, 1:2])
        grads = dot(act_a[...], dffn_a[...]) + dot(act_b[...], dffn_b[...])
        grads = (grads - mean * sums[0:1, :]).astype(BF16)

        @pl.when(step < 2)
        def _():
            gone[...] = grads

        @pl.when(step >= 2)
        def _():
            kept[...] = grads

    out = shape(units // 2, wide, kind=BF16)
    act_spec = pl.BlockSpec((tile, rows), lambda j, where: (2 * half(j, where) + j % 2, 0))
    return call(
        down_grad_kernel, (where,), (*act_t, *dffn, means),
        [act_spec, act_spec, whole(dffn[0]), whole(dffn[1]), pl.BlockSpec((tile, PAIR), lambda j, *_: (j % 2, 0))],
        (out, out),
        [
            pl.BlockSpec((tile, wide), lambda j, *_: (jnp.minimum(j, 1), 0)),
            pl.BlockSpec((tile, wide), lambda j, *_: (jnp.maximum(j - 2, 0), 0)),
        ],
        4, [pltpu.VMEM((8, wide), F32)], flops=4 * rows * units * wide, mib=24,
    )


def halved(terms, bit, own):
    return [(array, path + ((bit, own),)) for array, path in terms]


def term(array):
    return array, ()


def block_of(path, where):
    index = 0
    for bit, own in path:
        side = (where[0] >> bit(where)) & 1
        index = 2 * index + (side if own else 1 - side)
    return index


def add(terms):
    return "add", terms, None


def join(pieces, bit):
    return "join", [term(t) for t in pieces], bit


def rows_of(array, path):
    return array.shape[0] >> len(path)


def mixed(where, *jobs):
    if any(rows_of(*job[1][0]) % 16 for job in jobs):
        return [plain(where, *job) for job in jobs]
    operands, specs, outs = [], [], []
    for kind, terms, _ in jobs:
        for array, path in terms:
            block = rows_of(array, path), array.shape[1]
            operands.append(array)
            specs.append(pl.BlockSpec(block, lambda j, where, path=path: (block_of(path, where), 0)))
        outs.append(shape((2 if kind == "join" else 1) * block[0], block[1], kind=BF16))

    def mixed_kernel(where, *refs):
        sources, targets = refs[: len(operands)], refs[len(operands) :]
        for (kind, terms, bit), target in zip(jobs, targets):
            mine, sources = sources[: len(terms)], sources[len(terms) :]
            if kind == "join":
                rows = mine[0].shape[0]
                side = (where[0] >> bit(where)) & 1
                target[pl.ds(pl.multiple_of(side * rows, 16), rows), :] = mine[0][...]
                target[pl.ds(pl.multiple_of((1 - side) * rows, 16), rows), :] = mine[1][...]
            else:
                total = mine[0][...].astype(F32)
                for other in mine[1:]:
                    total = total + other[...].astype(F32)
                target[...] = total.astype(BF16)

    return call(
        mixed_kernel, (where,), operands, specs, outs, [whole(a) for a in outs], mib=24,
        far=[i for i, a in enumerate(operands) if a.size >= BLOCK * BLOCK * 4],
    )


def plain(where, kind, terms, bit):
    if kind == "join":
        (first, _), (second, _) = terms
        side = (where[0] >> bit(where)) & 1
        return jnp.where(
            side == 0, jnp.concatenate([first, second], 0), jnp.concatenate([second, first], 0)
        )
    total = 0.0
    for array, path in terms:
        rows = rows_of(array, path)
        piece = lax.dynamic_slice_in_dim(array, block_of(path, where) * rows, rows, 0)
        total = total + piece.astype(F32)
    return total.astype(BF16)


def finish(where, pieces, means, vectors):
    half, columns = pieces[0].shape
    wide, width = 2 * half, columns // 4

    def finish_kernel(where, first, second, means, vectors, *outs):
        side = (where[0] >> where[1]) & 1
        for place in range(2):
            rows = slice(place * half, (place + 1) * half)
            piece = jnp.where(side == place, first[...], second[...]).astype(F32)
            x_mean = means[rows, 6:7]
            for i, (at, begin) in enumerate(((6, 0), (6, width), (7, 0))):
                sums = vectors[at : at + 1, begin : begin + width]
                outs[i][rows, :] = piece[:, i * width : (i + 1) * width] + x_mean * sums
            columns = slice(place * width, (place + 1) * width)
            outs[3][:, columns] = piece[:, 3 * width :] + means[:width, 5:6] * vectors[5:6, columns]

    outs = (shape(wide, width),) * 3 + (shape(width, wide),)
    operands = (*pieces, means, vectors)
    return call(
        finish_kernel, (where,), operands, [whole(a) for a in operands], outs, [whole(a) for a in outs],
        mib=32,
    )


def swap(tensor):
    return lax.ppermute(tensor, "mp", [(0, 1), (1, 0)])


def flip(tensor, bits):
    count = lax.axis_size("dp")
    return lax.ppermute(tensor, "dp", [(i, i ^ bits) for i in range(count)])


def bit_count():
    return lax.axis_size("dp").bit_length() - 1


def seal(*values):
    return lax.optimization_barrier(values)


def plane(step):
    return lambda where: where[1] ^ step


def over(bit):
    return lambda where: bit


def cross(tensor, step):
    count = lax.axis_size("dp")
    pairs = [
        (2 * d + c, 2 * (d ^ (1 << (step ^ c))) + c) for d in range(count) for c in range(2)
    ]
    return lax.ppermute(tensor, ("dp", "mp"), pairs)


def gather_small(tensor, beside):
    bits = list(range(bit_count()))
    groups = []
    while bits:
        groups.append(bits[-2:])
        bits = bits[:-2]
    tensor, offsets = tensor[None], [0]
    done = []
    for number, group in enumerate(groups):
        ways = range(1 << len(group))
        pieces = [tensor] + [flip(tensor, way << group[0]) for way in ways if way]
        places = [[(way << group[0]) | o for o in offsets] for way in ways]
        if number < len(beside) and beside[number]:
            pieces, work, tensor = seal(pieces, beside[number](tensor), tensor)
            done.append(work)
        if number == len(groups) - 1:
            return pieces, places, done
        tensor = jnp.concatenate(pieces, 0)
        offsets = [o for part in places for o in part]


def shards(
    tokens_in, proj_query, bias_query, proj_key, proj_value, bias_value, proj_out, bias_out,
    gain_attn, shift_attn, proj_in, bias_in, proj_down, bias_down, gain_ffn, shift_ffn,
    bucket, lengths, positive,
):
    spot, me = lax.axis_index("dp"), lax.axis_index("mp")
    wide = tokens_in.shape[1]
    width = proj_query.shape[1]
    units = proj_in.shape[1]
    where = jnp.stack([spot, me]).astype(jnp.int32)
    scalars = (where, bucket, lengths)
    x = tokens_in

    bi = bias_in, swap(bias_in)
    wo, wi, wd = [(w, swap(w)) for w in (proj_out, proj_in, proj_down)]
    heads = attend(scalars, x, proj_query, bias_query, proj_key, proj_value, bias_value)
    heads, x_t = [h[:5] for h in heads], [h[5] for h in heads]
    ctx = heads[0][3], swap(heads[1][3])
    (hat_one, rate_one, hidden_t, act_a, act_b, slope_a, slope_b, hat_two, rate_two, packed, rate_u) = feed(
        scalars + (positive,), x, ctx, wo, bias_out, gain_attn, shift_attn, wi, bi, wd,
        bias_down, gain_ffn, shift_ffn,
    )

    def turn_beside(operands):
        def work(tensor):
            return turn(seal(operands, tensor)[0], where)

        return work

    own, offsets, (act_t,) = gather_small(packed, [None, turn_beside([act_a, act_b])])
    other = [swap(piece) for piece in own]
    act_t = act_t[0], swap(act_t[1])

    loss, query_embed, passage_embed, gres_two, dffn, sums_two, common, means = contrast(
        scalars, own, other, offsets, packed, rate_u, hat_two, rate_two, gain_ffn
    )

    def outer(mean, sums):
        return mean[:, None] * sums[None, :]

    bits = bit_count()
    rest = list(range(2, bits))

    low, *high = rest

    def kept(terms, bit, other):
        return halved(terms, bit, True) + [term(other)]

    def sent(terms, bit):
        return add(halved(terms, bit, False))

    def exchange(tensor):
        for bit in high:
            (tensor,) = mixed(where, add([term(tensor), term(flip(tensor, 1 << bit))]))
        return tensor

    def hold(*values):
        arrays = seal(*[[t[0] for t in v] if is_sum(v) else v for v in values])
        return [
            [(t, old[1]) for t, old in zip(new, v)] if is_sum(v) else new
            for new, v in zip(arrays, values)
        ]

    def is_sum(value):
        return isinstance(value, list) and all(isinstance(t, tuple) and len(t) == 2 and isinstance(t[1], tuple) for t in value)

    dffns = dffn, swap(dffn)
    gone, own = down_grad(where, act_t, dffns, means)
    gone, own, dffn, common, sums_two = seal(gone, own, dffn, common, sums_two)
    down = [term(own), term(cross(gone, 0))]
    fed = feed_back(
        where, dffn, gres_two, wd, wi, (slope_a, slope_b), hat_one, rate_one, gain_attn, hidden_t,
        means, sums_two,
    )
    down, fed = hold(down, fed)
    into_a, into_b, gres_one, dattn, vectors_a, vectors_b = fed

    (gone,) = mixed(where, sent(down, plane(1)))
    gone, down, dattn, into_b = hold(gone, down, dattn, into_b)
    down = kept(down, plane(1), cross(gone, 1))
    into = [term(into_a), term(swap(into_b))]
    dattn_b = swap(dattn)
    back_a = attend_back(scalars, heads[0], dattn, wo[0])
    down, into, back_a, dattn_b = hold(down, into, back_a, dattn_b)

    gone = mixed(where, sent(into, plane(0)), sent(down, over(low)))
    gone, into, down, dattn_b, back_a = hold(gone, into, down, dattn_b, back_a)
    into = kept(into, plane(0), cross(gone[0], 0))
    down = kept(down, over(low), flip(gone[1], 1 << low))
    extra = (*x_t, heads[0][3], dattn, *back_a, means, vectors_a)
    back_b = attend_back(scalars, heads[1], dattn_b, wo[0], extra)
    into, down, back_b = hold(into, down, back_b)
    attn_gone, attn_kept, vectors_a = back_b[2:]

    down, gone = mixed(where, add(down), sent(into, plane(1)))
    gone, into, down = hold(gone, into, down)
    moved = [flip(down, 1 << bit) for bit in high[:1]]
    into = kept(into, plane(1), cross(gone, 1))
    (into,) = hold(into)
    (gone,) = mixed(where, sent(into, over(low)))
    gone, down = hold(gone, down)
    (down,) = mixed(where, add([term(down)] + [term(t) for t in moved]))
    for bit in high[1:]:
        (down,) = mixed(where, add([term(down), term(flip(down, 1 << bit))]))
    into, down, gone, attn_gone, attn_kept = hold(into, down, gone, attn_gone, attn_kept)

    attn = [term(attn_kept), term(cross(attn_gone, 0))]
    into = kept(into, over(low), flip(gone, 1 << low))
    down = [down, flip(down, 1 << low)]
    small = [vectors_a, swap(vectors_b)]
    small, attn, into, down = hold(small, attn, into, down)

    gone, down, into = mixed(where, sent(attn, plane(1)), join(down, over(low)), add(into))
    gone, attn, into, down, small = hold(gone, attn, into, down, small)
    attn = kept(attn, plane(1), cross(gone, 1))
    down = [down, cross(down, 1)]
    into = exchange(into)
    small = small[0] + small[1]
    small = [small, flip(small, 1)]
    attn, down, into, small = hold(attn, down, into, small)

    down, gone = mixed(where, join(down, plane(1)), sent(attn, over(low)))
    gone, attn, down, into, small = hold(gone, attn, down, into, small)
    down = [down, cross(down, 0)]
    attn = kept(attn, over(low), flip(gone, 1 << low))
    into = [into, flip(into, 1 << low)]
    small = small[0] + small[1]
    small = small + flip(small, 2)
    small, gres_one, backs = seal(small, gres_one, (back_a[:2], back_b[:2]))
    grad_in = []
    for dqk, dv in backs:
        parts = dot(dqk[:, :width], proj_query, LANES) + dot(dqk[:, width:], proj_key, LANES)
        grad_in.append(parts + dot(dv, proj_value, LANES))
    grad_in = grad_in[0] + gres_one, grad_in[1].astype(BF16)
    attn, down, into, small, grad_in = hold(attn, down, into, small, grad_in)

    into, attn = mixed(where, join(into, over(low)), add(attn))
    attn, into, down, small = seal(attn, into, down, small)
    into = [into, cross(into, 1)]
    attn = exchange(attn)
    small = small + flip(small, 1 << low)
    down = plain(where, *join(down, plane(0)))
    attn, into, down, small, grad_in = seal(attn, into, down, small, grad_in)

    (into,) = mixed(where, join(into, plane(1)))
    attn, into, small, grad_in = seal(attn, into, small, grad_in)
    into = [into, cross(into, 0)]
    attn = [attn, flip(attn, 1 << low)]
    for bit in high:
        small = small + flip(small, 1 << bit)
    grad_in = (grad_in[0] + swap(grad_in[1]).astype(F32)).astype(BF16)
    attn, into, small, down, grad_in, common = seal(attn, into, small, down, grad_in, common)

    attn = plain(where, *join(attn, over(low)))
    attn, into, small, common = seal(attn, into, small, common)
    attn = [attn, cross(attn, 1)]
    into = plain(where, *join(into, plane(0)))
    share = lax.dynamic_slice_in_dim(small[0:6], me * width, width, 1)
    d_g2, d_s2, d_bd, d_g1, d_s1, d_bo = [share[i] for i in range(6)]
    own_half = small[6:].reshape(-1)
    d_bq, d_bv = own_half[:width], own_half[2 * width : 3 * width]
    d_bi = small[8:10].reshape(units)
    act_mean, hidden_mean = common[0:2].reshape(units), common[4]
    factors = act_mean, small[2], hidden_mean, d_bi
    attn, into, down, factors = seal(attn, into, down, factors)

    (attn,) = mixed(where, join(attn, plane(1)))
    attn, into, down, factors = seal(attn, into, down, factors)
    attn = [attn, cross(attn, 0)]
    other_in = swap(grad_in)
    grad_input = jnp.where(
        me == 0,
        jnp.concatenate([grad_in, other_in], 0),
        jnp.concatenate([other_in, grad_in], 0),
    )
    grad_down = down.astype(F32) + outer(*factors[0:2])
    grad_into = into.astype(F32) + outer(*factors[2:4])
    attn, grad_down, grad_into, grad_input = seal(attn, grad_down, grad_into, grad_input)
    grad_q, grad_k, grad_v, grad_o = finish(where, attn, means, small)
    return (
        loss[0, 0],
        query_embed,
        passage_embed,
        grad_input,
        grad_q,
        d_bq,
        grad_k,
        grad_v,
        d_bv,
        grad_o,
        d_bo,
        d_g1,
        d_s1,
        grad_into,
        d_bi,
        grad_down,
        d_bd,
        d_g2,
        d_s2,
    )


def solution(mesh):
    half, rows = P(None, "mp"), P("mp", None)
    return jax.shard_map(
        shards,
        mesh=mesh,
        in_specs=(
            P("dp", None), half, P("mp"), half, half, P("mp"), rows, P(), P(), P(),
            half, P("mp"), rows, P(), P(), P(), P("dp"), P("dp", None), P("dp"),
        ),
        out_specs=(
            P(), P("dp", None), P("dp", None), P("dp", None),
            half, P("mp"), half, half, P("mp"), rows, P("mp"), P("mp"), P("mp"),
            half, P("mp"), rows, P("mp"), P("mp"), P("mp"),
        ),
        check_vma=False,
    )
```

```python
from functools import partial

import jax
import jax.numpy as jnp
from jax import lax
from jax.experimental import pallas as pl
from jax.experimental.pallas import tpu as pltpu
from jax.sharding import PartitionSpec as P

HEAD_DIM = 64
BLOCK = 512
PAIR = 2 * HEAD_DIM
CHUNK = 128
SLOTS = 16
EPS = 1e-05
TEMP = 0.01
MASKED = -10000.0
HIGH = lax.Precision.HIGHEST
F32 = jnp.float32
BF16 = jnp.bfloat16
VMEM = pl.BlockSpec(memory_space=pltpu.VMEM)
SMEM = pl.BlockSpec(memory_space=pltpu.SMEM)


def dot(a, b, dims=((1,), (0,)), precision=None):
    return lax.dot_general(a, b, (dims, ((), ())), precision=precision, preferred_element_type=F32)


ROWS = ((0,), (0,))
LANES = ((1,), (1,))


def pieces_of(x, count=3):
    pieces = []
    for _ in range(count):
        pieces.append(x.astype(BF16))
        x = x - pieces[-1].astype(F32)
    return pieces


def dots(a, b, dims=((1,), (0,))):
    total = 0.0
    for i, x in enumerate(a):
        for j, y in enumerate(b):
            if i + j < 3:
                total = total + dot(x, y, dims)
    return total


def params(mib):
    return pltpu.CompilerParams(vmem_limit_bytes=mib * 1024 * 1024)


def row(ref):
    return ref[...].reshape(1, ref.shape[0])


def shape(*dims, kind=F32):
    return jax.ShapeDtypeStruct(dims, kind)


def lane_masks(kind):
    first = (lax.broadcasted_iota(jnp.int32, (1, PAIR), 1) < HEAD_DIM).astype(F32)
    return first.astype(kind), (1.0 - first).astype(kind)


def layout(bucket, lengths, me, axis):
    code = bucket[me]
    dims = (BLOCK, 1) if axis == 0 else (1, BLOCK)
    places = lax.broadcasted_iota(jnp.int32, dims, axis)
    shift = jnp.full(dims, jnp.where(code == 3, 9, 5 + code), jnp.int32)
    slot = lax.shift_right_logical(places, shift)
    offset = places - lax.shift_left(slot, shift)
    length = jnp.zeros(dims, jnp.int32)
    for s in range(SLOTS):
        length = jnp.where(slot == s, lengths[me, s], length)
    return slot, jnp.where(offset < length, slot, -1)


def pooling(bucket, lengths, me):
    _, kid = layout(bucket, lengths, me, 1)
    slots = lax.broadcasted_iota(jnp.int32, (SLOTS, BLOCK), 0)
    rows = lax.broadcasted_iota(jnp.int32, (SLOTS, 1), 0)
    length = jnp.zeros((SLOTS, 1), jnp.int32)
    for s in range(SLOTS):
        length = jnp.where(rows == s, lengths[me, s], length)
    return (slots == kid).astype(BF16), jnp.maximum(length, 1).astype(F32)


def attend_kernel(
    where, bucket, lengths,
    x, wq, bq, wk, wv, bv,
    q_a, q_b, k_a, k_b, v_a, v_b, ctx_a, ctx_b, lse_a, lse_b, x_t_a, x_t_b,
):
    width = wq.shape[1]
    first, second = lane_masks(BF16)
    low = lax.broadcasted_iota(jnp.int32, (CHUNK, PAIR), 1) < HEAD_DIM
    lane = lax.broadcasted_iota(jnp.int32, (CHUNK, PAIR), 1)
    ones = jnp.ones((BLOCK, PAIR), BF16)
    for me, q_o, k_o, v_o, ctx_o, lse_o, x_t in (
        (1 - where[1], q_b, k_b, v_b, ctx_b, lse_b, x_t_b),
        (where[1], q_a, k_a, v_a, ctx_a, lse_a, x_t_a),
    ):
        tokens = x[pl.ds(pl.multiple_of(me * BLOCK, BLOCK), BLOCK), :]
        x_t[...] = jnp.transpose(tokens)
        slot_col, _ = layout(bucket, lengths, me, 0)
        _, kid_row = layout(bucket, lengths, me, 1)
        q_o[...] = (dot(tokens, wq[...]) + row(bq)).astype(BF16)
        k_o[...] = dot(tokens, wk[...]).astype(BF16)
        v_o[...] = (dot(tokens, wv[...]) + row(bv)).astype(BF16)
        for r in range(BLOCK // CHUNK):
            rows = slice(r * CHUNK, (r + 1) * CHUNK)
            mask = slot_col[rows, :] == kid_row
            mask = jnp.concatenate([mask, mask], 0)
            levels = jnp.zeros((CHUNK, PAIR), F32)
            for pair in range(width // PAIR):
                cols = slice(pair * PAIR, (pair + 1) * PAIR)
                query = q_o[rows, cols] * jnp.asarray(HEAD_DIM**-0.5, BF16)
                both = jnp.concatenate([query * first, query * second], 0)
                scores = jnp.where(mask, dot(both, k_o[:, cols], LANES), MASKED)
                summit = jnp.max(scores, 1, keepdims=True)
                raised = jnp.exp(scores - summit).astype(BF16)
                out = dot(raised, jnp.concatenate([v_o[:, cols], ones], 1))
                mass = out[:, PAIR:]
                out = out[:, :PAIR] / mass
                ctx_o[rows, cols] = jnp.where(low, out[:CHUNK], out[CHUNK:]).astype(BF16)
                logs = jnp.log(mass) + summit
                levels = jnp.where(lane == 2 * pair, logs[:CHUNK], levels)
                levels = jnp.where(lane == 2 * pair + 1, logs[CHUNK:], levels)
            lse_o[rows, :] = levels


def whole(a):
    return pl.BlockSpec(a.shape, lambda j, *_: (0,) * len(a.shape))


def block_rows(a):
    return pl.BlockSpec((BLOCK, a.shape[1]), lambda j, where, *_: (where[1], 0))


def turn_of(side, steps):
    if side is None:
        return lambda j: j
    if side == 0:
        return lambda j: jnp.minimum(j, steps - 1)
    return lambda j: jnp.maximum(j - steps, 0)


def columns(a, tile, side=None):
    at = turn_of(side, a.shape[1] // tile)
    return pl.BlockSpec((a.shape[0], tile), lambda j, *_: (0, at(j)))


def down_rows(a, tile, side=None):
    at = turn_of(side, a.shape[0] // tile)
    return pl.BlockSpec((tile, a.shape[1]), lambda j, *_: (at(j), 0))


def call(
    kernel, scalars, operands, in_specs, outs, out_specs, steps=1, scratch=(), flops=0, mib=60, far=()
):
    operands = [
        pltpu.with_memory_space_constraint(a, pltpu.HBM) if i in far else a
        for i, a in enumerate(operands)
    ]
    moved = sum(a.size * a.dtype.itemsize for a in list(operands) + list(outs))
    return pl.pallas_call(
        kernel,
        grid_spec=pltpu.PrefetchScalarGridSpec(
            num_scalar_prefetch=len(scalars),
            grid=(steps,),
            in_specs=in_specs,
            out_specs=tuple(out_specs),
            scratch_shapes=list(scratch),
        ),
        out_shape=tuple(outs),
        compiler_params=params(mib),
        cost_estimate=pl.CostEstimate(flops=flops, bytes_accessed=moved, transcendentals=0),
        name=kernel.__name__,
    )(*scalars, *operands)


def attend(scalars, x, wq, bq, wk, wv, bv):
    wide, width = wq.shape
    low, level = shape(BLOCK, width, kind=BF16), shape(BLOCK, PAIR)
    turned = shape(wide, BLOCK, kind=BF16)
    outs = (low,) * 8 + (level,) * 2 + (turned,) * 2
    operands = (x, wq, bq, wk, wv, bv)
    flops = 4 * BLOCK * width * (3 * wide + 4 * BLOCK)
    outs = call(
        attend_kernel, scalars, operands, [whole(a) for a in operands],
        outs, [whole(a) for a in outs], flops=flops,
    )
    return outs[0::2], outs[1::2]


def attend_back_block(
    me, bucket, lengths, q, k, v, ctx, lse, dattn, wo, dqk_o, dv_o, sums_o, dscore_s
):
    width = q.shape[1]
    first, second = lane_masks(BF16)
    scale = jnp.asarray(HEAD_DIM**-0.5, BF16)
    dctx = dot(dattn[...], wo[...], LANES).astype(BF16)
    head_of = lax.broadcasted_iota(jnp.int32, (width, PAIR), 0) >> 6
    select = (head_of == lax.broadcasted_iota(jnp.int32, (width, PAIR), 1)).astype(F32)
    inner_sums = dot(select, dctx.astype(F32) * ctx[...].astype(F32), ((0,), (1,)), HIGH)
    levels = jnp.transpose(lse[...])
    slots, _ = layout(bucket, lengths, me, 1)
    _, kid_col = layout(bucket, lengths, me, 0)
    sums_o[...] = jnp.zeros(sums_o.shape, F32)
    low = lax.broadcasted_iota(jnp.int32, (TILE, PAIR), 1) < HEAD_DIM
    for pair in range(width // PAIR):
        cols = slice(pair * PAIR, (pair + 1) * PAIR)
        query = q[:, cols] * scale
        grad = dctx[:, cols]
        sum_k = jnp.zeros((1, PAIR), F32)
        sum_v = jnp.zeros((1, PAIR), F32)
        for c in range(BLOCK // TILE):
            rows = slice(c * TILE, (c + 1) * TILE)
            mask = kid_col[rows, :] == slots
            key_part, value_part = k[rows, cols], v[rows, cols]
            keys = jnp.concatenate([key_part * first, key_part * second], 0)
            values = jnp.concatenate([value_part * first, value_part * second], 0)
            scores, dprobs = dot(keys, query, LANES), dot(values, grad, LANES)
            probs, dscores = [], []
            for e in range(2):
                head, at = 2 * pair + e, slice(e * TILE, (e + 1) * TILE)
                prob = jnp.exp(jnp.where(mask, scores[at], MASKED) - levels[head : head + 1, :])
                dscore = (prob * (dprobs[at] - inner_sums[head : head + 1, :])).astype(BF16)
                dscore_s[e, rows, :] = dscore
                probs.append(prob.astype(BF16))
                dscores.append(dscore)
            dk = dot(jnp.concatenate(dscores, 0), query)
            dv = dot(jnp.concatenate(probs, 0), grad)
            dk = jnp.where(low, dk[:TILE], dk[TILE:]).astype(BF16)
            dv = jnp.where(low, dv[:TILE], dv[TILE:]).astype(BF16)
            dqk_o[rows, width + pair * PAIR : width + (pair + 1) * PAIR] = dk
            dv_o[rows, cols] = dv
            sum_k = sum_k + jnp.sum(dk.astype(F32), 0, keepdims=True)
            sum_v = sum_v + jnp.sum(dv.astype(F32), 0, keepdims=True)
        keys = jnp.transpose(k[:, cols])
        dq = [dot(keys[:HEAD_DIM], dscore_s[0]), dot(keys[HEAD_DIM:], dscore_s[1])]
        dq = (jnp.transpose(jnp.concatenate(dq, 0)) * HEAD_DIM**-0.5).astype(BF16)
        dqk_o[:, cols] = dq
        sums_o[0:1, cols] = jnp.sum(dq.astype(F32), 0, keepdims=True)
        sums_o[1:2, cols] = sum_k
        sums_o[2:3, cols] = sum_v


def own_back_kernel(
    where, bucket, lengths, q, k, v, ctx, lse, dattn, wo, dqk_o, dv_o, sums_o, dscore_s
):
    attend_back_block(
        where[1], bucket, lengths, q, k, v, ctx, lse, dattn, wo, dqk_o, dv_o, sums_o, dscore_s
    )


def other_back_kernel(
    where, bucket, lengths, q, k, v, ctx, lse, dattn, wo,
    x_t_a, x_t_b, ctx_a, dattn_a, dqk_a, dv_a, sums_a, means, vectors,
    dqk_o, dv_o, gone_a_o, gone_b_o, kept_a_o, kept_b_o, vectors_o,
    dscore_s, sums_o,
):
    attend_back_block(
        1 - where[1], bucket, lengths, q, k, v, ctx, lse, dattn, wo, dqk_o, dv_o, sums_o, dscore_s
    )
    width = q.shape[1]
    sums = sums_o[...] + sums_a[...]
    vectors_o[...] = vectors[...]
    vectors_o[6:7, :width] = sums[0:1, :]
    vectors_o[6:7, width:] = sums[1:2, :]
    vectors_o[7:8, :width] = sums[2:3, :]
    bias_out = vectors[5:6, :] + jnp.sum(dattn[...].astype(F32), 0, keepdims=True)
    turned_a, turned_b = jnp.transpose(ctx_a[...]), jnp.transpose(ctx[...])
    side = (where[0] >> where[1]) & 1
    for half, first, second in ((1 - side, gone_a_o, gone_b_o), (side, kept_a_o, kept_b_o)):
        rows = pl.ds(pl.multiple_of(half * width, width), width)
        rows_a, rows_b = x_t_a[rows, :], x_t_b[rows, :]
        x_mean = means[rows, :][:, 6:7]
        for i, (source_a, source_b, at) in enumerate(
            ((dqk_a, dqk_o, 0), (dqk_a, dqk_o, width), (dv_a, dv_o, 0))
        ):
            grads = dot(rows_a, source_a[:, at : at + width])
            grads = grads + dot(rows_b, source_b[:, at : at + width]) - x_mean * sums[i : i + 1, :]
            out = (first, first, second)[i]
            out[:, at : at + width] = grads.astype(BF16)
        grads = dot(turned_a, dattn_a[:, rows]) + dot(turned_b, dattn[:, rows])
        sums_here = jnp.where(half == 0, bias_out[:, :width], bias_out[:, width:])
        grads = grads - means[:width, 5:6] * sums_here
        second[:, width:] = grads.astype(BF16)


def attend_back(scalars, heads, dattn, wo, extra=None):
    rows, width = heads[0].shape
    wide = dattn.shape[1]
    outs = [shape(rows, 2 * width, kind=BF16), shape(rows, width, kind=BF16)]
    operands = (*heads, dattn, wo)
    scratch = [pltpu.VMEM((2, rows, rows), BF16)]
    if extra is None:
        kernel = own_back_kernel
        outs += [shape(8, width)]
    else:
        kernel = other_back_kernel
        operands += extra
        outs += [shape(wide // 2, 2 * width, kind=BF16)] * 4 + [shape(SLOTS, wide)]
        scratch += [pltpu.VMEM((8, width), F32)]
    return call(
        kernel, scalars, operands, [whole(a) for a in operands],
        outs, [whole(a) for a in outs], 1, scratch, flops=24 * rows * rows * width,
    )


def input_grad(where, gres, backs, weights):
    rows, wide = gres.shape
    width = weights[0].shape[1]

    def input_grad_kernel(where, gres, dqk_a, dv_a, dqk_b, dv_b, wq, wk, wv, own_o, other_o):
        for dqk, dv, out in ((dqk_a, dv_a, own_o), (dqk_b, dv_b, other_o)):
            parts = dot(dqk[:, :width], wq[...], LANES) + dot(dqk[:, width:], wk[...], LANES)
            parts = parts + dot(dv[...], wv[...], LANES)
            out[...] = parts + gres[...] if out is own_o else parts.astype(BF16)

    operands = (gres, *backs[0], *backs[1], *weights)
    outs = shape(rows, wide), shape(rows, wide, kind=BF16)
    return call(
        input_grad_kernel, (where,), operands, [whole(a) for a in operands],
        outs, [whole(a) for a in outs], flops=12 * rows * wide * width, mib=28, far=range(8),
    )


def normed(resid):
    center = resid - jnp.mean(resid, -1, keepdims=True)
    rate = lax.rsqrt(jnp.mean(center * center, -1, keepdims=True) + EPS)
    return center * rate, rate


def normed_back(grad, hat, rate):
    return (
        grad - jnp.mean(grad, -1, keepdims=True) - hat * jnp.mean(grad * hat, -1, keepdims=True)
    ) * rate


def feed_kernel(
    where, bucket, lengths, positive,
    x, ctx_a, ctx_b, wo_a, wo_b, bias_out, gain_one, shift_one,
    wi_a, wi_b, bi_a, bi_b, wd_a, wd_b, bias_down, gain_two, shift_two,
    hat_one_o, rate_one_o, hidden_t_o, act_t_a_o, act_t_b_o, slope_a_o, slope_b_o, hat_two_o, rate_two_o,
    unit_o, packed_o, rate_u_o,
    total, sums, act_sums, hidden_o, packing,
):
    step = pl.program_id(0)
    me = where[1]
    wide = total.shape[1]

    @pl.when(step == 0)
    def _():
        tokens = x[...].astype(F32)
        attn = dot(ctx_a[...], wo_a[...]) + dot(ctx_b[...], wo_b[...]) + row(bias_out)
        hat, rate = normed(tokens + attn)
        hidden = hat * row(gain_one) + row(shift_one)
        hat_one_o[...] = hat
        rate_one_o[...] = jnp.broadcast_to(rate, rate_one_o.shape)
        hidden_low = hidden.astype(BF16)
        hidden_o[...] = hidden_low
        hidden_t_o[...] = jnp.transpose(hidden_low)
        total[...] = hidden + row(bias_down)
        sums[...] = jnp.zeros(sums.shape, F32)
        act_sums[...] = jnp.zeros(act_sums.shape, F32)
        sums[0:1, :] = jnp.sum(hidden, 0, keepdims=True)
        half = ctx_a.shape[1]
        sums[1:2, :half] = jnp.sum(ctx_a[...].astype(F32), 0, keepdims=True)
        sums[1:2, half:] = jnp.sum(ctx_b[...].astype(F32), 0, keepdims=True)
        sums[2:3, :] = jnp.sum(tokens, 0, keepdims=True)

    place = pl.ds(pl.multiple_of(step * WIDE, WIDE), WIDE)

    def chunk(c, carry):
        rows = pl.ds(pl.multiple_of(c * ROWS_AT_ONCE, ROWS_AT_ONCE), ROWS_AT_ONCE)
        hidden = hidden_o[rows, :]
        added = []
        for side, (wi, bi, wd, act_o, slope_o) in enumerate((
            (wi_a, bi_a, wd_a, act_t_a_o, slope_a_o),
            (wi_b, bi_b, wd_b, act_t_b_o, slope_b_o),
        )):
            inner = dot(hidden, wi[...]) + row(bi)
            below = 0.5 + 0.5 * lax.erf(inner * (0.5**0.5))
            bell = jnp.exp(inner * inner * -0.5) * 0.3989422804014327
            act = inner * below
            act_sums[side : side + 1, place] += jnp.sum(act, 0, keepdims=True)
            act = act.astype(BF16)
            act_o[:, rows] = jnp.transpose(act)
            slope_o[rows, :] = (below + inner * bell).astype(BF16)
            added.append(dot(act, wd[...]))
        total[rows, :] += added[0] + added[1]
        return carry

    lax.fori_loop(0, BLOCK // ROWS_AT_ONCE, chunk, 0)

    @pl.when(step == pl.num_programs(0) - 1)
    def _():
        hat, rate = normed(total[...])
        hat_two_o[...] = hat
        rate_two_o[...] = jnp.broadcast_to(rate, rate_two_o.shape)
        output = hat * row(gain_two) + row(shift_two)
        member, length = pooling(bucket, lengths, me)
        raw = dots([member], pieces_of(output)) / length
        rate_u = lax.rsqrt(jnp.sum(raw * raw, 1, keepdims=True) + 1e-06)
        rate_u_o[...] = jnp.broadcast_to(rate_u, rate_u_o.shape)
        unit = raw * rate_u
        unit_o[...] = unit
        packing[...] = unit

        @pl.when(me == 1)
        def _():
            packing[4:8, :] = unit[0:4] - unit[0:4].astype(BF16).astype(F32)
            lane = lax.broadcasted_iota(jnp.int32, (1, wide), 1)
            extra = jnp.zeros((1, wide), jnp.int32)
            for s in range(SLOTS):
                extra = jnp.where(lane == s, positive[s] & 255, extra)
                extra = jnp.where(lane == 2 * SLOTS + s, positive[s] >> 8, extra)
            for s in range(2):
                extra = jnp.where(lane == 4 * SLOTS + s, bucket[s], extra)
            packing[8:9, :] = extra.astype(F32)
            packing[9:10, :] = act_sums[0:1, :wide]
            packing[10:11, :] = act_sums[0:1, wide:]
            packing[11:12, :] = act_sums[1:2, :wide]
            packing[12:13, :] = act_sums[1:2, wide:]
            packing[13:16, :] = sums[0:3, :]

        packed_o[...] = packing[...].astype(BF16)


TILE = 256
WIDE = 512
ROWS_AT_ONCE = 256


def feed(scalars, x, ctx, wo, bias_out, gain_one, shift_one, wi, bi, wd, bias_down, gain_two, shift_two):
    rows, wide = BLOCK, x.shape[1]
    units = wi[0].shape[1]
    full = shape(rows, wide)
    rate = shape(rows, PAIR)
    low = shape(rows, units, kind=BF16)
    turned = shape(units, rows, kind=BF16)
    hidden = shape(wide, rows, kind=BF16)
    operands = (
        x, ctx[0], ctx[1], wo[0], wo[1], bias_out, gain_one, shift_one,
        wi[0], wi[1], bi[0], bi[1], wd[0], wd[1], bias_down, gain_two, shift_two,
    )
    specs = [block_rows(x)] + [whole(a) for a in operands[1:]]
    for side in range(2):
        specs[8 + side] = columns(wi[side], WIDE)
        specs[10 + side] = pl.BlockSpec((WIDE,), lambda j, *_: (j,))
        specs[12 + side] = down_rows(wd[side], WIDE)
    outs = (
        full, rate, hidden, turned, turned, low, low, full, rate,
        shape(SLOTS, wide), shape(SLOTS, wide, kind=BF16), shape(SLOTS, PAIR),
    )
    out_specs = [whole(a) for a in outs]
    for place in (3, 4):
        out_specs[place] = down_rows(outs[place], WIDE)
    for place in (5, 6):
        out_specs[place] = columns(outs[place], WIDE)
    scratch = [
        pltpu.VMEM((rows, wide), F32), pltpu.VMEM((8, wide), F32), pltpu.VMEM((8, units), F32),
        pltpu.VMEM((rows, wide), BF16), pltpu.VMEM((SLOTS, wide), F32),
    ]
    return call(
        feed_kernel, scalars, operands, specs, outs, out_specs, units // WIDE, scratch,
        mib=48, far=[i for i in range(17) if i not in (2, 4, 9, 13)],
        flops=2 * rows * wide * (wide + 4 * units),
    )


def contrast_kernel(offsets, count, where, bucket, lengths, *refs):
    pieces = len(offsets)
    own, other = refs[:pieces], refs[pieces : 2 * pieces]
    unit, unit_b, rate_u, hat, rate, gain = refs[2 * pieces : 2 * pieces + 6]
    loss_o, query_o, passage_o, grad_o, low_o, sums_o, common_o, columns_o = refs[2 * pieces + 6 : 2 * pieces + 14]
    asks, table, notes, place_col, live_col, dlogits, common, grad_unit = refs[2 * pieces + 14 :]
    spot, me = where[0], where[1]
    wide = hat.shape[1]
    common[...] = jnp.zeros(common.shape, F32)
    notes[...] = jnp.zeros(notes.shape, F32)

    def spread(query_pieces, passage_pieces):
        for piece, places in zip(query_pieces, offsets):
            for i, offset in enumerate(places):
                source = spot ^ offset
                asks[pl.ds(pl.multiple_of(source * SLOTS, SLOTS), SLOTS), :] = piece[i]
        for piece, places in zip(passage_pieces, offsets):
            for i, offset in enumerate(places):
                source = spot ^ offset
                rows = piece[i].astype(F32)
                four = rows[0:4] + rows[4:8]
                four = jnp.concatenate([four, jnp.zeros_like(four)], 0)
                table[pl.ds(pl.multiple_of(source * 8, 8), 8), :] = four
                notes[pl.ds(source, 1), :] = rows[8:9, :PAIR]
                common[...] += rows[8:16]

    @pl.when(me == 0)
    def _():
        spread(own, other)

    @pl.when(me == 1)
    def _():
        spread(other, own)

    share = 1.0 / (count * BLOCK)
    first, second = common[1:3, :] * share, common[3:5, :] * share
    common_o[0:2, :] = jnp.where(me == 1, first, second)
    common_o[2:4, :] = jnp.where(me == 1, second, first)
    common_o[4:7, :] = common[5:8, :] * share
    common_o[7:8, :] = jnp.zeros((1, wide), F32)
    half = wide // 2

    @pl.when(me == 0)
    def _():
        common_o[5:6, :half] = common[6:7, half:] * share
        common_o[5:6, half:] = common[6:7, :half] * share

    padding = jnp.zeros((PAIR - 8, wide), F32)
    columns_o[...] = jnp.transpose(jnp.concatenate([common_o[...], padding], 0))

    turned = jnp.transpose(notes[...])
    slots = lax.broadcasted_iota(jnp.int32, (SLOTS, 1), 0).astype(F32)
    for d in range(count):
        at = slice(d * SLOTS, (d + 1) * SLOTS)
        place = turned[0:SLOTS, d : d + 1] + 256.0 * turned[2 * SLOTS : 3 * SLOTS, d : d + 1]
        place_col[at, :] = jnp.broadcast_to(place, (SLOTS, PAIR))
        held = jnp.where(turned[4 * SLOTS : 4 * SLOTS + 1, d : d + 1] == 0.0, 16.0, 8.0)
        live_col[at, :] = jnp.broadcast_to((slots < held).astype(F32), (SLOTS, PAIR))
    wide_p = table.shape[0]
    cells = lax.broadcasted_iota(jnp.int32, (PAIR, wide_p), 1)
    sources = lax.broadcasted_iota(jnp.int32, (PAIR, wide_p), 0)
    held = jnp.where(notes[:, 4 * SLOTS + 1 : 4 * SLOTS + 2] == 2.0, 4, 1)
    live_p = ((cells >> 3) == sources) & ((cells & 7) < held)
    live_p = jnp.sum(live_p.astype(F32), 0, keepdims=True)

    count_q = jnp.sum(live_col[:, :1], 0, keepdims=True)
    rows_q = min(asks.shape[0], BLOCK // 2)

    passages = pieces_of(table[...], 2)

    def scored(asking, at):
        alive = live_col[at, :][:, :1]
        places = place_col[at, :][:, :1].astype(jnp.int32)
        places = (places >> 2) * 8 + (places & 3)
        logits = dots(asking, passages, LANES) / TEMP
        logits = jnp.where(live_p > 0, logits, MASKED)
        summit = jnp.max(logits, 1, keepdims=True)
        raised = jnp.exp(logits - summit)
        mass = jnp.sum(raised, 1, keepdims=True)
        normal = summit + jnp.log(mass)
        target = lax.broadcasted_iota(jnp.int32, logits.shape, 1) == places
        picked = jnp.sum(jnp.where(target, logits, 0.0), 1, keepdims=True)
        grads = (jnp.exp(logits - normal) - target.astype(F32)) * (alive / count_q)
        return grads, jnp.sum(alive * (normal - picked), 0, keepdims=True)

    def part(i, total):
        at = pl.ds(pl.multiple_of(i * rows_q, rows_q), rows_q)
        dlogits[at, :], loss = scored([asks[at, :]], at)
        return total + loss

    total = jnp.zeros((1, 1), F32)
    if asks.shape[0] == rows_q:
        total = part(0, total)
    else:
        total = lax.fori_loop(0, asks.shape[0] // rows_q, part, total)
    loss_o[...] = total / count_q

    query_o[...] = jnp.where(me == 0, unit[...], unit_b[...])
    passage_o[...] = jnp.where(me == 0, unit_b[0:4, :], unit[0:4, :])

    @pl.when(me == 0)
    def _():
        mine, _ = scored(pieces_of(unit[...]), pl.ds(pl.multiple_of(spot * SLOTS, SLOTS), SLOTS))
        grad_unit[...] = dots(pieces_of(mine), passages) / TEMP

    @pl.when(me == 1)
    def _():
        cell = lax.broadcasted_iota(jnp.int32, (SLOTS, wide_p), 1)
        slot = lax.broadcasted_iota(jnp.int32, (SLOTS, wide_p), 0)
        mine = ((cell == slot + spot * 8) & (slot < 4)).astype(BF16)
        weights = dots([mine], pieces_of(dlogits[...]), LANES)
        grad_unit[...] = dots(pieces_of(weights), [asks[...]]) / TEMP

    slot = lax.broadcasted_iota(jnp.int32, (SLOTS, 1), 0)
    units = jnp.where((slot < 4) | (me == 0), unit[...], 0.0)
    grads = grad_unit[...]
    grad_embed = (grads - units * jnp.sum(units * grads, 1, keepdims=True)) * rate_u[:, :1]
    member, length = pooling(bucket, lengths, me)
    grad_out = dots([member], pieces_of(grad_embed / length), ROWS)
    hats = hat[...]
    resid = normed_back(grad_out * row(gain), hats, rate[:, :1])
    grad_o[...] = resid
    low = resid.astype(BF16)
    low_o[...] = low
    sums_o[0:1, :] = jnp.sum(grad_out * hats, 0, keepdims=True)
    sums_o[1:2, :] = jnp.sum(grad_out, 0, keepdims=True)
    sums_o[2:3, :] = jnp.sum(low.astype(F32), 0, keepdims=True)
    sums_o[3:8, :] = jnp.zeros((5, wide), F32)


def contrast(scalars, own, other, offsets, unit, unit_b, rate_u, hat, rate, gain):
    rows, wide = hat.shape
    count = sum(len(o) for o in offsets)
    operands = (*own, *other, unit, unit_b, rate_u, hat, rate, gain)
    outs = (
        shape(1, 1), shape(SLOTS, wide), shape(4, wide), shape(rows, wide),
        shape(rows, wide, kind=BF16), shape(8, wide), shape(8, wide), shape(wide, PAIR),
    )
    queries, passages = count * SLOTS, count * 8
    scratch = [pltpu.VMEM((queries, wide), BF16)] + [
        pltpu.VMEM(dims, F32)
        for dims in (
            (passages, wide), (PAIR, PAIR), (queries, PAIR), (queries, PAIR),
            (queries, passages), (8, wide), (SLOTS, wide),
        )
    ]
    kernel = partial(contrast_kernel, offsets, count)
    kernel.__name__ = "contrast"
    specs = [whole(a) for a in operands]
    return call(
        kernel, scalars, operands, specs, outs, [whole(a) for a in outs],
        1, scratch, flops=2_000_000_000, mib=40 if count <= 16 else 60,
        far=(len(operands) - 3, len(operands) - 1),
    )


def feed_back_kernel(
    where, dffn, gres, wd_a, wd_b, wi_a, wi_b, slope_a, slope_b, hat, rate, gain, hidden_t, means, sums_two,
    into_a_o, into_b_o, grad_o, low_o, vectors_a_o, vectors_b_o,
    total, bias,
):
    step = pl.program_id(0)
    steps = pl.num_programs(0) // 2
    wide = total.shape[1]

    @pl.when(step == 0)
    def _():
        total[...] = gres[...]

    def units(side, step, wd, wi, slope, into_o):
        inner = (dot(dffn[...], wd[...], LANES) * slope[...].astype(F32)).astype(BF16)
        sums = jnp.sum(inner.astype(F32), 0, keepdims=True)
        bias[side : side + 1, pl.ds(pl.multiple_of(step * WIDE, WIDE), WIDE)] = sums
        total[...] += dot(inner, wi[...], LANES)
        into_o[...] = (dot(hidden_t[...], inner) - means[:, 4:5] * sums).astype(BF16)

    @pl.when(step < steps)
    def _():
        units(0, step, wd_a, wi_a, slope_a, into_a_o)

    @pl.when(step >= steps)
    def _():
        units(1, step - steps, wd_b, wi_b, slope_b, into_b_o)

    @pl.when(step == pl.num_programs(0) - 1)
    def _():
        grad = total[...]
        hats = hat[...]
        resid = normed_back(grad * row(gain), hats, rate[:, :1])
        grad_o[...] = resid
        low = resid.astype(BF16)
        low_o[...] = low
        for side, vectors in enumerate((vectors_a_o, vectors_b_o)):
            vectors[...] = jnp.zeros(vectors.shape, F32)
            vectors[0:3, :] = sums_two[0:3, :]
            vectors[3:4, :] = jnp.sum(grad * hats, 0, keepdims=True)
            vectors[4:5, :] = jnp.sum(grad, 0, keepdims=True)
            vectors[5:6, :] = jnp.sum(low.astype(F32), 0, keepdims=True)
            vectors[8:9, :] = bias[side : side + 1, :wide]
            vectors[9:10, :] = bias[side : side + 1, wide:]


def feed_back(where, dffn, gres, wd, wi, slope, hat, rate, gain, hidden_t, means, sums_two):
    rows, wide = dffn.shape
    units = wd[0].shape[0]
    operands = (
        dffn, gres, wd[0], wd[1], wi[0], wi[1], slope[0], slope[1], hat, rate, gain, hidden_t, means, sums_two,
    )
    specs = [whole(a) for a in operands]
    for side in range(2):
        specs[2 + side] = down_rows(wd[side], WIDE, side)
        specs[4 + side] = columns(wi[side], WIDE, side)
        specs[6 + side] = columns(slope[side], WIDE, side)
    into = shape(wide, units, kind=BF16)
    vectors = shape(SLOTS, wide)
    outs = (into, into, shape(rows, wide), shape(rows, wide, kind=BF16), vectors, vectors)
    out_specs = [whole(a) for a in outs]
    for side in range(2):
        out_specs[side] = columns(into, WIDE, side)
    return call(
        feed_back_kernel, (where,), operands, specs, outs, out_specs, 2 * units // WIDE,
        [pltpu.VMEM((rows, wide), F32), pltpu.VMEM((8, units), F32)],
        flops=12 * rows * wide * units, mib=44,
    )


def down_grad(where, act_t, dffn, means):
    units, rows = act_t[0].shape
    wide = dffn[0].shape[1]
    tile = wide // 2

    def half(j, where):
        side = (where[0] >> where[1]) & 1
        return jnp.where(j < 2, 1 - side, side)

    def down_grad_kernel(where, act_a, act_b, dffn_a, dffn_b, means, gone, kept, sums):
        step = pl.program_id(0)

        @pl.when(step == 0)
        def _():
            both = dffn_a[...].astype(F32) + dffn_b[...].astype(F32)
            sums[...] = jnp.broadcast_to(jnp.sum(both, 0, keepdims=True), sums.shape)

        mean = jnp.where(half(step, where) == 0, means[:, 0:1], means[:, 1:2])
        grads = dot(act_a[...], dffn_a[...]) + dot(act_b[...], dffn_b[...])
        grads = (grads - mean * sums[0:1, :]).astype(BF16)

        @pl.when(step < 2)
        def _():
            gone[...] = grads

        @pl.when(step >= 2)
        def _():
            kept[...] = grads

    out = shape(units // 2, wide, kind=BF16)
    act_spec = pl.BlockSpec((tile, rows), lambda j, where: (2 * half(j, where) + j % 2, 0))
    return call(
        down_grad_kernel, (where,), (*act_t, *dffn, means),
        [act_spec, act_spec, whole(dffn[0]), whole(dffn[1]), pl.BlockSpec((tile, PAIR), lambda j, *_: (j % 2, 0))],
        (out, out),
        [
            pl.BlockSpec((tile, wide), lambda j, *_: (jnp.minimum(j, 1), 0)),
            pl.BlockSpec((tile, wide), lambda j, *_: (jnp.maximum(j - 2, 0), 0)),
        ],
        4, [pltpu.VMEM((8, wide), F32)], flops=4 * rows * units * wide, mib=24,
    )


def halved(terms, bit, own):
    return [(array, path + ((bit, own),), half) for array, path, half in terms]


def term(array):
    return array, (), None


def columns_of(terms, half):
    return [(array, path, half) for array, path, _ in terms]


def block_of(path, where):
    index = 0
    for bit, own in path:
        side = (where[0] >> bit(where)) & 1
        index = 2 * index + (side if own else 1 - side)
    return index


def add(terms):
    return "add", terms, None


def join(pieces, bit):
    return "join", [term(t) for t in pieces], bit


def extent(array, path, half):
    return array.shape[0] >> len(path), array.shape[1] >> (half is not None)


def mixed(where, *jobs):
    if any(extent(*job[1][0])[0] % 16 for job in jobs):
        return [plain(where, *job) for job in jobs]
    operands, specs, outs = [], [], []
    for kind, terms, _ in jobs:
        for array, path, half in terms:
            block = extent(array, path, half)
            operands.append(array)
            specs.append(
                pl.BlockSpec(
                    block, lambda j, where, path=path, half=half: (block_of(path, where), half or 0)
                )
            )
        outs.append(shape((2 if kind == "join" else 1) * block[0], block[1], kind=BF16))

    def mixed_kernel(where, *refs):
        sources, targets = refs[: len(operands)], refs[len(operands) :]
        for (kind, terms, bit), target in zip(jobs, targets):
            mine, sources = sources[: len(terms)], sources[len(terms) :]
            if kind == "join":
                rows = mine[0].shape[0]
                side = (where[0] >> bit(where)) & 1
                target[pl.ds(pl.multiple_of(side * rows, 16), rows), :] = mine[0][...]
                target[pl.ds(pl.multiple_of((1 - side) * rows, 16), rows), :] = mine[1][...]
            else:
                total = mine[0][...].astype(F32)
                for other in mine[1:]:
                    total = total + other[...].astype(F32)
                target[...] = total.astype(BF16)

    return call(
        mixed_kernel, (where,), operands, specs, outs, [whole(a) for a in outs], mib=24,
        far=[i for i, a in enumerate(operands) if a.size >= BLOCK * BLOCK * 4],
    )


def plain(where, kind, terms, bit):
    if kind == "join":
        (first, _, _), (second, _, _) = terms
        side = (where[0] >> bit(where)) & 1
        return jnp.where(
            side == 0, jnp.concatenate([first, second], 0), jnp.concatenate([second, first], 0)
        )
    total = 0.0
    for array, path, half in terms:
        rows, columns = extent(array, path, half)
        piece = lax.dynamic_slice_in_dim(array, block_of(path, where) * rows, rows, 0)
        piece = piece[:, (half or 0) * columns : ((half or 0) + 1) * columns]
        total = total + piece.astype(F32)
    return total.astype(BF16)


def finish(where, pieces, means, vectors):
    half, width = pieces[0][0].shape[0], pieces[0][0].shape[1] // 2
    wide = 2 * half

    def finish_kernel(where, first_a, second_a, first_b, second_b, means, vectors, *outs):
        side = (where[0] >> where[1]) & 1
        for place in range(2):
            rows = slice(place * half, (place + 1) * half)
            x_mean = means[rows, 6:7]
            piece = jnp.where(side == place, first_a[...], second_a[...]).astype(F32)
            outs[0][rows, :] = piece[:, :width] + x_mean * vectors[6:7, :width]
            outs[1][rows, :] = piece[:, width:] + x_mean * vectors[6:7, width:]
            piece = jnp.where(side == place, first_b[...], second_b[...]).astype(F32)
            outs[2][rows, :] = piece[:, :width] + x_mean * vectors[7:8, :width]
            columns = slice(place * width, (place + 1) * width)
            outs[3][:, columns] = piece[:, width:] + means[:width, 5:6] * vectors[5:6, columns]

    outs = (shape(wide, width),) * 3 + (shape(width, wide),)
    operands = (*pieces[0], *pieces[1], means, vectors)
    return call(
        finish_kernel, (where,), operands, [whole(a) for a in operands], outs, [whole(a) for a in outs],
        mib=32,
    )


def swap(tensor):
    return lax.ppermute(tensor, "mp", [(0, 1), (1, 0)])


def flip(tensor, bits):
    count = lax.axis_size("dp")
    return lax.ppermute(tensor, "dp", [(i, i ^ bits) for i in range(count)])


def bit_count():
    return lax.axis_size("dp").bit_length() - 1


def seal(*values):
    return lax.optimization_barrier(values)


def plane(step):
    return lambda where: where[1] ^ step


def over(bit):
    return lambda where: bit


def cross(tensor, step):
    count = lax.axis_size("dp")
    pairs = [
        (2 * d + c, 2 * (d ^ (1 << (step ^ c))) + c) for d in range(count) for c in range(2)
    ]
    return lax.ppermute(tensor, ("dp", "mp"), pairs)


def gather_small(tensor, beside):
    bits = list(range(bit_count()))
    groups = []
    while bits:
        groups.append(bits[-2:])
        bits = bits[:-2]
    tensor, offsets = tensor[None], [0]
    for number, group in enumerate(groups):
        ways = range(1 << len(group))
        pieces = [tensor] + [flip(tensor, way << group[0]) for way in ways if way]
        places = [[(way << group[0]) | o for o in offsets] for way in ways]
        if number == 0:
            pieces, beside = seal(pieces, beside)
        if number == len(groups) - 1:
            return pieces, places, beside
        tensor = jnp.concatenate(pieces, 0)
        offsets = [o for part in places for o in part]


def shards(
    tokens_in, proj_query, bias_query, proj_key, proj_value, bias_value, proj_out, bias_out,
    gain_attn, shift_attn, proj_in, bias_in, proj_down, bias_down, gain_ffn, shift_ffn,
    bucket, lengths, positive,
):
    spot, me = lax.axis_index("dp"), lax.axis_index("mp")
    wide = tokens_in.shape[1]
    width = proj_query.shape[1]
    units = proj_in.shape[1]
    where = jnp.stack([spot, me]).astype(jnp.int32)
    scalars = (where, bucket, lengths)
    x = tokens_in

    bi = bias_in, swap(bias_in)
    wo, wi, wd = [(w, swap(w)) for w in (proj_out, proj_in, proj_down)]
    heads = attend(scalars, x, proj_query, bias_query, proj_key, proj_value, bias_value)
    heads, x_t = [h[:5] for h in heads], [h[5] for h in heads]
    ctx = heads[0][3], swap(heads[1][3])
    (hat_one, rate_one, hidden_t, act_t_a, act_t_b, slope_a, slope_b, hat_two, rate_two, unit, packed, rate_u) = feed(
        scalars + (positive,), x, ctx, wo, bias_out, gain_attn, shift_attn, wi, bi, wd,
        bias_down, gain_ffn, shift_ffn,
    )

    own, offsets, (unit_b, act_t_b) = gather_small(packed, [swap(unit), swap(act_t_b)])
    other = [swap(piece) for piece in own]
    act_t = act_t_a, act_t_b

    loss, query_embed, passage_embed, gres_two, dffn, sums_two, common, means = contrast(
        scalars, own, other, offsets, unit, unit_b, rate_u, hat_two, rate_two, gain_ffn
    )

    def outer(mean, sums):
        return mean[:, None] * sums[None, :]

    bits = bit_count()
    rest = list(range(2, bits))

    low, *high = rest

    def kept(terms, bit, other):
        return halved(terms, bit, True) + [term(other)]

    def sent(terms, bit):
        return add(halved(terms, bit, False))

    def hold(*values):
        arrays = seal(*[[t[0] for t in v] if is_sum(v) else v for v in values])
        return [
            [(t, *old[1:]) for t, old in zip(new, v)] if is_sum(v) else new
            for new, v in zip(arrays, values)
        ]

    def is_sum(value):
        return isinstance(value, list) and all(
            isinstance(t, tuple) and len(t) == 3 and isinstance(t[1], tuple) for t in value
        )

    dffns = dffn, swap(dffn)
    gone, own = down_grad(where, act_t, dffns, means)
    gone, own, dffn, common, sums_two = seal(gone, own, dffn, common, sums_two)
    down = [term(own), term(cross(gone, 0))]
    fed = feed_back(
        where, dffn, gres_two, wd, wi, (slope_a, slope_b), hat_one, rate_one, gain_attn, hidden_t,
        means, sums_two,
    )
    down, fed = hold(down, fed)
    into_a, into_b, gres_one, dattn, vectors_a, vectors_b = fed

    (gone,) = mixed(where, sent(down, plane(1)))
    gone, down, dattn, into_b = hold(gone, down, dattn, into_b)
    down = kept(down, plane(1), cross(gone, 1))
    into = [term(into_a), term(swap(into_b))]
    dattn_b = swap(dattn)
    back_a = attend_back(scalars, heads[0], dattn, wo[0])
    down, into, back_a, dattn_b = hold(down, into, back_a, dattn_b)

    gone = mixed(where, sent(into, plane(0)), sent(down, over(low)))
    gone, into, down, dattn_b, back_a = hold(gone, into, down, dattn_b, back_a)
    into = kept(into, plane(0), cross(gone[0], 0))
    down = kept(down, over(low), flip(gone[1], 1 << low))
    extra = (*x_t, heads[0][3], dattn, *back_a, means, vectors_a)
    back_b = attend_back(scalars, heads[1], dattn_b, wo[0], extra)
    into, down, back_b = hold(into, down, back_b)
    attn_gone, attn_kept, vectors_a = back_b[2:4], back_b[4:6], back_b[6]

    token = vectors_a

    def enter(*values):
        return hold(*values, token)[:-1]

    def over_high(tensor, sent):
        for bit in high[1:]:
            (tensor,) = mixed(where, add([term(tensor), term(sent)]))
            sent = flip(tensor, 1 << bit)
        return [term(tensor), term(sent)]

    def to_high(tensor):
        return tensor, flip(tensor, 1 << high[0])

    downs = [columns_of(down, half) for half in range(2)]
    intos = [columns_of(into, half) for half in range(2)]
    attns = [None, None]
    for h in range(2):
        downs[h], intos[h] = enter(downs[h], intos[h])
        downs[h], token = mixed(where, add(downs[h]), sent(intos[h], plane(1)))
        downs[h] = to_high(downs[h])
        intos[h] = kept(intos[h], plane(1), cross(token, 1))
    small = [vectors_a, swap(vectors_b)]
    for h in range(2):
        downs[h], intos[h] = enter(downs[h], intos[h])
        downs[h], token = mixed(where, add(over_high(*downs[h])), sent(intos[h], over(low)))
        attns[h] = [term(attn_kept[h]), term(cross(attn_gone[h], 0))]
        intos[h] = kept(intos[h], over(low), flip(token, 1 << low))
        downs[h] = [downs[h], flip(downs[h], 1 << low)]
    for h in range(2):
        attns[h], downs[h], intos[h] = enter(attns[h], downs[h], intos[h])
        token, downs[h], intos[h] = mixed(
            where, sent(attns[h], plane(1)), join(downs[h], over(low)), add(intos[h])
        )
        attns[h] = kept(attns[h], plane(1), cross(token, 1))
        downs[h] = [downs[h], cross(downs[h], 1)]
        intos[h] = to_high(intos[h])
    (small,) = enter(small)
    token = small = small[0] + small[1]
    small = [small, flip(small, 1)]
    for h in range(2):
        downs[h], attns[h], intos[h] = enter(downs[h], attns[h], intos[h])
        downs[h], token, intos[h] = mixed(
            where, join(downs[h], plane(1)), sent(attns[h], over(low)), add(over_high(*intos[h]))
        )
        downs[h] = [downs[h], cross(downs[h], 0)]
        attns[h] = kept(attns[h], over(low), flip(token, 1 << low))
        intos[h] = [intos[h], flip(intos[h], 1 << low)]
    (small,) = enter(small)
    token = small = small[0] + small[1]
    small = [small, flip(small, 2)]
    for h in range(2):
        intos[h], attns[h], downs[h] = enter(intos[h], attns[h], downs[h])
        intos[h], token = mixed(where, join(intos[h], over(low)), add(attns[h]))
        intos[h] = [intos[h], cross(intos[h], 1)]
        attns[h] = to_high(token)
    (small,) = enter(small)
    token = small = small[0] + small[1]
    small = [small, flip(small, 1 << low)]
    for h in range(2):
        intos[h], attns[h] = enter(intos[h], attns[h])
        intos[h], token = mixed(where, join(intos[h], plane(1)), add(over_high(*attns[h])))
        intos[h] = [intos[h], cross(intos[h], 0)]
        attns[h] = [token, flip(token, 1 << low)]
    for bit in high:
        (small,) = enter(small)
        token = small = small[0] + small[1]
        small = [small, flip(small, 1 << bit)]
    (gres_one,) = enter(gres_one)
    token = grad_in = input_grad(
        where, gres_one, (back_a[:2], back_b[:2]), (proj_query, proj_key, proj_value)
    )
    for h in range(2):
        (attns[h],) = enter(attns[h])
        (token,) = mixed(where, join(attns[h], over(low)))
        attns[h] = [token, cross(token, 1)]
    small, downs, common = enter(small, downs, common)
    small = small[0] + small[1]
    share = lax.dynamic_slice_in_dim(small[0:6], me * width, width, 1)
    d_g2, d_s2, d_bd, d_g1, d_s1, d_bo = [share[i] for i in range(6)]
    own_half = small[6:].reshape(-1)
    d_bq, d_bv = own_half[:width], own_half[2 * width : 3 * width]
    d_bi = small[8:10].reshape(units)
    act_mean, hidden_mean = common[0:2].reshape(units), common[4]
    downs = [plain(where, *join(down, plane(0))) for down in downs]
    token = grad_down = jnp.concatenate(downs, 1).astype(F32) + outer(act_mean, small[2])
    for h in range(2):
        attns[h], intos[h] = enter(attns[h], intos[h])
        (token,) = mixed(where, join(attns[h], plane(1)))
        attns[h] = [token, cross(token, 0)]
    intos, hidden_mean, d_bi, grad_in = enter(intos, hidden_mean, d_bi, grad_in)
    intos = [plain(where, *join(into, plane(0))) for into in intos]
    grad_into = jnp.concatenate(intos, 1).astype(F32) + outer(hidden_mean, d_bi)
    grad_in = (grad_in[0] + swap(grad_in[1]).astype(F32)).astype(BF16)
    other_in = swap(grad_in)
    grad_input = jnp.where(
        me == 0,
        jnp.concatenate([grad_in, other_in], 0),
        jnp.concatenate([other_in, grad_in], 0),
    )
    attns, grad_down, grad_into, grad_input = seal(attns, grad_down, grad_into, grad_input)
    grad_q, grad_k, grad_v, grad_o = finish(where, attns, means, small)
    return (
        loss[0, 0],
        query_embed,
        passage_embed,
        grad_input,
        grad_q,
        d_bq,
        grad_k,
        grad_v,
        d_bv,
        grad_o,
        d_bo,
        d_g1,
        d_s1,
        grad_into,
        d_bi,
        grad_down,
        d_bd,
        d_g2,
        d_s2,
    )


def solution(mesh):
    half, rows = P(None, "mp"), P("mp", None)
    return jax.shard_map(
        shards,
        mesh=mesh,
        in_specs=(
            P("dp", None), half, P("mp"), half, half, P("mp"), rows, P(), P(), P(),
            half, P("mp"), rows, P(), P(), P(), P("dp"), P("dp", None), P("dp"),
        ),
        out_specs=(
            P(), P("dp", None), P("dp", None), P("dp", None),
            half, P("mp"), half, half, P("mp"), rows, P("mp"), P("mp"), P("mp"),
            half, P("mp"), rows, P("mp"), P("mp"), P("mp"),
        ),
        check_vma=False,
    )
```

```python
from functools import partial

import jax
import jax.numpy as jnp
from jax import lax
from jax.experimental import pallas as pl
from jax.experimental.pallas import tpu as pltpu
from jax.sharding import PartitionSpec as P

HEAD_DIM = 64
BLOCK = 512
PAIR = 2 * HEAD_DIM
CHUNK = 128
SLOTS = 16
EPS = 1e-05
TEMP = 0.01
MASKED = -10000.0
HIGH = lax.Precision.HIGHEST
F32 = jnp.float32
BF16 = jnp.bfloat16
VMEM = pl.BlockSpec(memory_space=pltpu.VMEM)
SMEM = pl.BlockSpec(memory_space=pltpu.SMEM)


def dot(a, b, dims=((1,), (0,)), precision=None):
    return lax.dot_general(a, b, (dims, ((), ())), precision=precision, preferred_element_type=F32)


ROWS = ((0,), (0,))
LANES = ((1,), (1,))


def pieces_of(x, count=3):
    pieces = []
    for _ in range(count):
        pieces.append(x.astype(BF16))
        x = x - pieces[-1].astype(F32)
    return pieces


def dots(a, b, dims=((1,), (0,))):
    total = 0.0
    for i, x in enumerate(a):
        for j, y in enumerate(b):
            if i + j < 3:
                total = total + dot(x, y, dims)
    return total


def params(mib):
    return pltpu.CompilerParams(vmem_limit_bytes=mib * 1024 * 1024)


def row(ref):
    return ref[...].reshape(1, ref.shape[0])


def shape(*dims, kind=F32):
    return jax.ShapeDtypeStruct(dims, kind)


def lane_masks(kind):
    first = (lax.broadcasted_iota(jnp.int32, (1, PAIR), 1) < HEAD_DIM).astype(F32)
    return first.astype(kind), (1.0 - first).astype(kind)


def layout(bucket, lengths, me, axis):
    code = bucket[me]
    dims = (BLOCK, 1) if axis == 0 else (1, BLOCK)
    places = lax.broadcasted_iota(jnp.int32, dims, axis)
    shift = jnp.full(dims, jnp.where(code == 3, 9, 5 + code), jnp.int32)
    slot = lax.shift_right_logical(places, shift)
    offset = places - lax.shift_left(slot, shift)
    length = jnp.zeros(dims, jnp.int32)
    for s in range(SLOTS):
        length = jnp.where(slot == s, lengths[me, s], length)
    return slot, jnp.where(offset < length, slot, -1)


def pooling(bucket, lengths, me):
    _, kid = layout(bucket, lengths, me, 1)
    slots = lax.broadcasted_iota(jnp.int32, (SLOTS, BLOCK), 0)
    rows = lax.broadcasted_iota(jnp.int32, (SLOTS, 1), 0)
    length = jnp.zeros((SLOTS, 1), jnp.int32)
    for s in range(SLOTS):
        length = jnp.where(rows == s, lengths[me, s], length)
    return (slots == kid).astype(BF16), jnp.maximum(length, 1).astype(F32)


def attend_kernel(
    where, bucket, lengths,
    x, wq, bq, wk, wv, bv,
    q_a, q_b, k_a, k_b, v_a, v_b, ctx_a, ctx_b, lse_a, lse_b, x_t_a, x_t_b,
):
    width = wq.shape[1]
    first, second = lane_masks(BF16)
    low = lax.broadcasted_iota(jnp.int32, (CHUNK, PAIR), 1) < HEAD_DIM
    lane = lax.broadcasted_iota(jnp.int32, (CHUNK, PAIR), 1)
    ones = jnp.ones((BLOCK, PAIR), BF16)
    for me, q_o, k_o, v_o, ctx_o, lse_o, x_t in (
        (1 - where[1], q_b, k_b, v_b, ctx_b, lse_b, x_t_b),
        (where[1], q_a, k_a, v_a, ctx_a, lse_a, x_t_a),
    ):
        tokens = x[pl.ds(pl.multiple_of(me * BLOCK, BLOCK), BLOCK), :]
        x_t[...] = jnp.transpose(tokens)
        slot_col, _ = layout(bucket, lengths, me, 0)
        _, kid_row = layout(bucket, lengths, me, 1)
        q_o[...] = (dot(tokens, wq[...]) + row(bq)).astype(BF16)
        k_o[...] = dot(tokens, wk[...]).astype(BF16)
        v_o[...] = (dot(tokens, wv[...]) + row(bv)).astype(BF16)
        for r in range(BLOCK // CHUNK):
            rows = slice(r * CHUNK, (r + 1) * CHUNK)
            mask = slot_col[rows, :] == kid_row
            mask = jnp.concatenate([mask, mask], 0)
            levels = jnp.zeros((CHUNK, PAIR), F32)
            for pair in range(width // PAIR):
                cols = slice(pair * PAIR, (pair + 1) * PAIR)
                query = q_o[rows, cols] * jnp.asarray(HEAD_DIM**-0.5, BF16)
                both = jnp.concatenate([query * first, query * second], 0)
                scores = jnp.where(mask, dot(both, k_o[:, cols], LANES), MASKED)
                summit = jnp.max(scores, 1, keepdims=True)
                raised = jnp.exp(scores - summit).astype(BF16)
                out = dot(raised, jnp.concatenate([v_o[:, cols], ones], 1))
                mass = out[:, PAIR:]
                out = out[:, :PAIR] / mass
                ctx_o[rows, cols] = jnp.where(low, out[:CHUNK], out[CHUNK:]).astype(BF16)
                logs = jnp.log(mass) + summit
                levels = jnp.where(lane == 2 * pair, logs[:CHUNK], levels)
                levels = jnp.where(lane == 2 * pair + 1, logs[CHUNK:], levels)
            lse_o[rows, :] = levels


def whole(a):
    return pl.BlockSpec(a.shape, lambda j, *_: (0,) * len(a.shape))


def block_rows(a):
    return pl.BlockSpec((BLOCK, a.shape[1]), lambda j, where, *_: (where[1], 0))


def turn_of(side, steps):
    if side is None:
        return lambda j: j
    if side == 0:
        return lambda j: jnp.minimum(j, steps - 1)
    return lambda j: jnp.maximum(j - steps, 0)


def columns(a, tile, side=None):
    at = turn_of(side, a.shape[1] // tile)
    return pl.BlockSpec((a.shape[0], tile), lambda j, *_: (0, at(j)))


def down_rows(a, tile, side=None):
    at = turn_of(side, a.shape[0] // tile)
    return pl.BlockSpec((tile, a.shape[1]), lambda j, *_: (at(j), 0))


def call(
    kernel, scalars, operands, in_specs, outs, out_specs, steps=1, scratch=(), flops=0, mib=60, far=()
):
    operands = [
        pltpu.with_memory_space_constraint(a, pltpu.HBM) if i in far else a
        for i, a in enumerate(operands)
    ]
    moved = sum(a.size * a.dtype.itemsize for a in list(operands) + list(outs))
    return pl.pallas_call(
        kernel,
        grid_spec=pltpu.PrefetchScalarGridSpec(
            num_scalar_prefetch=len(scalars),
            grid=(steps,),
            in_specs=in_specs,
            out_specs=tuple(out_specs),
            scratch_shapes=list(scratch),
        ),
        out_shape=tuple(outs),
        compiler_params=params(mib),
        cost_estimate=pl.CostEstimate(flops=flops, bytes_accessed=moved, transcendentals=0),
        name=kernel.__name__,
    )(*scalars, *operands)


def attend(scalars, x, wq, bq, wk, wv, bv):
    wide, width = wq.shape
    low, level = shape(BLOCK, width, kind=BF16), shape(BLOCK, PAIR)
    turned = shape(wide, BLOCK, kind=BF16)
    outs = (low,) * 8 + (level,) * 2 + (turned,) * 2
    operands = (x, wq, bq, wk, wv, bv)
    flops = 4 * BLOCK * width * (3 * wide + 4 * BLOCK)
    outs = call(
        attend_kernel, scalars, operands, [whole(a) for a in operands],
        outs, [whole(a) for a in outs], flops=flops,
    )
    return outs[0::2], outs[1::2]


def attend_back_block(
    me, bucket, lengths, q, k, v, ctx, lse, dattn, wo, dqk_o, dv_o, sums_o, dscore_s
):
    width = q.shape[1]
    first, second = lane_masks(BF16)
    scale = jnp.asarray(HEAD_DIM**-0.5, BF16)
    dctx = dot(dattn[...], wo[...], LANES).astype(BF16)
    head_of = lax.broadcasted_iota(jnp.int32, (width, PAIR), 0) >> 6
    select = (head_of == lax.broadcasted_iota(jnp.int32, (width, PAIR), 1)).astype(F32)
    inner_sums = dot(select, dctx.astype(F32) * ctx[...].astype(F32), ((0,), (1,)), HIGH)
    levels = jnp.transpose(lse[...])
    slots, _ = layout(bucket, lengths, me, 1)
    _, kid_col = layout(bucket, lengths, me, 0)
    sums_o[...] = jnp.zeros(sums_o.shape, F32)
    low = lax.broadcasted_iota(jnp.int32, (TILE, PAIR), 1) < HEAD_DIM
    for pair in range(width // PAIR):
        cols = slice(pair * PAIR, (pair + 1) * PAIR)
        query = q[:, cols] * scale
        grad = dctx[:, cols]
        sum_k = jnp.zeros((1, PAIR), F32)
        sum_v = jnp.zeros((1, PAIR), F32)
        for c in range(BLOCK // TILE):
            rows = slice(c * TILE, (c + 1) * TILE)
            mask = kid_col[rows, :] == slots
            key_part, value_part = k[rows, cols], v[rows, cols]
            keys = jnp.concatenate([key_part * first, key_part * second], 0)
            values = jnp.concatenate([value_part * first, value_part * second], 0)
            scores, dprobs = dot(keys, query, LANES), dot(values, grad, LANES)
            probs, dscores = [], []
            for e in range(2):
                head, at = 2 * pair + e, slice(e * TILE, (e + 1) * TILE)
                prob = jnp.exp(jnp.where(mask, scores[at], MASKED) - levels[head : head + 1, :])
                dscore = (prob * (dprobs[at] - inner_sums[head : head + 1, :])).astype(BF16)
                dscore_s[e, rows, :] = dscore
                probs.append(prob.astype(BF16))
                dscores.append(dscore)
            dk = dot(jnp.concatenate(dscores, 0), query)
            dv = dot(jnp.concatenate(probs, 0), grad)
            dk = jnp.where(low, dk[:TILE], dk[TILE:]).astype(BF16)
            dv = jnp.where(low, dv[:TILE], dv[TILE:]).astype(BF16)
            dqk_o[rows, width + pair * PAIR : width + (pair + 1) * PAIR] = dk
            dv_o[rows, cols] = dv
            sum_k = sum_k + jnp.sum(dk.astype(F32), 0, keepdims=True)
            sum_v = sum_v + jnp.sum(dv.astype(F32), 0, keepdims=True)
        keys = jnp.transpose(k[:, cols])
        dq = [dot(keys[:HEAD_DIM], dscore_s[0]), dot(keys[HEAD_DIM:], dscore_s[1])]
        dq = (jnp.transpose(jnp.concatenate(dq, 0)) * HEAD_DIM**-0.5).astype(BF16)
        dqk_o[:, cols] = dq
        sums_o[0:1, cols] = jnp.sum(dq.astype(F32), 0, keepdims=True)
        sums_o[1:2, cols] = sum_k
        sums_o[2:3, cols] = sum_v


def own_back_kernel(
    where, bucket, lengths, q, k, v, ctx, lse, dattn, wo, dqk_o, dv_o, sums_o, dscore_s
):
    attend_back_block(
        where[1], bucket, lengths, q, k, v, ctx, lse, dattn, wo, dqk_o, dv_o, sums_o, dscore_s
    )


def other_back_kernel(
    where, bucket, lengths, q, k, v, ctx, lse, dattn, wo,
    x_t_a, x_t_b, ctx_a, dattn_a, dqk_a, dv_a, sums_a, means, vectors,
    dqk_o, dv_o, gone_a_o, gone_b_o, kept_a_o, kept_b_o, vectors_o,
    dscore_s, sums_o,
):
    attend_back_block(
        1 - where[1], bucket, lengths, q, k, v, ctx, lse, dattn, wo, dqk_o, dv_o, sums_o, dscore_s
    )
    width = q.shape[1]
    sums = sums_o[...] + sums_a[...]
    vectors_o[...] = vectors[...]
    vectors_o[6:7, :width] = sums[0:1, :]
    vectors_o[6:7, width:] = sums[1:2, :]
    vectors_o[7:8, :width] = sums[2:3, :]
    bias_out = vectors[5:6, :] + jnp.sum(dattn[...].astype(F32), 0, keepdims=True)
    turned_a, turned_b = jnp.transpose(ctx_a[...]), jnp.transpose(ctx[...])
    side = (where[0] >> where[1]) & 1
    for half, first, second in ((1 - side, gone_a_o, gone_b_o), (side, kept_a_o, kept_b_o)):
        rows = pl.ds(pl.multiple_of(half * width, width), width)
        rows_a, rows_b = x_t_a[rows, :], x_t_b[rows, :]
        x_mean = means[rows, :][:, 6:7]
        for i, (source_a, source_b, at) in enumerate(
            ((dqk_a, dqk_o, 0), (dqk_a, dqk_o, width), (dv_a, dv_o, 0))
        ):
            grads = dot(rows_a, source_a[:, at : at + width])
            grads = grads + dot(rows_b, source_b[:, at : at + width]) - x_mean * sums[i : i + 1, :]
            out = (first, first, second)[i]
            out[:, at : at + width] = grads.astype(BF16)
        grads = dot(turned_a, dattn_a[:, rows]) + dot(turned_b, dattn[:, rows])
        sums_here = jnp.where(half == 0, bias_out[:, :width], bias_out[:, width:])
        grads = grads - means[:width, 5:6] * sums_here
        second[:, width:] = grads.astype(BF16)


def attend_back(scalars, heads, dattn, wo, extra=None):
    rows, width = heads[0].shape
    wide = dattn.shape[1]
    outs = [shape(rows, 2 * width, kind=BF16), shape(rows, width, kind=BF16)]
    operands = (*heads, dattn, wo)
    scratch = [pltpu.VMEM((2, rows, rows), BF16)]
    if extra is None:
        kernel = own_back_kernel
        outs += [shape(8, width)]
    else:
        kernel = other_back_kernel
        operands += extra
        outs += [shape(wide // 2, 2 * width, kind=BF16)] * 4 + [shape(SLOTS, wide)]
        scratch += [pltpu.VMEM((8, width), F32)]
    return call(
        kernel, scalars, operands, [whole(a) for a in operands],
        outs, [whole(a) for a in outs], 1, scratch, flops=24 * rows * rows * width,
    )


def input_grad(where, gres, backs, weights):
    rows, wide = gres.shape
    width = weights[0].shape[1]

    def input_grad_kernel(where, gres, dqk_a, dv_a, dqk_b, dv_b, wq, wk, wv, own_o, other_o):
        for dqk, dv, out in ((dqk_a, dv_a, own_o), (dqk_b, dv_b, other_o)):
            parts = dot(dqk[:, :width], wq[...], LANES) + dot(dqk[:, width:], wk[...], LANES)
            parts = parts + dot(dv[...], wv[...], LANES)
            out[...] = parts + gres[...] if out is own_o else parts.astype(BF16)

    operands = (gres, *backs[0], *backs[1], *weights)
    outs = shape(rows, wide), shape(rows, wide, kind=BF16)
    return call(
        input_grad_kernel, (where,), operands, [whole(a) for a in operands],
        outs, [whole(a) for a in outs], flops=12 * rows * wide * width, mib=28, far=range(8),
    )


def normed(resid):
    center = resid - jnp.mean(resid, -1, keepdims=True)
    rate = lax.rsqrt(jnp.mean(center * center, -1, keepdims=True) + EPS)
    return center * rate, rate


def normed_back(grad, hat, rate):
    return (
        grad - jnp.mean(grad, -1, keepdims=True) - hat * jnp.mean(grad * hat, -1, keepdims=True)
    ) * rate


def feed_kernel(
    where, bucket, lengths, positive,
    x, ctx_a, ctx_b, wo_a, wo_b, bias_out, gain_one, shift_one,
    wi_a, wi_b, bi_a, bi_b, wd_a, wd_b, bias_down, gain_two, shift_two,
    hat_one_o, rate_one_o, hidden_t_o, act_t_a_o, act_t_b_o, slope_a_o, slope_b_o, hat_two_o, rate_two_o,
    unit_o, packed_o, rate_u_o,
    total, sums, act_sums, hidden_o, packing,
):
    step = pl.program_id(0)
    me = where[1]
    wide = total.shape[1]

    @pl.when(step == 0)
    def _():
        tokens = x[...].astype(F32)
        attn = dot(ctx_a[...], wo_a[...]) + dot(ctx_b[...], wo_b[...]) + row(bias_out)
        hat, rate = normed(tokens + attn)
        hidden = hat * row(gain_one) + row(shift_one)
        hat_one_o[...] = hat
        rate_one_o[...] = jnp.broadcast_to(rate, rate_one_o.shape)
        hidden_low = hidden.astype(BF16)
        hidden_o[...] = hidden_low
        hidden_t_o[...] = jnp.transpose(hidden_low)
        total[...] = hidden + row(bias_down)
        sums[...] = jnp.zeros(sums.shape, F32)
        act_sums[...] = jnp.zeros(act_sums.shape, F32)
        sums[0:1, :] = jnp.sum(hidden, 0, keepdims=True)
        half = ctx_a.shape[1]
        sums[1:2, :half] = jnp.sum(ctx_a[...].astype(F32), 0, keepdims=True)
        sums[1:2, half:] = jnp.sum(ctx_b[...].astype(F32), 0, keepdims=True)
        sums[2:3, :] = jnp.sum(tokens, 0, keepdims=True)

    place = pl.ds(pl.multiple_of(step * WIDE, WIDE), WIDE)

    def chunk(c, carry):
        rows = pl.ds(pl.multiple_of(c * ROWS_AT_ONCE, ROWS_AT_ONCE), ROWS_AT_ONCE)
        hidden = hidden_o[rows, :]
        added = []
        for side, (wi, bi, wd, act_o, slope_o) in enumerate((
            (wi_a, bi_a, wd_a, act_t_a_o, slope_a_o),
            (wi_b, bi_b, wd_b, act_t_b_o, slope_b_o),
        )):
            inner = dot(hidden, wi[...]) + row(bi)
            below = 0.5 + 0.5 * lax.erf(inner * (0.5**0.5))
            bell = jnp.exp(inner * inner * -0.5) * 0.3989422804014327
            act = inner * below
            act_sums[side : side + 1, place] += jnp.sum(act, 0, keepdims=True)
            act = act.astype(BF16)
            act_o[:, rows] = jnp.transpose(act)
            slope_o[rows, :] = (below + inner * bell).astype(BF16)
            added.append(dot(act, wd[...]))
        total[rows, :] += added[0] + added[1]
        return carry

    lax.fori_loop(0, BLOCK // ROWS_AT_ONCE, chunk, 0)

    @pl.when(step == pl.num_programs(0) - 1)
    def _():
        hat, rate = normed(total[...])
        hat_two_o[...] = hat
        rate_two_o[...] = jnp.broadcast_to(rate, rate_two_o.shape)
        output = hat * row(gain_two) + row(shift_two)
        member, length = pooling(bucket, lengths, me)
        raw = dots([member], pieces_of(output)) / length
        rate_u = lax.rsqrt(jnp.sum(raw * raw, 1, keepdims=True) + 1e-06)
        rate_u_o[...] = jnp.broadcast_to(rate_u, rate_u_o.shape)
        unit = raw * rate_u
        unit_o[...] = unit
        packing[...] = unit

        @pl.when(me == 1)
        def _():
            packing[4:8, :] = unit[0:4] - unit[0:4].astype(BF16).astype(F32)
            lane = lax.broadcasted_iota(jnp.int32, (1, wide), 1)
            extra = jnp.zeros((1, wide), jnp.int32)
            for s in range(SLOTS):
                extra = jnp.where(lane == s, positive[s] & 255, extra)
                extra = jnp.where(lane == 2 * SLOTS + s, positive[s] >> 8, extra)
            for s in range(2):
                extra = jnp.where(lane == 4 * SLOTS + s, bucket[s], extra)
            packing[8:9, :] = extra.astype(F32)
            packing[9:10, :] = act_sums[0:1, :wide]
            packing[10:11, :] = act_sums[0:1, wide:]
            packing[11:12, :] = act_sums[1:2, :wide]
            packing[12:13, :] = act_sums[1:2, wide:]
            packing[13:16, :] = sums[0:3, :]

        packed_o[...] = packing[...].astype(BF16)


TILE = 256
WIDE = 512
ROWS_AT_ONCE = 256


def feed(scalars, x, ctx, wo, bias_out, gain_one, shift_one, wi, bi, wd, bias_down, gain_two, shift_two):
    rows, wide = BLOCK, x.shape[1]
    units = wi[0].shape[1]
    full = shape(rows, wide)
    rate = shape(rows, PAIR)
    low = shape(rows, units, kind=BF16)
    turned = shape(units, rows, kind=BF16)
    hidden = shape(wide, rows, kind=BF16)
    operands = (
        x, ctx[0], ctx[1], wo[0], wo[1], bias_out, gain_one, shift_one,
        wi[0], wi[1], bi[0], bi[1], wd[0], wd[1], bias_down, gain_two, shift_two,
    )
    specs = [block_rows(x)] + [whole(a) for a in operands[1:]]
    for side in range(2):
        specs[8 + side] = columns(wi[side], WIDE)
        specs[10 + side] = pl.BlockSpec((WIDE,), lambda j, *_: (j,))
        specs[12 + side] = down_rows(wd[side], WIDE)
    outs = (
        full, rate, hidden, turned, turned, low, low, full, rate,
        shape(SLOTS, wide), shape(SLOTS, wide, kind=BF16), shape(SLOTS, PAIR),
    )
    out_specs = [whole(a) for a in outs]
    for place in (3, 4):
        out_specs[place] = down_rows(outs[place], WIDE)
    for place in (5, 6):
        out_specs[place] = columns(outs[place], WIDE)
    scratch = [
        pltpu.VMEM((rows, wide), F32), pltpu.VMEM((8, wide), F32), pltpu.VMEM((8, units), F32),
        pltpu.VMEM((rows, wide), BF16), pltpu.VMEM((SLOTS, wide), F32),
    ]
    return call(
        feed_kernel, scalars, operands, specs, outs, out_specs, units // WIDE, scratch,
        mib=48, far=[i for i in range(17) if i not in (2, 4, 9, 13)],
        flops=2 * rows * wide * (wide + 4 * units),
    )


def contrast_kernel(offsets, count, where, bucket, lengths, *refs):
    pieces = len(offsets)
    own, other = refs[:pieces], refs[pieces : 2 * pieces]
    unit, unit_b, rate_u, hat, rate, gain = refs[2 * pieces : 2 * pieces + 6]
    loss_o, query_o, passage_o, grad_o, low_o, sums_o, common_o, columns_o = refs[2 * pieces + 6 : 2 * pieces + 14]
    asks, table, notes, place_col, live_col, dlogits, common, grad_unit = refs[2 * pieces + 14 :]
    spot, me = where[0], where[1]
    wide = hat.shape[1]
    common[...] = jnp.zeros(common.shape, F32)
    notes[...] = jnp.zeros(notes.shape, F32)

    def spread(query_pieces, passage_pieces):
        for piece, places in zip(query_pieces, offsets):
            for i, offset in enumerate(places):
                source = spot ^ offset
                asks[pl.ds(pl.multiple_of(source * SLOTS, SLOTS), SLOTS), :] = piece[i]
        for piece, places in zip(passage_pieces, offsets):
            for i, offset in enumerate(places):
                source = spot ^ offset
                rows = piece[i].astype(F32)
                four = rows[0:4] + rows[4:8]
                four = jnp.concatenate([four, jnp.zeros_like(four)], 0)
                table[pl.ds(pl.multiple_of(source * 8, 8), 8), :] = four
                notes[pl.ds(source, 1), :] = rows[8:9, :PAIR]
                common[...] += rows[8:16]

    @pl.when(me == 0)
    def _():
        spread(own, other)

    @pl.when(me == 1)
    def _():
        spread(other, own)

    share = 1.0 / (count * BLOCK)
    first, second = common[1:3, :] * share, common[3:5, :] * share
    common_o[0:2, :] = jnp.where(me == 1, first, second)
    common_o[2:4, :] = jnp.where(me == 1, second, first)
    common_o[4:7, :] = common[5:8, :] * share
    common_o[7:8, :] = jnp.zeros((1, wide), F32)
    half = wide // 2

    @pl.when(me == 0)
    def _():
        common_o[5:6, :half] = common[6:7, half:] * share
        common_o[5:6, half:] = common[6:7, :half] * share

    padding = jnp.zeros((PAIR - 8, wide), F32)
    columns_o[...] = jnp.transpose(jnp.concatenate([common_o[...], padding], 0))

    turned = jnp.transpose(notes[...])
    slots = lax.broadcasted_iota(jnp.int32, (SLOTS, 1), 0).astype(F32)
    for d in range(count):
        at = slice(d * SLOTS, (d + 1) * SLOTS)
        place = turned[0:SLOTS, d : d + 1] + 256.0 * turned[2 * SLOTS : 3 * SLOTS, d : d + 1]
        place_col[at, :] = jnp.broadcast_to(place, (SLOTS, PAIR))
        held = jnp.where(turned[4 * SLOTS : 4 * SLOTS + 1, d : d + 1] == 0.0, 16.0, 8.0)
        live_col[at, :] = jnp.broadcast_to((slots < held).astype(F32), (SLOTS, PAIR))
    wide_p = table.shape[0]
    cells = lax.broadcasted_iota(jnp.int32, (PAIR, wide_p), 1)
    sources = lax.broadcasted_iota(jnp.int32, (PAIR, wide_p), 0)
    held = jnp.where(notes[:, 4 * SLOTS + 1 : 4 * SLOTS + 2] == 2.0, 4, 1)
    live_p = ((cells >> 3) == sources) & ((cells & 7) < held)
    live_p = jnp.sum(live_p.astype(F32), 0, keepdims=True)

    count_q = jnp.sum(live_col[:, :1], 0, keepdims=True)
    rows_q = min(asks.shape[0], BLOCK // 2)

    passages = pieces_of(table[...], 2)

    def scored(asking, at):
        alive = live_col[at, :][:, :1]
        places = place_col[at, :][:, :1].astype(jnp.int32)
        places = (places >> 2) * 8 + (places & 3)
        logits = dots(asking, passages, LANES) / TEMP
        logits = jnp.where(live_p > 0, logits, MASKED)
        summit = jnp.max(logits, 1, keepdims=True)
        raised = jnp.exp(logits - summit)
        mass = jnp.sum(raised, 1, keepdims=True)
        normal = summit + jnp.log(mass)
        target = lax.broadcasted_iota(jnp.int32, logits.shape, 1) == places
        picked = jnp.sum(jnp.where(target, logits, 0.0), 1, keepdims=True)
        grads = (jnp.exp(logits - normal) - target.astype(F32)) * (alive / count_q)
        return grads, jnp.sum(alive * (normal - picked), 0, keepdims=True)

    def part(i, total):
        at = pl.ds(pl.multiple_of(i * rows_q, rows_q), rows_q)
        dlogits[at, :], loss = scored([asks[at, :]], at)
        return total + loss

    total = jnp.zeros((1, 1), F32)
    if asks.shape[0] == rows_q:
        total = part(0, total)
    else:
        total = lax.fori_loop(0, asks.shape[0] // rows_q, part, total)
    loss_o[...] = total / count_q

    query_o[...] = jnp.where(me == 0, unit[...], unit_b[...])
    passage_o[...] = jnp.where(me == 0, unit_b[0:4, :], unit[0:4, :])

    @pl.when(me == 0)
    def _():
        mine, _ = scored(pieces_of(unit[...]), pl.ds(pl.multiple_of(spot * SLOTS, SLOTS), SLOTS))
        grad_unit[...] = dots(pieces_of(mine), passages) / TEMP

    @pl.when(me == 1)
    def _():
        cell = lax.broadcasted_iota(jnp.int32, (SLOTS, wide_p), 1)
        slot = lax.broadcasted_iota(jnp.int32, (SLOTS, wide_p), 0)
        mine = ((cell == slot + spot * 8) & (slot < 4)).astype(BF16)
        weights = dots([mine], pieces_of(dlogits[...]), LANES)
        grad_unit[...] = dots(pieces_of(weights), [asks[...]]) / TEMP

    slot = lax.broadcasted_iota(jnp.int32, (SLOTS, 1), 0)
    units = jnp.where((slot < 4) | (me == 0), unit[...], 0.0)
    grads = grad_unit[...]
    grad_embed = (grads - units * jnp.sum(units * grads, 1, keepdims=True)) * rate_u[:, :1]
    member, length = pooling(bucket, lengths, me)
    grad_out = dots([member], pieces_of(grad_embed / length), ROWS)
    hats = hat[...]
    resid = normed_back(grad_out * row(gain), hats, rate[:, :1])
    grad_o[...] = resid
    low = resid.astype(BF16)
    low_o[...] = low
    sums_o[0:1, :] = jnp.sum(grad_out * hats, 0, keepdims=True)
    sums_o[1:2, :] = jnp.sum(grad_out, 0, keepdims=True)
    sums_o[2:3, :] = jnp.sum(low.astype(F32), 0, keepdims=True)
    sums_o[3:8, :] = jnp.zeros((5, wide), F32)


def contrast(scalars, own, other, offsets, unit, unit_b, rate_u, hat, rate, gain):
    rows, wide = hat.shape
    count = sum(len(o) for o in offsets)
    operands = (*own, *other, unit, unit_b, rate_u, hat, rate, gain)
    outs = (
        shape(1, 1), shape(SLOTS, wide), shape(4, wide), shape(rows, wide),
        shape(rows, wide, kind=BF16), shape(8, wide), shape(8, wide), shape(wide, PAIR),
    )
    queries, passages = count * SLOTS, count * 8
    scratch = [pltpu.VMEM((queries, wide), BF16)] + [
        pltpu.VMEM(dims, F32)
        for dims in (
            (passages, wide), (PAIR, PAIR), (queries, PAIR), (queries, PAIR),
            (queries, passages), (8, wide), (SLOTS, wide),
        )
    ]
    kernel = partial(contrast_kernel, offsets, count)
    kernel.__name__ = "contrast"
    specs = [whole(a) for a in operands]
    return call(
        kernel, scalars, operands, specs, outs, [whole(a) for a in outs],
        1, scratch, flops=2_000_000_000, mib=40 if count <= 16 else 60,
        far=(len(operands) - 3, len(operands) - 1),
    )


def feed_back_kernel(
    where, dffn, gres, wd_a, wd_b, wi_a, wi_b, slope_a, slope_b, hat, rate, gain, hidden_t, means, sums_two,
    into_a_o, into_b_o, grad_o, low_o, vectors_a_o, vectors_b_o,
    total, bias,
):
    step = pl.program_id(0)
    steps = pl.num_programs(0) // 2
    wide = total.shape[1]

    @pl.when(step == 0)
    def _():
        total[...] = gres[...]

    def units(side, step, wd, wi, slope, into_o):
        inner = (dot(dffn[...], wd[...], LANES) * slope[...].astype(F32)).astype(BF16)
        sums = jnp.sum(inner.astype(F32), 0, keepdims=True)
        bias[side : side + 1, pl.ds(pl.multiple_of(step * WIDE, WIDE), WIDE)] = sums
        total[...] += dot(inner, wi[...], LANES)
        into_o[...] = (dot(hidden_t[...], inner) - means[:, 4:5] * sums).astype(BF16)

    @pl.when(step < steps)
    def _():
        units(0, step, wd_a, wi_a, slope_a, into_a_o)

    @pl.when(step >= steps)
    def _():
        units(1, step - steps, wd_b, wi_b, slope_b, into_b_o)

    @pl.when(step == pl.num_programs(0) - 1)
    def _():
        grad = total[...]
        hats = hat[...]
        resid = normed_back(grad * row(gain), hats, rate[:, :1])
        grad_o[...] = resid
        low = resid.astype(BF16)
        low_o[...] = low
        for side, vectors in enumerate((vectors_a_o, vectors_b_o)):
            vectors[...] = jnp.zeros(vectors.shape, F32)
            vectors[0:3, :] = sums_two[0:3, :]
            vectors[3:4, :] = jnp.sum(grad * hats, 0, keepdims=True)
            vectors[4:5, :] = jnp.sum(grad, 0, keepdims=True)
            vectors[5:6, :] = jnp.sum(low.astype(F32), 0, keepdims=True)
            vectors[8:9, :] = bias[side : side + 1, :wide]
            vectors[9:10, :] = bias[side : side + 1, wide:]


def feed_back(where, dffn, gres, wd, wi, slope, hat, rate, gain, hidden_t, means, sums_two):
    rows, wide = dffn.shape
    units = wd[0].shape[0]
    operands = (
        dffn, gres, wd[0], wd[1], wi[0], wi[1], slope[0], slope[1], hat, rate, gain, hidden_t, means, sums_two,
    )
    specs = [whole(a) for a in operands]
    for side in range(2):
        specs[2 + side] = down_rows(wd[side], WIDE, side)
        specs[4 + side] = columns(wi[side], WIDE, side)
        specs[6 + side] = columns(slope[side], WIDE, side)
    into = shape(wide, units, kind=BF16)
    vectors = shape(SLOTS, wide)
    outs = (into, into, shape(rows, wide), shape(rows, wide, kind=BF16), vectors, vectors)
    out_specs = [whole(a) for a in outs]
    for side in range(2):
        out_specs[side] = columns(into, WIDE, side)
    return call(
        feed_back_kernel, (where,), operands, specs, outs, out_specs, 2 * units // WIDE,
        [pltpu.VMEM((rows, wide), F32), pltpu.VMEM((8, units), F32)],
        flops=12 * rows * wide * units, mib=44,
    )


def down_grad(where, act_t, dffn, means):
    units, rows = act_t[0].shape
    wide = dffn[0].shape[1]
    tile = wide // 2

    def half(j, where):
        side = (where[0] >> where[1]) & 1
        return jnp.where(j < 2, 1 - side, side)

    def down_grad_kernel(where, act_a, act_b, dffn_a, dffn_b, means, gone, kept, sums):
        step = pl.program_id(0)

        @pl.when(step == 0)
        def _():
            both = dffn_a[...].astype(F32) + dffn_b[...].astype(F32)
            sums[...] = jnp.broadcast_to(jnp.sum(both, 0, keepdims=True), sums.shape)

        mean = jnp.where(half(step, where) == 0, means[:, 0:1], means[:, 1:2])
        grads = dot(act_a[...], dffn_a[...]) + dot(act_b[...], dffn_b[...])
        grads = (grads - mean * sums[0:1, :]).astype(BF16)

        @pl.when(step < 2)
        def _():
            gone[...] = grads

        @pl.when(step >= 2)
        def _():
            kept[...] = grads

    out = shape(units // 2, wide, kind=BF16)
    act_spec = pl.BlockSpec((tile, rows), lambda j, where: (2 * half(j, where) + j % 2, 0))
    return call(
        down_grad_kernel, (where,), (*act_t, *dffn, means),
        [act_spec, act_spec, whole(dffn[0]), whole(dffn[1]), pl.BlockSpec((tile, PAIR), lambda j, *_: (j % 2, 0))],
        (out, out),
        [
            pl.BlockSpec((tile, wide), lambda j, *_: (jnp.minimum(j, 1), 0)),
            pl.BlockSpec((tile, wide), lambda j, *_: (jnp.maximum(j - 2, 0), 0)),
        ],
        4, [pltpu.VMEM((8, wide), F32)], flops=4 * rows * units * wide, mib=24,
    )


def halved(terms, bit, own):
    return [(array, path + ((bit, own),), half) for array, path, half in terms]


def term(array):
    return array, (), None


def columns_of(terms, half):
    return [(array, path, half) for array, path, _ in terms]


def block_of(path, where):
    index = 0
    for bit, own in path:
        side = (where[0] >> bit(where)) & 1
        index = 2 * index + (side if own else 1 - side)
    return index


def add(terms):
    return "add", terms, None


def join(pieces, bit):
    return "join", [term(t) for t in pieces], bit


def extent(array, path, half):
    return array.shape[0] >> len(path), array.shape[1] >> (half is not None)


def mixed(where, *jobs):
    if any(extent(*job[1][0])[0] % 16 for job in jobs):
        return [plain(where, *job) for job in jobs]
    operands, specs, outs = [], [], []
    for kind, terms, _ in jobs:
        for array, path, half in terms:
            block = extent(array, path, half)
            operands.append(array)
            specs.append(
                pl.BlockSpec(
                    block, lambda j, where, path=path, half=half: (block_of(path, where), half or 0)
                )
            )
        outs.append(shape((2 if kind == "join" else 1) * block[0], block[1], kind=BF16))

    def mixed_kernel(where, *refs):
        sources, targets = refs[: len(operands)], refs[len(operands) :]
        for (kind, terms, bit), target in zip(jobs, targets):
            mine, sources = sources[: len(terms)], sources[len(terms) :]
            if kind == "join":
                rows = mine[0].shape[0]
                side = (where[0] >> bit(where)) & 1
                target[pl.ds(pl.multiple_of(side * rows, 16), rows), :] = mine[0][...]
                target[pl.ds(pl.multiple_of((1 - side) * rows, 16), rows), :] = mine[1][...]
            else:
                total = mine[0][...].astype(F32)
                for other in mine[1:]:
                    total = total + other[...].astype(F32)
                target[...] = total.astype(BF16)

    return call(
        mixed_kernel, (where,), operands, specs, outs, [whole(a) for a in outs], mib=24,
        far=[i for i, a in enumerate(operands) if a.size >= BLOCK * BLOCK * 4],
    )


def plain(where, kind, terms, bit):
    if kind == "join":
        (first, _, _), (second, _, _) = terms
        side = (where[0] >> bit(where)) & 1
        return jnp.where(
            side == 0, jnp.concatenate([first, second], 0), jnp.concatenate([second, first], 0)
        )
    total = 0.0
    for array, path, half in terms:
        rows, columns = extent(array, path, half)
        piece = lax.dynamic_slice_in_dim(array, block_of(path, where) * rows, rows, 0)
        piece = piece[:, (half or 0) * columns : ((half or 0) + 1) * columns]
        total = total + piece.astype(F32)
    return total.astype(BF16)


def finish(where, pieces, means, vectors):
    half, width = pieces[0][0].shape[0], pieces[0][0].shape[1] // 2
    wide = 2 * half

    def finish_kernel(where, first_a, second_a, first_b, second_b, means, vectors, *outs):
        side = (where[0] >> where[1]) & 1
        for place in range(2):
            rows = slice(place * half, (place + 1) * half)
            x_mean = means[rows, 6:7]
            piece = jnp.where(side == place, first_a[...], second_a[...]).astype(F32)
            outs[0][rows, :] = piece[:, :width] + x_mean * vectors[6:7, :width]
            outs[1][rows, :] = piece[:, width:] + x_mean * vectors[6:7, width:]
            piece = jnp.where(side == place, first_b[...], second_b[...]).astype(F32)
            outs[2][rows, :] = piece[:, :width] + x_mean * vectors[7:8, :width]
            columns = slice(place * width, (place + 1) * width)
            outs[3][:, columns] = piece[:, width:] + means[:width, 5:6] * vectors[5:6, columns]

    outs = (shape(wide, width),) * 3 + (shape(width, wide),)
    operands = (*pieces[0], *pieces[1], means, vectors)
    return call(
        finish_kernel, (where,), operands, [whole(a) for a in operands], outs, [whole(a) for a in outs],
        mib=32,
    )


def swap(tensor):
    return lax.ppermute(tensor, "mp", [(0, 1), (1, 0)])


def flip(tensor, bits):
    count = lax.axis_size("dp")
    return lax.ppermute(tensor, "dp", [(i, i ^ bits) for i in range(count)])


def bit_count():
    return lax.axis_size("dp").bit_length() - 1


def seal(*values):
    return lax.optimization_barrier(values)


def plane(step):
    return lambda where: where[1] ^ step


def over(bit):
    return lambda where: bit


def cross(tensor, step):
    count = lax.axis_size("dp")
    pairs = [
        (2 * d + c, 2 * (d ^ (1 << (step ^ c))) + c) for d in range(count) for c in range(2)
    ]
    return lax.ppermute(tensor, ("dp", "mp"), pairs)


def gather_small(tensor, beside):
    bits = list(range(bit_count()))
    groups = []
    while bits:
        groups.append(bits[-2:])
        bits = bits[:-2]
    tensor, offsets = tensor[None], [0]
    for number, group in enumerate(groups):
        ways = range(1 << len(group))
        pieces = [tensor] + [flip(tensor, way << group[0]) for way in ways if way]
        places = [[(way << group[0]) | o for o in offsets] for way in ways]
        if number == 0:
            pieces, beside = seal(pieces, beside)
        if number == len(groups) - 1:
            return pieces, places, beside
        tensor = jnp.concatenate(pieces, 0)
        offsets = [o for part in places for o in part]


def shards(
    tokens_in, proj_query, bias_query, proj_key, proj_value, bias_value, proj_out, bias_out,
    gain_attn, shift_attn, proj_in, bias_in, proj_down, bias_down, gain_ffn, shift_ffn,
    bucket, lengths, positive,
):
    spot, me = lax.axis_index("dp"), lax.axis_index("mp")
    wide = tokens_in.shape[1]
    width = proj_query.shape[1]
    units = proj_in.shape[1]
    where = jnp.stack([spot, me]).astype(jnp.int32)
    scalars = (where, bucket, lengths)
    x = tokens_in

    bi = bias_in, swap(bias_in)
    wo, wi, wd = [(w, swap(w)) for w in (proj_out, proj_in, proj_down)]
    heads = attend(scalars, x, proj_query, bias_query, proj_key, proj_value, bias_value)
    heads, x_t = [h[:5] for h in heads], [h[5] for h in heads]
    ctx = heads[0][3], swap(heads[1][3])
    (hat_one, rate_one, hidden_t, act_t_a, act_t_b, slope_a, slope_b, hat_two, rate_two, unit, packed, rate_u) = feed(
        scalars + (positive,), x, ctx, wo, bias_out, gain_attn, shift_attn, wi, bi, wd,
        bias_down, gain_ffn, shift_ffn,
    )

    own, offsets, (unit_b, act_t_b) = gather_small(packed, [swap(unit), swap(act_t_b)])
    other = [swap(piece) for piece in own]
    act_t = act_t_a, act_t_b

    loss, query_embed, passage_embed, gres_two, dffn, sums_two, common, means = contrast(
        scalars, own, other, offsets, unit, unit_b, rate_u, hat_two, rate_two, gain_ffn
    )

    def outer(mean, sums):
        return mean[:, None] * sums[None, :]

    bits = bit_count()
    rest = list(range(2, bits))

    low, *high = rest

    def kept(terms, bit, other):
        return halved(terms, bit, True) + [term(other)]

    def sent(terms, bit):
        return add(halved(terms, bit, False))

    def hold(*values):
        arrays = seal(*[[t[0] for t in v] if is_sum(v) else v for v in values])
        return [
            [(t, *old[1:]) for t, old in zip(new, v)] if is_sum(v) else new
            for new, v in zip(arrays, values)
        ]

    def is_sum(value):
        return isinstance(value, list) and all(
            isinstance(t, tuple) and len(t) == 3 and isinstance(t[1], tuple) for t in value
        )

    dffns = dffn, swap(dffn)
    gone, own = down_grad(where, act_t, dffns, means)
    gone, own, dffn, common, sums_two = seal(gone, own, dffn, common, sums_two)
    down = [term(own), term(cross(gone, 0))]
    fed = feed_back(
        where, dffn, gres_two, wd, wi, (slope_a, slope_b), hat_one, rate_one, gain_attn, hidden_t,
        means, sums_two,
    )
    down, fed = hold(down, fed)
    into_a, into_b, gres_one, dattn, vectors_a, vectors_b = fed

    (gone,) = mixed(where, sent(down, plane(1)))
    gone, down, dattn, into_b = hold(gone, down, dattn, into_b)
    down = kept(down, plane(1), cross(gone, 1))
    into = [term(into_a), term(swap(into_b))]
    dattn_b = swap(dattn)
    back_a = attend_back(scalars, heads[0], dattn, wo[0])
    down, into, back_a, dattn_b = hold(down, into, back_a, dattn_b)

    gone = mixed(where, sent(into, plane(0)), sent(down, over(low)))
    gone, into, down, dattn_b, back_a = hold(gone, into, down, dattn_b, back_a)
    into = kept(into, plane(0), cross(gone[0], 0))
    down = kept(down, over(low), flip(gone[1], 1 << low))
    extra = (*x_t, heads[0][3], dattn, *back_a, means, vectors_a)
    back_b = attend_back(scalars, heads[1], dattn_b, wo[0], extra)
    into, down, back_b = hold(into, down, back_b)
    attn_gone, attn_kept, vectors_a = back_b[2:4], back_b[4:6], back_b[6]

    token = vectors_a

    def enter(*values):
        return hold(*values, token)[:-1]

    def over_high(tensor, sent):
        for bit in high[1:]:
            (tensor,) = mixed(where, add([term(tensor), term(sent)]))
            sent = flip(tensor, 1 << bit)
        return [term(tensor), term(sent)]

    def to_high(tensor):
        return tensor, flip(tensor, 1 << high[0])

    downs = [columns_of(down, half) for half in range(2)]
    intos = [columns_of(into, half) for half in range(2)]
    attns = [None, None]
    for h in range(2):
        downs[h], intos[h] = enter(downs[h], intos[h])
        downs[h], token = mixed(where, add(downs[h]), sent(intos[h], plane(1)))
        downs[h] = to_high(downs[h])
        intos[h] = kept(intos[h], plane(1), cross(token, 1))
    small = [vectors_a, swap(vectors_b)]
    for h in range(2):
        downs[h], intos[h] = enter(downs[h], intos[h])
        downs[h], token = mixed(where, add(over_high(*downs[h])), sent(intos[h], over(low)))
        attns[h] = [term(attn_kept[h]), term(cross(attn_gone[h], 0))]
        intos[h] = kept(intos[h], over(low), flip(token, 1 << low))
        downs[h] = [downs[h], flip(downs[h], 1 << low)]
    for h in range(2):
        attns[h], downs[h], intos[h] = enter(attns[h], downs[h], intos[h])
        token, downs[h], intos[h] = mixed(
            where, sent(attns[h], plane(1)), join(downs[h], over(low)), add(intos[h])
        )
        attns[h] = kept(attns[h], plane(1), cross(token, 1))
        downs[h] = [downs[h], cross(downs[h], 1)]
        intos[h] = to_high(intos[h])
    (small,) = enter(small)
    token = small = small[0] + small[1]
    small = [small, flip(small, 1)]
    for h in range(2):
        downs[h], attns[h], intos[h] = enter(downs[h], attns[h], intos[h])
        downs[h], token, intos[h] = mixed(
            where, join(downs[h], plane(1)), sent(attns[h], over(low)), add(over_high(*intos[h]))
        )
        downs[h] = [downs[h], cross(downs[h], 0)]
        attns[h] = kept(attns[h], over(low), flip(token, 1 << low))
        intos[h] = [intos[h], flip(intos[h], 1 << low)]
    (small,) = enter(small)
    token = small = small[0] + small[1]
    small = [small, flip(small, 2)]
    for h in range(2):
        intos[h], attns[h], downs[h] = enter(intos[h], attns[h], downs[h])
        intos[h], token = mixed(where, join(intos[h], over(low)), add(attns[h]))
        intos[h] = [intos[h], cross(intos[h], 1)]
        attns[h] = to_high(token)
    (small,) = enter(small)
    token = small = small[0] + small[1]
    small = [small, flip(small, 1 << low)]
    for h in range(2):
        intos[h], attns[h] = enter(intos[h], attns[h])
        intos[h], token = mixed(where, join(intos[h], plane(1)), add(over_high(*attns[h])))
        intos[h] = [intos[h], cross(intos[h], 0)]
        attns[h] = [token, flip(token, 1 << low)]
    for bit in high:
        (small,) = enter(small)
        token = small = small[0] + small[1]
        small = [small, flip(small, 1 << bit)]
    (gres_one,) = enter(gres_one)
    token = grad_in = input_grad(
        where, gres_one, (back_a[:2], back_b[:2]), (proj_query, proj_key, proj_value)
    )
    for h in range(2):
        (attns[h],) = enter(attns[h])
        (token,) = mixed(where, join(attns[h], over(low)))
        attns[h] = [token, cross(token, 1)]
    small, downs, common = enter(small, downs, common)
    small = small[0] + small[1]
    share = lax.dynamic_slice_in_dim(small[0:6], me * width, width, 1)
    d_g2, d_s2, d_bd, d_g1, d_s1, d_bo = [share[i] for i in range(6)]
    own_half = small[6:].reshape(-1)
    d_bq, d_bv = own_half[:width], own_half[2 * width : 3 * width]
    d_bi = small[8:10].reshape(units)
    act_mean, hidden_mean = common[0:2].reshape(units), common[4]
    for h in range(2):
        (attns[h],) = enter(attns[h])
        (token,) = mixed(where, join(attns[h], plane(1)))
        attns[h] = [token, cross(token, 0)]
    (downs,) = enter(downs)
    downs = [plain(where, *join(down, plane(0))) for down in downs]
    grad_down = jnp.concatenate(downs, 1).astype(F32) + outer(act_mean, small[2])
    intos, hidden_mean, d_bi, grad_in = enter(intos, hidden_mean, d_bi, grad_in)
    intos = [plain(where, *join(into, plane(0))) for into in intos]
    grad_into = jnp.concatenate(intos, 1).astype(F32) + outer(hidden_mean, d_bi)
    grad_in = (grad_in[0] + swap(grad_in[1]).astype(F32)).astype(BF16)
    other_in = swap(grad_in)
    grad_input = jnp.where(
        me == 0,
        jnp.concatenate([grad_in, other_in], 0),
        jnp.concatenate([other_in, grad_in], 0),
    )
    attns, grad_down, grad_into, grad_input = seal(attns, grad_down, grad_into, grad_input)
    grad_q, grad_k, grad_v, grad_o = finish(where, attns, means, small)
    return (
        loss[0, 0],
        query_embed,
        passage_embed,
        grad_input,
        grad_q,
        d_bq,
        grad_k,
        grad_v,
        d_bv,
        grad_o,
        d_bo,
        d_g1,
        d_s1,
        grad_into,
        d_bi,
        grad_down,
        d_bd,
        d_g2,
        d_s2,
    )


def solution(mesh):
    half, rows = P(None, "mp"), P("mp", None)
    return jax.shard_map(
        shards,
        mesh=mesh,
        in_specs=(
            P("dp", None), half, P("mp"), half, half, P("mp"), rows, P(), P(), P(),
            half, P("mp"), rows, P(), P(), P(), P("dp"), P("dp", None), P("dp"),
        ),
        out_specs=(
            P(), P("dp", None), P("dp", None), P("dp", None),
            half, P("mp"), half, half, P("mp"), rows, P("mp"), P("mp"), P("mp"),
            half, P("mp"), rows, P("mp"), P("mp"), P("mp"),
        ),
        check_vma=False,
    )
```

```python
from functools import partial

import jax
import jax.numpy as jnp
from jax import lax
from jax.experimental import pallas as pl
from jax.experimental.pallas import tpu as pltpu
from jax.sharding import PartitionSpec as P

HEAD_DIM = 64
BLOCK = 512
PAIR = 2 * HEAD_DIM
CHUNK = 128
SLOTS = 16
EPS = 1e-05
TEMP = 0.01
MASKED = -10000.0
HIGH = lax.Precision.HIGHEST
F32 = jnp.float32
BF16 = jnp.bfloat16
VMEM = pl.BlockSpec(memory_space=pltpu.VMEM)
SMEM = pl.BlockSpec(memory_space=pltpu.SMEM)


def dot(a, b, dims=((1,), (0,)), precision=None):
    return lax.dot_general(a, b, (dims, ((), ())), precision=precision, preferred_element_type=F32)


ROWS = ((0,), (0,))
LANES = ((1,), (1,))


def pieces_of(x, count=3):
    pieces = []
    for _ in range(count):
        pieces.append(x.astype(BF16))
        x = x - pieces[-1].astype(F32)
    return pieces


def dots(a, b, dims=((1,), (0,))):
    total = 0.0
    for i, x in enumerate(a):
        for j, y in enumerate(b):
            if i + j < 3:
                total = total + dot(x, y, dims)
    return total


def params(mib):
    return pltpu.CompilerParams(vmem_limit_bytes=mib * 1024 * 1024)


def row(ref):
    return ref[...].reshape(1, ref.shape[0])


def shape(*dims, kind=F32):
    return jax.ShapeDtypeStruct(dims, kind)


def lane_masks(kind):
    first = (lax.broadcasted_iota(jnp.int32, (1, PAIR), 1) < HEAD_DIM).astype(F32)
    return first.astype(kind), (1.0 - first).astype(kind)


def layout(bucket, lengths, me, axis):
    code = bucket[me]
    dims = (BLOCK, 1) if axis == 0 else (1, BLOCK)
    places = lax.broadcasted_iota(jnp.int32, dims, axis)
    shift = jnp.full(dims, jnp.where(code == 3, 9, 5 + code), jnp.int32)
    slot = lax.shift_right_logical(places, shift)
    offset = places - lax.shift_left(slot, shift)
    length = jnp.zeros(dims, jnp.int32)
    for s in range(SLOTS):
        length = jnp.where(slot == s, lengths[me, s], length)
    return slot, jnp.where(offset < length, slot, -1)


def pooling(bucket, lengths, me):
    _, kid = layout(bucket, lengths, me, 1)
    slots = lax.broadcasted_iota(jnp.int32, (SLOTS, BLOCK), 0)
    rows = lax.broadcasted_iota(jnp.int32, (SLOTS, 1), 0)
    length = jnp.zeros((SLOTS, 1), jnp.int32)
    for s in range(SLOTS):
        length = jnp.where(rows == s, lengths[me, s], length)
    return (slots == kid).astype(BF16), jnp.maximum(length, 1).astype(F32)


def attend_kernel(
    where, bucket, lengths,
    x, wq, bq, wk, wv, bv,
    q_a, q_b, k_a, k_b, v_a, v_b, ctx_a, ctx_b, lse_a, lse_b, x_t_a, x_t_b,
):
    width = wq.shape[1]
    first, second = lane_masks(BF16)
    low = lax.broadcasted_iota(jnp.int32, (CHUNK, PAIR), 1) < HEAD_DIM
    lane = lax.broadcasted_iota(jnp.int32, (CHUNK, PAIR), 1)
    ones = jnp.ones((BLOCK, PAIR), BF16)
    for me, q_o, k_o, v_o, ctx_o, lse_o, x_t in (
        (1 - where[1], q_b, k_b, v_b, ctx_b, lse_b, x_t_b),
        (where[1], q_a, k_a, v_a, ctx_a, lse_a, x_t_a),
    ):
        tokens = x[pl.ds(pl.multiple_of(me * BLOCK, BLOCK), BLOCK), :]
        x_t[...] = jnp.transpose(tokens)
        slot_col, _ = layout(bucket, lengths, me, 0)
        _, kid_row = layout(bucket, lengths, me, 1)
        q_o[...] = (dot(tokens, wq[...]) + row(bq)).astype(BF16)
        k_o[...] = dot(tokens, wk[...]).astype(BF16)
        v_o[...] = (dot(tokens, wv[...]) + row(bv)).astype(BF16)
        for r in range(BLOCK // CHUNK):
            rows = slice(r * CHUNK, (r + 1) * CHUNK)
            mask = slot_col[rows, :] == kid_row
            mask = jnp.concatenate([mask, mask], 0)
            levels = jnp.zeros((CHUNK, PAIR), F32)
            for pair in range(width // PAIR):
                cols = slice(pair * PAIR, (pair + 1) * PAIR)
                query = q_o[rows, cols] * jnp.asarray(HEAD_DIM**-0.5, BF16)
                both = jnp.concatenate([query * first, query * second], 0)
                scores = jnp.where(mask, dot(both, k_o[:, cols], LANES), MASKED)
                summit = jnp.max(scores, 1, keepdims=True)
                raised = jnp.exp(scores - summit).astype(BF16)
                out = dot(raised, jnp.concatenate([v_o[:, cols], ones], 1))
                mass = out[:, PAIR:]
                out = out[:, :PAIR] / mass
                ctx_o[rows, cols] = jnp.where(low, out[:CHUNK], out[CHUNK:]).astype(BF16)
                logs = jnp.log(mass) + summit
                levels = jnp.where(lane == 2 * pair, logs[:CHUNK], levels)
                levels = jnp.where(lane == 2 * pair + 1, logs[CHUNK:], levels)
            lse_o[rows, :] = levels


def whole(a):
    return pl.BlockSpec(a.shape, lambda j, *_: (0,) * len(a.shape))


def block_rows(a):
    return pl.BlockSpec((BLOCK, a.shape[1]), lambda j, where, *_: (where[1], 0))


def turn_of(side, steps):
    if side is None:
        return lambda j: j
    if side == 0:
        return lambda j: jnp.minimum(j, steps - 1)
    return lambda j: jnp.maximum(j - steps, 0)


def columns(a, tile, side=None):
    at = turn_of(side, a.shape[1] // tile)
    return pl.BlockSpec((a.shape[0], tile), lambda j, *_: (0, at(j)))


def down_rows(a, tile, side=None):
    at = turn_of(side, a.shape[0] // tile)
    return pl.BlockSpec((tile, a.shape[1]), lambda j, *_: (at(j), 0))


def call(
    kernel, scalars, operands, in_specs, outs, out_specs, steps=1, scratch=(), flops=0, mib=60, far=()
):
    operands = [
        pltpu.with_memory_space_constraint(a, pltpu.HBM) if i in far else a
        for i, a in enumerate(operands)
    ]
    moved = sum(a.size * a.dtype.itemsize for a in list(operands) + list(outs))
    return pl.pallas_call(
        kernel,
        grid_spec=pltpu.PrefetchScalarGridSpec(
            num_scalar_prefetch=len(scalars),
            grid=(steps,),
            in_specs=in_specs,
            out_specs=tuple(out_specs),
            scratch_shapes=list(scratch),
        ),
        out_shape=tuple(outs),
        compiler_params=params(mib),
        cost_estimate=pl.CostEstimate(flops=flops, bytes_accessed=moved, transcendentals=0),
        name=kernel.__name__,
    )(*scalars, *operands)


def attend(scalars, x, wq, bq, wk, wv, bv):
    wide, width = wq.shape
    low, level = shape(BLOCK, width, kind=BF16), shape(BLOCK, PAIR)
    turned = shape(wide, BLOCK, kind=BF16)
    outs = (low,) * 8 + (level,) * 2 + (turned,) * 2
    operands = (x, wq, bq, wk, wv, bv)
    flops = 4 * BLOCK * width * (3 * wide + 4 * BLOCK)
    outs = call(
        attend_kernel, scalars, operands, [whole(a) for a in operands],
        outs, [whole(a) for a in outs], flops=flops,
    )
    return outs[0::2], outs[1::2]


def attend_back_block(
    me, bucket, lengths, q, k, v, ctx, lse, dattn, wo, dqk_o, dv_o, sums_o, dscore_s
):
    width = q.shape[1]
    first, second = lane_masks(BF16)
    scale = jnp.asarray(HEAD_DIM**-0.5, BF16)
    dctx = dot(dattn[...], wo[...], LANES).astype(BF16)
    head_of = lax.broadcasted_iota(jnp.int32, (width, PAIR), 0) >> 6
    select = (head_of == lax.broadcasted_iota(jnp.int32, (width, PAIR), 1)).astype(F32)
    inner_sums = dot(select, dctx.astype(F32) * ctx[...].astype(F32), ((0,), (1,)), HIGH)
    levels = jnp.transpose(lse[...])
    slots, _ = layout(bucket, lengths, me, 1)
    _, kid_col = layout(bucket, lengths, me, 0)
    sums_o[...] = jnp.zeros(sums_o.shape, F32)
    low = lax.broadcasted_iota(jnp.int32, (TILE, PAIR), 1) < HEAD_DIM
    for pair in range(width // PAIR):
        cols = slice(pair * PAIR, (pair + 1) * PAIR)
        query = q[:, cols] * scale
        grad = dctx[:, cols]
        sum_k = jnp.zeros((1, PAIR), F32)
        sum_v = jnp.zeros((1, PAIR), F32)
        for c in range(BLOCK // TILE):
            rows = slice(c * TILE, (c + 1) * TILE)
            mask = kid_col[rows, :] == slots
            key_part, value_part = k[rows, cols], v[rows, cols]
            keys = jnp.concatenate([key_part * first, key_part * second], 0)
            values = jnp.concatenate([value_part * first, value_part * second], 0)
            scores, dprobs = dot(keys, query, LANES), dot(values, grad, LANES)
            probs, dscores = [], []
            for e in range(2):
                head, at = 2 * pair + e, slice(e * TILE, (e + 1) * TILE)
                prob = jnp.exp(jnp.where(mask, scores[at], MASKED) - levels[head : head + 1, :])
                dscore = (prob * (dprobs[at] - inner_sums[head : head + 1, :])).astype(BF16)
                dscore_s[e, rows, :] = dscore
                probs.append(prob.astype(BF16))
                dscores.append(dscore)
            dk = dot(jnp.concatenate(dscores, 0), query)
            dv = dot(jnp.concatenate(probs, 0), grad)
            dk = jnp.where(low, dk[:TILE], dk[TILE:]).astype(BF16)
            dv = jnp.where(low, dv[:TILE], dv[TILE:]).astype(BF16)
            dqk_o[rows, width + pair * PAIR : width + (pair + 1) * PAIR] = dk
            dv_o[rows, cols] = dv
            sum_k = sum_k + jnp.sum(dk.astype(F32), 0, keepdims=True)
            sum_v = sum_v + jnp.sum(dv.astype(F32), 0, keepdims=True)
        keys = jnp.transpose(k[:, cols])
        dq = [dot(keys[:HEAD_DIM], dscore_s[0]), dot(keys[HEAD_DIM:], dscore_s[1])]
        dq = (jnp.transpose(jnp.concatenate(dq, 0)) * HEAD_DIM**-0.5).astype(BF16)
        dqk_o[:, cols] = dq
        sums_o[0:1, cols] = jnp.sum(dq.astype(F32), 0, keepdims=True)
        sums_o[1:2, cols] = sum_k
        sums_o[2:3, cols] = sum_v


def own_back_kernel(
    where, bucket, lengths, q, k, v, ctx, lse, dattn, wo, dqk_o, dv_o, sums_o, dscore_s
):
    attend_back_block(
        where[1], bucket, lengths, q, k, v, ctx, lse, dattn, wo, dqk_o, dv_o, sums_o, dscore_s
    )


def other_back_kernel(
    where, bucket, lengths, q, k, v, ctx, lse, dattn, wo,
    x_t_a, x_t_b, ctx_a, dattn_a, dqk_a, dv_a, sums_a, means, vectors,
    dqk_o, dv_o, gone_a_o, gone_b_o, kept_a_o, kept_b_o, vectors_o,
    dscore_s, sums_o,
):
    attend_back_block(
        1 - where[1], bucket, lengths, q, k, v, ctx, lse, dattn, wo, dqk_o, dv_o, sums_o, dscore_s
    )
    width = q.shape[1]
    sums = sums_o[...] + sums_a[...]
    vectors_o[...] = vectors[...]
    vectors_o[6:7, :width] = sums[0:1, :]
    vectors_o[6:7, width:] = sums[1:2, :]
    vectors_o[7:8, :width] = sums[2:3, :]
    bias_out = vectors[5:6, :] + jnp.sum(dattn[...].astype(F32), 0, keepdims=True)
    turned_a, turned_b = jnp.transpose(ctx_a[...]), jnp.transpose(ctx[...])
    side = (where[0] >> where[1]) & 1
    for half, first, second in ((1 - side, gone_a_o, gone_b_o), (side, kept_a_o, kept_b_o)):
        rows = pl.ds(pl.multiple_of(half * width, width), width)
        rows_a, rows_b = x_t_a[rows, :], x_t_b[rows, :]
        x_mean = means[rows, :][:, 6:7]
        for i, (source_a, source_b, at) in enumerate(
            ((dqk_a, dqk_o, 0), (dqk_a, dqk_o, width), (dv_a, dv_o, 0))
        ):
            grads = dot(rows_a, source_a[:, at : at + width])
            grads = grads + dot(rows_b, source_b[:, at : at + width]) - x_mean * sums[i : i + 1, :]
            out = (first, first, second)[i]
            out[:, at : at + width] = grads.astype(BF16)
        grads = dot(turned_a, dattn_a[:, rows]) + dot(turned_b, dattn[:, rows])
        sums_here = jnp.where(half == 0, bias_out[:, :width], bias_out[:, width:])
        grads = grads - means[:width, 5:6] * sums_here
        second[:, width:] = grads.astype(BF16)


def attend_back(scalars, heads, dattn, wo, extra=None):
    rows, width = heads[0].shape
    wide = dattn.shape[1]
    outs = [shape(rows, 2 * width, kind=BF16), shape(rows, width, kind=BF16)]
    operands = (*heads, dattn, wo)
    scratch = [pltpu.VMEM((2, rows, rows), BF16)]
    if extra is None:
        kernel = own_back_kernel
        outs += [shape(8, width)]
    else:
        kernel = other_back_kernel
        operands += extra
        outs += [shape(wide // 2, 2 * width, kind=BF16)] * 4 + [shape(SLOTS, wide)]
        scratch += [pltpu.VMEM((8, width), F32)]
    return call(
        kernel, scalars, operands, [whole(a) for a in operands],
        outs, [whole(a) for a in outs], 1, scratch, flops=24 * rows * rows * width,
    )


def input_grad(where, gres, backs, weights):
    rows, wide = gres.shape
    width = weights[0].shape[1]

    def input_grad_kernel(where, gres, dqk_a, dv_a, dqk_b, dv_b, wq, wk, wv, own_o, other_o):
        for dqk, dv, out in ((dqk_a, dv_a, own_o), (dqk_b, dv_b, other_o)):
            parts = dot(dqk[:, :width], wq[...], LANES) + dot(dqk[:, width:], wk[...], LANES)
            parts = parts + dot(dv[...], wv[...], LANES)
            out[...] = parts + gres[...] if out is own_o else parts.astype(BF16)

    operands = (gres, *backs[0], *backs[1], *weights)
    outs = shape(rows, wide), shape(rows, wide, kind=BF16)
    return call(
        input_grad_kernel, (where,), operands, [whole(a) for a in operands],
        outs, [whole(a) for a in outs], flops=12 * rows * wide * width, mib=28, far=range(8),
    )


def normed(resid):
    center = resid - jnp.mean(resid, -1, keepdims=True)
    rate = lax.rsqrt(jnp.mean(center * center, -1, keepdims=True) + EPS)
    return center * rate, rate


def normed_back(grad, hat, rate):
    return (
        grad - jnp.mean(grad, -1, keepdims=True) - hat * jnp.mean(grad * hat, -1, keepdims=True)
    ) * rate


def feed_kernel(
    where, bucket, lengths, positive,
    x, ctx_a, ctx_b, wo_a, wo_b, bias_out, gain_one, shift_one,
    wi_a, wi_b, bi_a, bi_b, wd_a, wd_b, bias_down, gain_two, shift_two,
    hat_one_o, rate_one_o, hidden_t_o, act_t_a_o, act_t_b_o, slope_a_o, slope_b_o, hat_two_o, rate_two_o,
    unit_o, packed_o, rate_u_o,
    total, sums, act_sums, hidden_o, packing,
):
    step = pl.program_id(0)
    me = where[1]
    wide = total.shape[1]

    @pl.when(step == 0)
    def _():
        tokens = x[...].astype(F32)
        attn = dot(ctx_a[...], wo_a[...]) + dot(ctx_b[...], wo_b[...]) + row(bias_out)
        hat, rate = normed(tokens + attn)
        hidden = hat * row(gain_one) + row(shift_one)
        hat_one_o[...] = hat
        rate_one_o[...] = jnp.broadcast_to(rate, rate_one_o.shape)
        hidden_low = hidden.astype(BF16)
        hidden_o[...] = hidden_low
        hidden_t_o[...] = jnp.transpose(hidden_low)
        total[...] = hidden + row(bias_down)
        sums[...] = jnp.zeros(sums.shape, F32)
        act_sums[...] = jnp.zeros(act_sums.shape, F32)
        sums[0:1, :] = jnp.sum(hidden, 0, keepdims=True)
        half = ctx_a.shape[1]
        sums[1:2, :half] = jnp.sum(ctx_a[...].astype(F32), 0, keepdims=True)
        sums[1:2, half:] = jnp.sum(ctx_b[...].astype(F32), 0, keepdims=True)
        sums[2:3, :] = jnp.sum(tokens, 0, keepdims=True)

    place = pl.ds(pl.multiple_of(step * WIDE, WIDE), WIDE)

    def chunk(c, carry):
        rows = pl.ds(pl.multiple_of(c * ROWS_AT_ONCE, ROWS_AT_ONCE), ROWS_AT_ONCE)
        hidden = hidden_o[rows, :]
        added = []
        for side, (wi, bi, wd, act_o, slope_o) in enumerate((
            (wi_a, bi_a, wd_a, act_t_a_o, slope_a_o),
            (wi_b, bi_b, wd_b, act_t_b_o, slope_b_o),
        )):
            inner = dot(hidden, wi[...]) + row(bi)
            below = 0.5 + 0.5 * lax.erf(inner * (0.5**0.5))
            bell = jnp.exp(inner * inner * -0.5) * 0.3989422804014327
            act = inner * below
            act_sums[side : side + 1, place] += jnp.sum(act, 0, keepdims=True)
            act = act.astype(BF16)
            act_o[:, rows] = jnp.transpose(act)
            slope_o[rows, :] = (below + inner * bell).astype(BF16)
            added.append(dot(act, wd[...]))
        total[rows, :] += added[0] + added[1]
        return carry

    lax.fori_loop(0, BLOCK // ROWS_AT_ONCE, chunk, 0)

    @pl.when(step == pl.num_programs(0) - 1)
    def _():
        hat, rate = normed(total[...])
        hat_two_o[...] = hat
        rate_two_o[...] = jnp.broadcast_to(rate, rate_two_o.shape)
        output = hat * row(gain_two) + row(shift_two)
        member, length = pooling(bucket, lengths, me)
        raw = dots([member], pieces_of(output)) / length
        rate_u = lax.rsqrt(jnp.sum(raw * raw, 1, keepdims=True) + 1e-06)
        rate_u_o[...] = jnp.broadcast_to(rate_u, rate_u_o.shape)
        unit = raw * rate_u
        unit_o[...] = unit
        packing[...] = unit

        @pl.when(me == 1)
        def _():
            packing[4:8, :] = unit[0:4] - unit[0:4].astype(BF16).astype(F32)
            lane = lax.broadcasted_iota(jnp.int32, (1, wide), 1)
            extra = jnp.zeros((1, wide), jnp.int32)
            for s in range(SLOTS):
                extra = jnp.where(lane == s, positive[s] & 255, extra)
                extra = jnp.where(lane == 2 * SLOTS + s, positive[s] >> 8, extra)
            for s in range(2):
                extra = jnp.where(lane == 4 * SLOTS + s, bucket[s], extra)
            packing[8:9, :] = extra.astype(F32)
            packing[9:10, :] = act_sums[0:1, :wide]
            packing[10:11, :] = act_sums[0:1, wide:]
            packing[11:12, :] = act_sums[1:2, :wide]
            packing[12:13, :] = act_sums[1:2, wide:]
            packing[13:16, :] = sums[0:3, :]

        packed_o[...] = packing[...].astype(BF16)


TILE = 256
WIDE = 512
ROWS_AT_ONCE = 512


def feed(scalars, x, ctx, wo, bias_out, gain_one, shift_one, wi, bi, wd, bias_down, gain_two, shift_two):
    rows, wide = BLOCK, x.shape[1]
    units = wi[0].shape[1]
    full = shape(rows, wide)
    rate = shape(rows, PAIR)
    low = shape(rows, units, kind=BF16)
    turned = shape(units, rows, kind=BF16)
    hidden = shape(wide, rows, kind=BF16)
    operands = (
        x, ctx[0], ctx[1], wo[0], wo[1], bias_out, gain_one, shift_one,
        wi[0], wi[1], bi[0], bi[1], wd[0], wd[1], bias_down, gain_two, shift_two,
    )
    specs = [block_rows(x)] + [whole(a) for a in operands[1:]]
    for side in range(2):
        specs[8 + side] = columns(wi[side], WIDE)
        specs[10 + side] = pl.BlockSpec((WIDE,), lambda j, *_: (j,))
        specs[12 + side] = down_rows(wd[side], WIDE)
    outs = (
        full, rate, hidden, turned, turned, low, low, full, rate,
        shape(SLOTS, wide), shape(SLOTS, wide, kind=BF16), shape(SLOTS, PAIR),
    )
    out_specs = [whole(a) for a in outs]
    for place in (3, 4):
        out_specs[place] = down_rows(outs[place], WIDE)
    for place in (5, 6):
        out_specs[place] = columns(outs[place], WIDE)
    scratch = [
        pltpu.VMEM((rows, wide), F32), pltpu.VMEM((8, wide), F32), pltpu.VMEM((8, units), F32),
        pltpu.VMEM((rows, wide), BF16), pltpu.VMEM((SLOTS, wide), F32),
    ]
    return call(
        feed_kernel, scalars, operands, specs, outs, out_specs, units // WIDE, scratch,
        mib=48, far=[i for i in range(17) if i not in (2, 4, 9, 13)],
        flops=2 * rows * wide * (wide + 4 * units),
    )


def contrast_kernel(offsets, count, where, bucket, lengths, *refs):
    pieces = len(offsets)
    own, other = refs[:pieces], refs[pieces : 2 * pieces]
    unit, unit_b, rate_u, hat, rate, gain = refs[2 * pieces : 2 * pieces + 6]
    loss_o, query_o, passage_o, grad_o, low_o, sums_o, common_o, columns_o = refs[2 * pieces + 6 : 2 * pieces + 14]
    asks, table, notes, place_col, live_col, dlogits, common, grad_unit = refs[2 * pieces + 14 :]
    spot, me = where[0], where[1]
    wide = hat.shape[1]
    common[...] = jnp.zeros(common.shape, F32)
    notes[...] = jnp.zeros(notes.shape, F32)

    def spread(query_pieces, passage_pieces):
        for piece, places in zip(query_pieces, offsets):
            for i, offset in enumerate(places):
                source = spot ^ offset
                asks[pl.ds(pl.multiple_of(source * SLOTS, SLOTS), SLOTS), :] = piece[i]
        for piece, places in zip(passage_pieces, offsets):
            for i, offset in enumerate(places):
                source = spot ^ offset
                rows = piece[i].astype(F32)
                four = rows[0:4] + rows[4:8]
                four = jnp.concatenate([four, jnp.zeros_like(four)], 0)
                table[pl.ds(pl.multiple_of(source * 8, 8), 8), :] = four
                notes[pl.ds(source, 1), :] = rows[8:9, :PAIR]
                common[...] += rows[8:16]

    @pl.when(me == 0)
    def _():
        spread(own, other)

    @pl.when(me == 1)
    def _():
        spread(other, own)

    share = 1.0 / (count * BLOCK)
    first, second = common[1:3, :] * share, common[3:5, :] * share
    common_o[0:2, :] = jnp.where(me == 1, first, second)
    common_o[2:4, :] = jnp.where(me == 1, second, first)
    common_o[4:7, :] = common[5:8, :] * share
    common_o[7:8, :] = jnp.zeros((1, wide), F32)
    half = wide // 2

    @pl.when(me == 0)
    def _():
        common_o[5:6, :half] = common[6:7, half:] * share
        common_o[5:6, half:] = common[6:7, :half] * share

    padding = jnp.zeros((PAIR - 8, wide), F32)
    columns_o[...] = jnp.transpose(jnp.concatenate([common_o[...], padding], 0))

    turned = jnp.transpose(notes[...])
    slots = lax.broadcasted_iota(jnp.int32, (SLOTS, 1), 0).astype(F32)
    for d in range(count):
        at = slice(d * SLOTS, (d + 1) * SLOTS)
        place = turned[0:SLOTS, d : d + 1] + 256.0 * turned[2 * SLOTS : 3 * SLOTS, d : d + 1]
        place_col[at, :] = jnp.broadcast_to(place, (SLOTS, PAIR))
        held = jnp.where(turned[4 * SLOTS : 4 * SLOTS + 1, d : d + 1] == 0.0, 16.0, 8.0)
        live_col[at, :] = jnp.broadcast_to((slots < held).astype(F32), (SLOTS, PAIR))
    wide_p = table.shape[0]
    cells = lax.broadcasted_iota(jnp.int32, (PAIR, wide_p), 1)
    sources = lax.broadcasted_iota(jnp.int32, (PAIR, wide_p), 0)
    held = jnp.where(notes[:, 4 * SLOTS + 1 : 4 * SLOTS + 2] == 2.0, 4, 1)
    live_p = ((cells >> 3) == sources) & ((cells & 7) < held)
    live_p = jnp.sum(live_p.astype(F32), 0, keepdims=True)

    count_q = jnp.sum(live_col[:, :1], 0, keepdims=True)
    rows_q = min(asks.shape[0], BLOCK // 2)

    passages = pieces_of(table[...], 2)

    def scored(asking, at):
        alive = live_col[at, :][:, :1]
        places = place_col[at, :][:, :1].astype(jnp.int32)
        places = (places >> 2) * 8 + (places & 3)
        logits = dots(asking, passages, LANES) / TEMP
        logits = jnp.where(live_p > 0, logits, MASKED)
        summit = jnp.max(logits, 1, keepdims=True)
        raised = jnp.exp(logits - summit)
        mass = jnp.sum(raised, 1, keepdims=True)
        normal = summit + jnp.log(mass)
        target = lax.broadcasted_iota(jnp.int32, logits.shape, 1) == places
        picked = jnp.sum(jnp.where(target, logits, 0.0), 1, keepdims=True)
        grads = (jnp.exp(logits - normal) - target.astype(F32)) * (alive / count_q)
        return grads, jnp.sum(alive * (normal - picked), 0, keepdims=True)

    def part(i, total):
        at = pl.ds(pl.multiple_of(i * rows_q, rows_q), rows_q)
        dlogits[at, :], loss = scored([asks[at, :]], at)
        return total + loss

    total = jnp.zeros((1, 1), F32)
    if asks.shape[0] == rows_q:
        total = part(0, total)
    else:
        total = lax.fori_loop(0, asks.shape[0] // rows_q, part, total)
    loss_o[...] = total / count_q

    query_o[...] = jnp.where(me == 0, unit[...], unit_b[...])
    passage_o[...] = jnp.where(me == 0, unit_b[0:4, :], unit[0:4, :])

    @pl.when(me == 0)
    def _():
        mine, _ = scored(pieces_of(unit[...]), pl.ds(pl.multiple_of(spot * SLOTS, SLOTS), SLOTS))
        grad_unit[...] = dots(pieces_of(mine), passages) / TEMP

    @pl.when(me == 1)
    def _():
        cell = lax.broadcasted_iota(jnp.int32, (SLOTS, wide_p), 1)
        slot = lax.broadcasted_iota(jnp.int32, (SLOTS, wide_p), 0)
        mine = ((cell == slot + spot * 8) & (slot < 4)).astype(BF16)
        weights = dots([mine], pieces_of(dlogits[...]), LANES)
        grad_unit[...] = dots(pieces_of(weights), [asks[...]]) / TEMP

    slot = lax.broadcasted_iota(jnp.int32, (SLOTS, 1), 0)
    units = jnp.where((slot < 4) | (me == 0), unit[...], 0.0)
    grads = grad_unit[...]
    grad_embed = (grads - units * jnp.sum(units * grads, 1, keepdims=True)) * rate_u[:, :1]
    member, length = pooling(bucket, lengths, me)
    grad_out = dots([member], pieces_of(grad_embed / length), ROWS)
    hats = hat[...]
    resid = normed_back(grad_out * row(gain), hats, rate[:, :1])
    grad_o[...] = resid
    low = resid.astype(BF16)
    low_o[...] = low
    sums_o[0:1, :] = jnp.sum(grad_out * hats, 0, keepdims=True)
    sums_o[1:2, :] = jnp.sum(grad_out, 0, keepdims=True)
    sums_o[2:3, :] = jnp.sum(low.astype(F32), 0, keepdims=True)
    sums_o[3:8, :] = jnp.zeros((5, wide), F32)


def contrast(scalars, own, other, offsets, unit, unit_b, rate_u, hat, rate, gain):
    rows, wide = hat.shape
    count = sum(len(o) for o in offsets)
    operands = (*own, *other, unit, unit_b, rate_u, hat, rate, gain)
    outs = (
        shape(1, 1), shape(SLOTS, wide), shape(4, wide), shape(rows, wide),
        shape(rows, wide, kind=BF16), shape(8, wide), shape(8, wide), shape(wide, PAIR),
    )
    queries, passages = count * SLOTS, count * 8
    scratch = [pltpu.VMEM((queries, wide), BF16)] + [
        pltpu.VMEM(dims, F32)
        for dims in (
            (passages, wide), (PAIR, PAIR), (queries, PAIR), (queries, PAIR),
            (queries, passages), (8, wide), (SLOTS, wide),
        )
    ]
    kernel = partial(contrast_kernel, offsets, count)
    kernel.__name__ = "contrast"
    specs = [whole(a) for a in operands]
    return call(
        kernel, scalars, operands, specs, outs, [whole(a) for a in outs],
        1, scratch, flops=2_000_000_000, mib=40 if count <= 16 else 60,
        far=(len(operands) - 3, len(operands) - 1),
    )


def feed_back_kernel(
    where, dffn, gres, wd_a, wd_b, wi_a, wi_b, slope_a, slope_b, hat, rate, gain, hidden_t, means, sums_two,
    into_a_o, into_b_o, grad_o, low_o, vectors_a_o, vectors_b_o,
    total, bias,
):
    step = pl.program_id(0)
    steps = pl.num_programs(0) // 2
    wide = total.shape[1]

    @pl.when(step == 0)
    def _():
        total[...] = gres[...]

    def units(side, step, wd, wi, slope, into_o):
        inner = (dot(dffn[...], wd[...], LANES) * slope[...].astype(F32)).astype(BF16)
        sums = jnp.sum(inner.astype(F32), 0, keepdims=True)
        bias[side : side + 1, pl.ds(pl.multiple_of(step * WIDE, WIDE), WIDE)] = sums
        total[...] += dot(inner, wi[...], LANES)
        into_o[...] = (dot(hidden_t[...], inner) - means[:, 4:5] * sums).astype(BF16)

    @pl.when(step < steps)
    def _():
        units(0, step, wd_a, wi_a, slope_a, into_a_o)

    @pl.when(step >= steps)
    def _():
        units(1, step - steps, wd_b, wi_b, slope_b, into_b_o)

    @pl.when(step == pl.num_programs(0) - 1)
    def _():
        grad = total[...]
        hats = hat[...]
        resid = normed_back(grad * row(gain), hats, rate[:, :1])
        grad_o[...] = resid
        low = resid.astype(BF16)
        low_o[...] = low
        for side, vectors in enumerate((vectors_a_o, vectors_b_o)):
            vectors[...] = jnp.zeros(vectors.shape, F32)
            vectors[0:3, :] = sums_two[0:3, :]
            vectors[3:4, :] = jnp.sum(grad * hats, 0, keepdims=True)
            vectors[4:5, :] = jnp.sum(grad, 0, keepdims=True)
            vectors[5:6, :] = jnp.sum(low.astype(F32), 0, keepdims=True)
            vectors[8:9, :] = bias[side : side + 1, :wide]
            vectors[9:10, :] = bias[side : side + 1, wide:]


def feed_back(where, dffn, gres, wd, wi, slope, hat, rate, gain, hidden_t, means, sums_two):
    rows, wide = dffn.shape
    units = wd[0].shape[0]
    operands = (
        dffn, gres, wd[0], wd[1], wi[0], wi[1], slope[0], slope[1], hat, rate, gain, hidden_t, means, sums_two,
    )
    specs = [whole(a) for a in operands]
    for side in range(2):
        specs[2 + side] = down_rows(wd[side], WIDE, side)
        specs[4 + side] = columns(wi[side], WIDE, side)
        specs[6 + side] = columns(slope[side], WIDE, side)
    into = shape(wide, units, kind=BF16)
    vectors = shape(SLOTS, wide)
    outs = (into, into, shape(rows, wide), shape(rows, wide, kind=BF16), vectors, vectors)
    out_specs = [whole(a) for a in outs]
    for side in range(2):
        out_specs[side] = columns(into, WIDE, side)
    return call(
        feed_back_kernel, (where,), operands, specs, outs, out_specs, 2 * units // WIDE,
        [pltpu.VMEM((rows, wide), F32), pltpu.VMEM((8, units), F32)],
        flops=12 * rows * wide * units, mib=36,
    )


def down_grad(where, act_t, dffn, means):
    units, rows = act_t[0].shape
    wide = dffn[0].shape[1]
    tile = wide // 2

    def half(j, where):
        side = (where[0] >> where[1]) & 1
        return jnp.where(j < 2, 1 - side, side)

    def down_grad_kernel(where, act_a, act_b, dffn_a, dffn_b, means, gone, kept, sums):
        step = pl.program_id(0)

        @pl.when(step == 0)
        def _():
            both = dffn_a[...].astype(F32) + dffn_b[...].astype(F32)
            sums[...] = jnp.broadcast_to(jnp.sum(both, 0, keepdims=True), sums.shape)

        mean = jnp.where(half(step, where) == 0, means[:, 0:1], means[:, 1:2])
        grads = dot(act_a[...], dffn_a[...]) + dot(act_b[...], dffn_b[...])
        grads = (grads - mean * sums[0:1, :]).astype(BF16)

        @pl.when(step < 2)
        def _():
            gone[...] = grads

        @pl.when(step >= 2)
        def _():
            kept[...] = grads

    out = shape(units // 2, wide, kind=BF16)
    act_spec = pl.BlockSpec((tile, rows), lambda j, where: (2 * half(j, where) + j % 2, 0))
    return call(
        down_grad_kernel, (where,), (*act_t, *dffn, means),
        [act_spec, act_spec, whole(dffn[0]), whole(dffn[1]), pl.BlockSpec((tile, PAIR), lambda j, *_: (j % 2, 0))],
        (out, out),
        [
            pl.BlockSpec((tile, wide), lambda j, *_: (jnp.minimum(j, 1), 0)),
            pl.BlockSpec((tile, wide), lambda j, *_: (jnp.maximum(j - 2, 0), 0)),
        ],
        4, [pltpu.VMEM((8, wide), F32)], flops=4 * rows * units * wide, mib=24,
    )


def halved(terms, bit, own):
    return [(array, path + ((bit, own),), half) for array, path, half in terms]


def term(array):
    return array, (), None


def columns_of(terms, half):
    return [(array, path, half) for array, path, _ in terms]


def block_of(path, where):
    index = 0
    for bit, own in path:
        side = (where[0] >> bit(where)) & 1
        index = 2 * index + (side if own else 1 - side)
    return index


def add(terms):
    return "add", terms, None


def join(pieces, bit):
    return "join", [term(t) for t in pieces], bit


def extent(array, path, half):
    return array.shape[0] >> len(path), array.shape[1] >> (half is not None)


def mixed(where, *jobs):
    if any(extent(*job[1][0])[0] % 16 for job in jobs):
        return [plain(where, *job) for job in jobs]
    operands, specs, outs = [], [], []
    for kind, terms, _ in jobs:
        for array, path, half in terms:
            block = extent(array, path, half)
            operands.append(array)
            specs.append(
                pl.BlockSpec(
                    block, lambda j, where, path=path, half=half: (block_of(path, where), half or 0)
                )
            )
        outs.append(shape((2 if kind == "join" else 1) * block[0], block[1], kind=BF16))

    def mixed_kernel(where, *refs):
        sources, targets = refs[: len(operands)], refs[len(operands) :]
        for (kind, terms, bit), target in zip(jobs, targets):
            mine, sources = sources[: len(terms)], sources[len(terms) :]
            if kind == "join":
                rows = mine[0].shape[0]
                side = (where[0] >> bit(where)) & 1
                target[pl.ds(pl.multiple_of(side * rows, 16), rows), :] = mine[0][...]
                target[pl.ds(pl.multiple_of((1 - side) * rows, 16), rows), :] = mine[1][...]
            else:
                total = mine[0][...].astype(F32)
                for other in mine[1:]:
                    total = total + other[...].astype(F32)
                target[...] = total.astype(BF16)

    return call(
        mixed_kernel, (where,), operands, specs, outs, [whole(a) for a in outs], mib=24,
        far=[i for i, a in enumerate(operands) if a.size >= BLOCK * BLOCK * 4],
    )


def plain(where, kind, terms, bit):
    if kind == "join":
        (first, _, _), (second, _, _) = terms
        side = (where[0] >> bit(where)) & 1
        return jnp.where(
            side == 0, jnp.concatenate([first, second], 0), jnp.concatenate([second, first], 0)
        )
    total = 0.0
    for array, path, half in terms:
        rows, columns = extent(array, path, half)
        piece = lax.dynamic_slice_in_dim(array, block_of(path, where) * rows, rows, 0)
        piece = piece[:, (half or 0) * columns : ((half or 0) + 1) * columns]
        total = total + piece.astype(F32)
    return total.astype(BF16)


def finish(where, pieces, means, vectors):
    half, width = pieces[0][0].shape[0], pieces[0][0].shape[1] // 2
    wide = 2 * half

    def finish_kernel(where, first_a, second_a, first_b, second_b, means, vectors, *outs):
        side = (where[0] >> where[1]) & 1
        for place in range(2):
            rows = slice(place * half, (place + 1) * half)
            x_mean = means[rows, 6:7]
            piece = jnp.where(side == place, first_a[...], second_a[...]).astype(F32)
            outs[0][rows, :] = piece[:, :width] + x_mean * vectors[6:7, :width]
            outs[1][rows, :] = piece[:, width:] + x_mean * vectors[6:7, width:]
            piece = jnp.where(side == place, first_b[...], second_b[...]).astype(F32)
            outs[2][rows, :] = piece[:, :width] + x_mean * vectors[7:8, :width]
            columns = slice(place * width, (place + 1) * width)
            outs[3][:, columns] = piece[:, width:] + means[:width, 5:6] * vectors[5:6, columns]

    outs = (shape(wide, width),) * 3 + (shape(width, wide),)
    operands = (*pieces[0], *pieces[1], means, vectors)
    return call(
        finish_kernel, (where,), operands, [whole(a) for a in operands], outs, [whole(a) for a in outs],
        mib=32,
    )


def swap(tensor):
    return lax.ppermute(tensor, "mp", [(0, 1), (1, 0)])


def flip(tensor, bits):
    count = lax.axis_size("dp")
    return lax.ppermute(tensor, "dp", [(i, i ^ bits) for i in range(count)])


def bit_count():
    return lax.axis_size("dp").bit_length() - 1


def seal(*values):
    return lax.optimization_barrier(values)


def plane(step):
    return lambda where: where[1] ^ step


def over(bit):
    return lambda where: bit


def cross(tensor, step):
    count = lax.axis_size("dp")
    pairs = [
        (2 * d + c, 2 * (d ^ (1 << (step ^ c))) + c) for d in range(count) for c in range(2)
    ]
    return lax.ppermute(tensor, ("dp", "mp"), pairs)


def gather_small(tensor, beside):
    bits = list(range(bit_count()))
    groups = []
    while bits:
        groups.append(bits[-2:])
        bits = bits[:-2]
    tensor, offsets = tensor[None], [0]
    for number, group in enumerate(groups):
        ways = range(1 << len(group))
        pieces = [tensor] + [flip(tensor, way << group[0]) for way in ways if way]
        places = [[(way << group[0]) | o for o in offsets] for way in ways]
        if number == 0:
            pieces, beside = seal(pieces, beside)
        if number == len(groups) - 1:
            return pieces, places, beside
        tensor = jnp.concatenate(pieces, 0)
        offsets = [o for part in places for o in part]


def shards(
    tokens_in, proj_query, bias_query, proj_key, proj_value, bias_value, proj_out, bias_out,
    gain_attn, shift_attn, proj_in, bias_in, proj_down, bias_down, gain_ffn, shift_ffn,
    bucket, lengths, positive,
):
    spot, me = lax.axis_index("dp"), lax.axis_index("mp")
    wide = tokens_in.shape[1]
    width = proj_query.shape[1]
    units = proj_in.shape[1]
    where = jnp.stack([spot, me]).astype(jnp.int32)
    scalars = (where, bucket, lengths)
    x = tokens_in

    bi = bias_in, swap(bias_in)
    wo, wi, wd = [(w, swap(w)) for w in (proj_out, proj_in, proj_down)]
    heads = attend(scalars, x, proj_query, bias_query, proj_key, proj_value, bias_value)
    heads, x_t = [h[:5] for h in heads], [h[5] for h in heads]
    ctx = heads[0][3], swap(heads[1][3])
    (hat_one, rate_one, hidden_t, act_t_a, act_t_b, slope_a, slope_b, hat_two, rate_two, unit, packed, rate_u) = feed(
        scalars + (positive,), x, ctx, wo, bias_out, gain_attn, shift_attn, wi, bi, wd,
        bias_down, gain_ffn, shift_ffn,
    )

    own, offsets, (unit_b, act_t_b) = gather_small(packed, [swap(unit), swap(act_t_b)])
    other = [swap(piece) for piece in own]
    act_t = act_t_a, act_t_b

    loss, query_embed, passage_embed, gres_two, dffn, sums_two, common, means = contrast(
        scalars, own, other, offsets, unit, unit_b, rate_u, hat_two, rate_two, gain_ffn
    )

    def outer(mean, sums):
        return mean[:, None] * sums[None, :]

    bits = bit_count()
    rest = list(range(2, bits))

    low, *high = rest

    def kept(terms, bit, other):
        return halved(terms, bit, True) + [term(other)]

    def sent(terms, bit):
        return add(halved(terms, bit, False))

    def hold(*values):
        arrays = seal(*[[t[0] for t in v] if is_sum(v) else v for v in values])
        return [
            [(t, *old[1:]) for t, old in zip(new, v)] if is_sum(v) else new
            for new, v in zip(arrays, values)
        ]

    def is_sum(value):
        return isinstance(value, list) and all(
            isinstance(t, tuple) and len(t) == 3 and isinstance(t[1], tuple) for t in value
        )

    dffns = dffn, swap(dffn)
    gone, own = down_grad(where, act_t, dffns, means)
    gone, own, dffn, common, sums_two = seal(gone, own, dffn, common, sums_two)
    down = [term(own), term(cross(gone, 0))]
    fed = feed_back(
        where, dffn, gres_two, wd, wi, (slope_a, slope_b), hat_one, rate_one, gain_attn, hidden_t,
        means, sums_two,
    )
    down, fed = hold(down, fed)
    into_a, into_b, gres_one, dattn, vectors_a, vectors_b = fed

    (gone,) = mixed(where, sent(down, plane(1)))
    gone, down, dattn, into_b = hold(gone, down, dattn, into_b)
    down = kept(down, plane(1), cross(gone, 1))
    into = [term(into_a), term(swap(into_b))]
    dattn_b = swap(dattn)
    back_a = attend_back(scalars, heads[0], dattn, wo[0])
    down, into, back_a, dattn_b = hold(down, into, back_a, dattn_b)

    gone = mixed(where, sent(into, plane(0)), sent(down, over(low)))
    gone, into, down, dattn_b, back_a = hold(gone, into, down, dattn_b, back_a)
    into = kept(into, plane(0), cross(gone[0], 0))
    down = kept(down, over(low), flip(gone[1], 1 << low))
    extra = (*x_t, heads[0][3], dattn, *back_a, means, vectors_a)
    back_b = attend_back(scalars, heads[1], dattn_b, wo[0], extra)
    into, down, back_b = hold(into, down, back_b)
    attn_gone, attn_kept, vectors_a = back_b[2:4], back_b[4:6], back_b[6]

    token = vectors_a

    def enter(*values):
        return hold(*values, token)[:-1]

    def over_high(tensor, sent):
        for bit in high[1:]:
            (tensor,) = mixed(where, add([term(tensor), term(sent)]))
            sent = flip(tensor, 1 << bit)
        return [term(tensor), term(sent)]

    def to_high(tensor):
        return tensor, flip(tensor, 1 << high[0])

    downs = [columns_of(down, half) for half in range(2)]
    intos = [columns_of(into, half) for half in range(2)]
    attns = [None, None]
    for h in range(2):
        downs[h], intos[h] = enter(downs[h], intos[h])
        downs[h], token = mixed(where, add(downs[h]), sent(intos[h], plane(1)))
        downs[h] = to_high(downs[h])
        intos[h] = kept(intos[h], plane(1), cross(token, 1))
    small = [vectors_a, swap(vectors_b)]
    for h in range(2):
        downs[h], intos[h] = enter(downs[h], intos[h])
        downs[h], token = mixed(where, add(over_high(*downs[h])), sent(intos[h], over(low)))
        attns[h] = [term(attn_kept[h]), term(cross(attn_gone[h], 0))]
        intos[h] = kept(intos[h], over(low), flip(token, 1 << low))
        downs[h] = [downs[h], flip(downs[h], 1 << low)]
    for h in range(2):
        attns[h], downs[h], intos[h] = enter(attns[h], downs[h], intos[h])
        token, downs[h], intos[h] = mixed(
            where, sent(attns[h], plane(1)), join(downs[h], over(low)), add(intos[h])
        )
        attns[h] = kept(attns[h], plane(1), cross(token, 1))
        downs[h] = [downs[h], cross(downs[h], 1)]
        intos[h] = to_high(intos[h])
    (small,) = enter(small)
    token = small = small[0] + small[1]
    small = [small, flip(small, 1)]
    for h in range(2):
        downs[h], attns[h], intos[h] = enter(downs[h], attns[h], intos[h])
        downs[h], token, intos[h] = mixed(
            where, join(downs[h], plane(1)), sent(attns[h], over(low)), add(over_high(*intos[h]))
        )
        downs[h] = [downs[h], cross(downs[h], 0)]
        attns[h] = kept(attns[h], over(low), flip(token, 1 << low))
        intos[h] = [intos[h], flip(intos[h], 1 << low)]
    (small,) = enter(small)
    token = small = small[0] + small[1]
    small = [small, flip(small, 2)]
    for h in range(2):
        intos[h], attns[h], downs[h] = enter(intos[h], attns[h], downs[h])
        intos[h], token = mixed(where, join(intos[h], over(low)), add(attns[h]))
        intos[h] = [intos[h], cross(intos[h], 1)]
        attns[h] = to_high(token)
    (small,) = enter(small)
    token = small = small[0] + small[1]
    small = [small, flip(small, 1 << low)]
    for h in range(2):
        intos[h], attns[h] = enter(intos[h], attns[h])
        intos[h], token = mixed(where, join(intos[h], plane(1)), add(over_high(*attns[h])))
        intos[h] = [intos[h], cross(intos[h], 0)]
        attns[h] = [token, flip(token, 1 << low)]
    for bit in high:
        (small,) = enter(small)
        token = small = small[0] + small[1]
        small = [small, flip(small, 1 << bit)]
    (gres_one,) = enter(gres_one)
    token = grad_in = input_grad(
        where, gres_one, (back_a[:2], back_b[:2]), (proj_query, proj_key, proj_value)
    )
    for h in range(2):
        (attns[h],) = enter(attns[h])
        (token,) = mixed(where, join(attns[h], over(low)))
        attns[h] = [token, cross(token, 1)]
    small, downs, common = enter(small, downs, common)
    small = small[0] + small[1]
    share = lax.dynamic_slice_in_dim(small[0:6], me * width, width, 1)
    d_g2, d_s2, d_bd, d_g1, d_s1, d_bo = [share[i] for i in range(6)]
    own_half = small[6:].reshape(-1)
    d_bq, d_bv = own_half[:width], own_half[2 * width : 3 * width]
    d_bi = small[8:10].reshape(units)
    act_mean, hidden_mean = common[0:2].reshape(units), common[4]
    for h in range(2):
        (attns[h],) = enter(attns[h])
        (token,) = mixed(where, join(attns[h], plane(1)))
        attns[h] = [token, cross(token, 0)]
    (downs,) = enter(downs)
    downs = [plain(where, *join(down, plane(0))) for down in downs]
    grad_down = jnp.concatenate(downs, 1).astype(F32) + outer(act_mean, small[2])
    intos, hidden_mean, d_bi, grad_in = enter(intos, hidden_mean, d_bi, grad_in)
    intos = [plain(where, *join(into, plane(0))) for into in intos]
    grad_into = jnp.concatenate(intos, 1).astype(F32) + outer(hidden_mean, d_bi)
    grad_in = (grad_in[0] + swap(grad_in[1]).astype(F32)).astype(BF16)
    other_in = swap(grad_in)
    grad_input = jnp.where(
        me == 0,
        jnp.concatenate([grad_in, other_in], 0),
        jnp.concatenate([other_in, grad_in], 0),
    )
    attns, grad_down, grad_into, grad_input = seal(attns, grad_down, grad_into, grad_input)
    grad_q, grad_k, grad_v, grad_o = finish(where, attns, means, small)
    return (
        loss[0, 0],
        query_embed,
        passage_embed,
        grad_input,
        grad_q,
        d_bq,
        grad_k,
        grad_v,
        d_bv,
        grad_o,
        d_bo,
        d_g1,
        d_s1,
        grad_into,
        d_bi,
        grad_down,
        d_bd,
        d_g2,
        d_s2,
    )


def solution(mesh):
    half, rows = P(None, "mp"), P("mp", None)
    return jax.shard_map(
        shards,
        mesh=mesh,
        in_specs=(
            P("dp", None), half, P("mp"), half, half, P("mp"), rows, P(), P(), P(),
            half, P("mp"), rows, P(), P(), P(), P("dp"), P("dp", None), P("dp"),
        ),
        out_specs=(
            P(), P("dp", None), P("dp", None), P("dp", None),
            half, P("mp"), half, half, P("mp"), rows, P("mp"), P("mp"), P("mp"),
            half, P("mp"), rows, P("mp"), P("mp"), P("mp"),
        ),
        check_vma=False,
    )
```
